128 devices in a mesh: gx: 16 (over y_hi, x, core), gy: 8 (over z, y_lo).
Axes of the slice: x: 4, y: 4 (y_hi: 2, y_lo: 2; y = y_hi * 2 + y_lo), z: 4, core: 2. Of those that a mesh axis runs over, the one named last changes fastest.
Arguments:
- control: float32 [16, 1024, 2048], P(None, 'gx', 'gy'), may hold values from -6 to 6
- sigma: float32 [16, 1024, 2048], P(None, 'gx', 'gy'), may hold values from 0.5 to 4
- vert_diff: float32 [15, 1024, 2048], P(None, 'gx', 'gy'), may hold values from 0.1 to 10
- zonal_diff: float32 [1024, 2048], P('gx', 'gy'), may hold values from 0.1 to 0.24
- merid_diff: float32 [1024, 2048], P('gx', 'gy'), may hold values from 0.1 to 0.24
- ocean_mask: int32 [1024, 2048], P('gx', 'gy'), may hold values from 0 to 1
- owner: int32 [262144, 1], P(('gx', 'gy')), may hold values from 0 to 127; in each aligned block of 2048 rows (0 to 2047, 2048 to 4095, ...) at most 64 rows name the same one
- cell: int32 [262144], P(('gx', 'gy')), may hold values from 0 to 16126, as said below
- interp_weights: float32 [4, 262144], P(None, ('gx', 'gy')), may hold values from 0 to 1, as said below
- innovation: float32 [16, 262144], P(None, ('gx', 'gy')), may hold values from -6 to 6
- obs_weight: float32 [16, 262144], P(None, ('gx', 'gy')), may hold values from 0.25 to 4
Outputs:
- increment: float32 [16, 1024, 2048], P(None, 'gx', 'gy')
- departures: float32 [16, 262144], P(None, ('gx', 'gy'))
- gradient: float32 [16, 1024, 2048], P(None, 'gx', 'gy')
The draws below stay inside these ranges and needn't reach their ends.
Inputs may be any that keep to these rules, and one draw needn't show every extreme that they name: Among the profiles stored on one device, at most 64 name any one owner; every device is named by some profile. c = a * 256 + b names cell (a, b) of the owner's block of 64 x 256 cells with a <= 62 and b <= 254, so all four corners lie in that block. `interp_weights`: the four weights of a profile are the products of (1 - s, s) and (1 - t, t) for offsets s, t in [0, 1], corner order (a, b), (a + 1, b), (a, b + 1), (a + 1, b + 1).
All inputs are finite; a program needn't handle non-finite values.
Results may differ from the reference program's by a relative error of at most 0.00013.
Values sent between devices are 32-bit elements; how exact they have to be, the bound alone decides.
A program may use at most 128 MiB of HBM per device.

```python
import math
import jax
import jax.numpy as jnp
import numpy as np

LEV = 16
STEPS = 10
CX = 64
CY = 256
PROF_DEV = 2048
NX = 1024
NY = 2048
PROFILES = 262144
CAP = 64
N_GX = 16
N_GY = 8


def draw_cell(key, part):
    first, second = jax.random.split(key)
    along_x = jax.random.randint(first, (PROFILES,), 0, CX - 1)
    along_y = jax.random.randint(second, (PROFILES,), 0, CY - 1)
    along_x = along_x.at[0].set(CX - 2).at[1].set(0)
    along_y = along_y.at[0].set(CY - 2).at[1].set(0)
    return (along_x * CY + along_y).astype(jnp.int32)


def draw_interp_weights(key, part):
    first, second = jax.random.split(key)
    offset_x = jax.random.uniform(first, (PROFILES,), jnp.float32)
    offset_y = jax.random.uniform(second, (PROFILES,), jnp.float32)
    stacked = jnp.stack([(1.0 - offset_x) * (1.0 - offset_y), offset_x * (1.0 - offset_y), (1.0 - offset_x) * offset_y, offset_x * offset_y])
    return stacked.astype(jnp.float32)


def draw_ocean_mask(key, part):
    first, second = jax.random.split(jax.random.fold_in(key, 7))
    tiles_x = (NX + 7) // 8
    tiles_y = (NY + 7) // 8
    coarse = jax.random.randint(first, (tiles_x, tiles_y), 0, 4)
    tile_row = jnp.arange(NX, dtype=jnp.int32) // 8
    tile_col = jnp.arange(NY, dtype=jnp.int32) // 8
    spread = coarse[tile_row][:, tile_col]
    speckle = jax.random.randint(second, (NX, NY), 0, 32)
    wet = (spread != 0) & (speckle != 0)
    return wet.astype(jnp.int32)


def face_coefficients(key):
    uniform_draw = jax.random.uniform(key, (NX, NY), jnp.float32)
    values = 0.1 + 0.14 * uniform_draw
    return values.astype(jnp.float32)


def draw_zonal_diff(key, part):
    return face_coefficients(jax.random.fold_in(key, 11))


def draw_merid_diff(key, part):
    return face_coefficients(jax.random.fold_in(key, 13))


def block_scale(key, dims, pieces, low, largest):
    def one(position, shards_of):
        heights = jax.random.uniform(jax.random.fold_in(jax.random.fold_in(key, 6), position), (shards_of,), jnp.float32, low / len(pieces), largest / len(pieces))
        return jnp.repeat(jnp.exp(heights), dims[position] // shards_of).reshape((-1,) + (1,) * (len(dims) - position - 1))

    gain = one(*pieces[0])
    for cut in pieces[1:]:
        gain = gain * one(*cut)
    return gain


def routed_block(rng, own, number, rows, amount, top, limit, lean):
    sequence = jax.random.permutation(rng, amount)
    crowded, ordinary = shares(amount, rows * top, limit, lean, True), shares(amount, rows * top, limit, lean, False)
    places = jnp.arange(amount)

    def named(tallies, offset_by):
        used = int((tallies > 0).sum())
        fixed = max(1, used // 4)
        passed = fixed + (places - fixed + offset_by * (used - fixed)) % max(1, amount - fixed)
        return jnp.zeros((amount,), jnp.int32).at[sequence[jnp.where(places < fixed, places, passed)]].set(jnp.asarray(tallies, jnp.int32))

    tallies = jnp.where(number % 4 == 0, named(crowded, number // 4), named(ordinary, number - number // 4 - 1))
    mixed = jax.random.permutation(jax.random.fold_in(own, 3), amount)
    donor, sink = mixed[0:amount // 2 * 2:2], mixed[1:amount // 2 * 2:2]
    room = jnp.minimum(tallies[donor] - 1, limit - tallies[sink]) // 2
    room = jnp.where((donor == sequence[0]) | (sink == sequence[0]) | (tallies[sink] == 0), 0, jnp.maximum(room, 0))
    passed = jax.random.randint(jax.random.fold_in(own, 4), (amount // 2,), 0, 1 << 20) % (room + 1)
    tallies = tallies.at[donor].add(-passed).at[sink].add(passed)
    members = jnp.searchsorted(jnp.cumsum(tallies), jnp.arange(rows * top), side="right").astype(jnp.int32)
    grid = members.reshape(top, rows).T
    grid = grid[jax.random.permutation(jax.random.fold_in(own, 1), rows)]
    offset_by = jax.random.randint(jax.random.fold_in(own, 2), (rows, 1), 0, top)
    return jnp.take_along_axis(grid, (jnp.arange(top)[None, :] + offset_by) % top, axis=1)


def shares(count, total, bound, lean, full):
    loads = [(1 << 20) // math.isqrt(rank ** lean) + 1 for rank in range(1, count + 1)]
    largest = bound if full else min(bound, max(-(-total // count), total * loads[0] // sum(loads)))
    least = 1 if total - largest >= count - 1 else 0
    holding, surplus = [largest] + [least] * (count - 1), total - largest - least * (count - 1)
    while surplus > 0:
        free = [i for i in range(1, count) if holding[i] < largest] or [i for i in range(1, count) if holding[i] < bound]
        whole, left = sum([loads[i] for i in free]), surplus
        for i in free:
            addition = min(bound - holding[i], max(1, left * loads[i] // whole), surplus)
            holding[i] = holding[i] + addition
            surplus = surplus - addition
    return np.array(holding)


def gaussian(key, dims, width, limit, shards=(), kind=jnp.bfloat16):
    result = jax.random.normal(key, dims, jnp.float32) * width
    if len(shards) > 0:
        result = block_scale(key, dims, shards, -0.22, 0.18) * result
    return jnp.clip(result, min=-limit, max=limit).astype(kind)


def setup_inputs(seed: int = 0) -> dict:
    key_list = jax.random.split(jax.random.key(seed), 12)
    control = gaussian(key_list[0], (LEV, NX, NY), 1.0, 6.0, ((1, 16), (2, 8)), jnp.float32)
    sigma = jnp.clip(jnp.exp(math.log(4.0) - 2.0794415 * jax.random.uniform(key_list[1], (LEV, NX, NY), jnp.float32) ** block_scale(key_list[1], (LEV, NX, NY), ((1, 16), (2, 8)), -0.2, 0.2)), 0.5, 4.0)
    vert_diff = jnp.clip(jnp.exp(math.log(10.0) - 4.6051702 * jax.random.uniform(key_list[2], (LEV - 1, NX, NY), jnp.float32) ** block_scale(key_list[2], (LEV - 1, NX, NY), ((1, 16), (2, 8)), -0.2, 0.2)), 0.1, 10.0)
    zonal_diff = draw_zonal_diff(jax.random.fold_in(key_list[11], 71), 0)
    merid_diff = draw_merid_diff(jax.random.fold_in(key_list[11], 71), 0)
    ocean_mask = draw_ocean_mask(jax.random.fold_in(key_list[11], 71), 0)
    owner_keys = jax.random.split(jax.random.fold_in(key_list[6], 1), PROFILES // PROF_DEV)
    owner_turns = jax.random.permutation(jax.random.fold_in(key_list[6], 3), PROFILES // PROF_DEV)
    owner = jax.vmap(lambda own, number: routed_block(jax.random.fold_in(key_list[6], 2), own, number, PROF_DEV, N_GX * N_GY, 1, CAP, 2))(owner_keys, owner_turns).reshape((PROFILES, 1))
    cell = draw_cell(jax.random.fold_in(key_list[11], 71), 0)
    interp_weights = draw_interp_weights(jax.random.fold_in(key_list[11], 71), 0)
    innovation = gaussian(key_list[9], (LEV, PROFILES), 1.0, 6.0, ((1, 128),), jnp.float32)
    obs_weight = jnp.clip(jnp.exp(math.log(4.0) - 2.7725887 * jax.random.uniform(key_list[10], (LEV, PROFILES), jnp.float32) ** block_scale(key_list[10], (LEV, PROFILES), ((1, 128),), -0.2, 0.2)), 0.25, 4.0)
    return {"control": control, "sigma": sigma, "vert_diff": vert_diff, "zonal_diff": zonal_diff, "merid_diff": merid_diff, "ocean_mask": ocean_mask, "owner": owner, "cell": cell, "interp_weights": interp_weights, "innovation": innovation, "obs_weight": obs_weight}


def thomas_factors(vert_diff):
    count = vert_diff.shape[0] + 1
    zero_plane = jnp.zeros_like(vert_diff[0])
    lower_diff = [zero_plane] + [vert_diff[level] for level in range(count - 1)]
    upper_diff = [vert_diff[level] for level in range(count - 1)] + [zero_plane]
    upper_factor = []
    inverse = []
    for level in range(count):
        diagonal = 1.0 + lower_diff[level] + upper_diff[level]
        if level > 0:
            diagonal = diagonal + lower_diff[level] * upper_factor[level - 1]
        pivot_inv = 1.0 / diagonal
        inverse.append(pivot_inv)
        upper_factor.append(-upper_diff[level] * pivot_inv)
    return lower_diff, upper_factor, inverse


def vertical_solve(rhs, lower_diff, upper_factor, inverse):
    count = rhs.shape[0]
    reduced = []
    for level in range(count):
        term = rhs[level]
        if level > 0:
            term = term + lower_diff[level] * reduced[level - 1]
        reduced.append(term * inverse[level])
    solution = [reduced[count - 1]]
    for level in range(count - 2, -1, -1):
        solution.insert(0, reduced[level] - upper_factor[level] * solution[0])
    return jnp.stack(solution)


def diffuse(field_now, face_x, face_y):
    east_flux = face_x[None] * (jnp.roll(field_now, -1, axis=1) - field_now)
    west_flux = jnp.roll(east_flux, 1, axis=1)
    north_next = jnp.concatenate([field_now[:, :, 1:], jnp.zeros_like(field_now[:, :, :1])], axis=2)
    north_flux = face_y[None] * (north_next - field_now)
    south_flux = jnp.concatenate([jnp.zeros_like(north_flux[:, :, :1]), north_flux[:, :, :-1]], axis=2)
    return field_now + east_flux - west_flux + north_flux - south_flux


def reference(control, sigma, vert_diff, zonal_diff, merid_diff, ocean_mask, owner, cell, interp_weights, innovation, obs_weight):
    wet_cells = ocean_mask.astype(jnp.float32)
    face_x = zonal_diff * wet_cells * jnp.roll(wet_cells, -1, axis=0)
    north_wet = jnp.concatenate([wet_cells[:, 1:], jnp.zeros((NX, 1), jnp.float32)], axis=1)
    face_y = merid_diff * wet_cells * north_wet
    lower_diff, upper_factor, inverse = thomas_factors(vert_diff)
    field_now = vertical_solve(wet_cells[None] * control, lower_diff, upper_factor, inverse)
    for step_index in range(STEPS):
        field_now = diffuse(field_now, face_x, face_y)
    increment = sigma * field_now
    target = owner[:, 0].astype(jnp.int32)
    row_x = (target // N_GY) * CX + cell // CY
    row_y = (target % N_GY) * CY + cell % CY
    corner_base = (row_x * NY + row_y).astype(jnp.int32)
    offsets = (0, NY, 1, NY + 1)
    flat_field = increment.reshape(LEV, NX * NY)
    model_vals = jnp.zeros((LEV, cell.shape[0]), jnp.float32)
    for corner in range(4):
        model_vals = model_vals + interp_weights[corner][None, :] * flat_field[:, corner_base + offsets[corner]]
    departures = model_vals - innovation
    forcing = obs_weight * departures
    adjoint = jnp.zeros((LEV, NX * NY), jnp.float32)
    for corner in range(4):
        adjoint = adjoint.at[:, corner_base + offsets[corner]].add(interp_weights[corner][None, :] * forcing)
    field_now = sigma * adjoint.reshape(LEV, NX, NY)
    for step_index in range(STEPS):
        field_now = diffuse(field_now, face_x, face_y)
    gradient = control + wet_cells[None] * vertical_solve(field_now, lower_diff, upper_factor, inverse)
    return increment, departures, gradient
```

```python
import functools

import jax
import jax.numpy as jnp
from jax import lax
from jax.experimental import pallas as pl
from jax.experimental.pallas import tpu as pltpu
from jax.sharding import PartitionSpec as P

MESH = pl.DeviceIdType.MESH
F32 = jnp.float32
BF16 = jnp.bfloat16
VMEM_LIMIT = 60 * 1024 * 1024

LEV = 16
STEPS = 10
CX = 64
CY = 256
NGX = 16
NGY = 8
NDEV = NGX * NGY
PROF = 2048
CAP = 64
TILES = PROF // 128
ROWS = CX + 2 * STEPS
SPAD = 6
SROWS = 96
GROUPS = 12
REC = 24
DIFFUSE_ROWS = 16
PACK_PAIRS = 4
UNPACK_OWNERS = 8


def lane_iota(rows):
    return lax.broadcasted_iota(jnp.int32, (rows, 128), 1)


def split_pair(low, high, left):
    first = jnp.where(left, low, pltpu.roll(high, 64, axis=1))
    second = jnp.where(left, pltpu.roll(low, 64, axis=1), high)
    return first, second


def pack_kernel(owner, cell, weights, innov, obsw, rec, rank_out, tab, cst):
    rows_o = lax.broadcasted_iota(jnp.int32, (NDEV, 256), 0)
    before = (
        lax.broadcasted_iota(jnp.int32, (256, 256), 0) < lax.broadcasted_iota(jnp.int32, (256, 256), 1)
    ).astype(F32).astype(BF16)
    ones = jnp.ones((256, 256), BF16)
    rows_r = lax.broadcasted_iota(jnp.int32, (CAP, 256), 0)
    cols_p = lax.broadcasted_iota(jnp.int32, (CAP, 256), 1)
    earlier = jnp.zeros((NDEV, 256), F32)
    table = jnp.zeros((NDEV, 128), F32)
    for block in range(PROF // 256):
        owners = jnp.concatenate([owner[2 * block : 2 * block + 1, :], owner[2 * block + 1 : 2 * block + 2, :]], axis=1)
        hot = (rows_o == owners).astype(F32)
        hot16 = hot.astype(BF16)
        count = earlier + jnp.dot(hot16, before, preferred_element_type=F32)
        rank = jnp.sum(hot * count, axis=0, keepdims=True).astype(jnp.int32)
        earlier = earlier + jnp.dot(hot16, ones, preferred_element_type=F32)
        rank_out[2 * block : 2 * block + 1, :] = rank[:, :128]
        rank_out[2 * block + 1 : 2 * block + 2, :] = rank[:, 128:]
        same = rows_r == rank
        lane = jnp.where(same, cols_p % 128, 0).astype(F32).astype(BF16)
        tile = jnp.where(same, 2 * block + 1 + cols_p // 128, 0).astype(F32).astype(BF16)
        table = table + lax.dot_general(
            hot16, jnp.concatenate([lane, tile], axis=0), (((1,), (1,)), ((), ())), preferred_element_type=F32
        )
    tab[...] = table.astype(jnp.int32)

    cst[...] = jnp.zeros_like(cst)
    for tile in range(TILES):
        cols = slice(128 * tile, 128 * tile + 128)
        cst[0:1, cols] = cell[tile : tile + 1, :].astype(F32)
        cst[1:2, cols] = weights[1:2, cols] + weights[3:4, cols]
        cst[2:3, cols] = weights[2:3, cols] + weights[3:4, cols]

    left = lane_iota(8) < 64

    def pair(j, carry):
        row0 = jnp.broadcast_to(tab[pl.ds(2 * j, 1), :], (8, 128))
        row1 = jnp.broadcast_to(tab[pl.ds(2 * j + 1, 1), :], (8, 128))
        lane = jnp.where(left, row0, pltpu.roll(row1, 64, axis=1))
        tile_of = jnp.where(left, pltpu.roll(row0, 64, axis=1), row1)
        found = [jnp.zeros((8, 128), F32)] * 5
        for tile in range(TILES):
            cols = slice(128 * tile, 128 * tile + 128)
            sources = (cst[:, cols], innov[0:8, cols], innov[8:16, cols], obsw[0:8, cols], obsw[8:16, cols])
            here = tile_of == tile + 1
            found = [
                jnp.where(here, jnp.take_along_axis(source, lane, axis=1, mode="promise_in_bounds"), old)
                for source, old in zip(sources, found)
            ]
        first_i, second_i = split_pair(found[1], found[2], left)
        first_o, second_o = split_pair(found[3], found[4], left)
        rec[2 * j] = jnp.concatenate([found[0], first_i, first_o], axis=0)
        rec[2 * j + 1] = jnp.concatenate([pltpu.roll(found[0], 64, axis=1), second_i, second_o], axis=0)
        return carry

    blocks(0, NDEV // 2, PACK_PAIRS, pair, 0)


def pack(owner, cell, weights, innov, obsw):
    return pl.pallas_call(
        pack_kernel,
        out_shape=(
            jax.ShapeDtypeStruct((NDEV, REC, 128), F32),
            jax.ShapeDtypeStruct((TILES, 128), jnp.int32),
        ),
        in_specs=[pl.BlockSpec(memory_space=pltpu.VMEM)] * 5,
        out_specs=(pl.BlockSpec(memory_space=pltpu.VMEM),) * 2,
        scratch_shapes=[pltpu.VMEM((NDEV, 128), jnp.int32), pltpu.VMEM((8, PROF), F32)],
        compiler_params=pltpu.CompilerParams(vmem_limit_bytes=VMEM_LIMIT),
        name="pack",
    )(owner, cell, weights, innov, obsw)


def unpack_kernel(ret, owner, rank, innov, dep):
    def one(o, found):
        tile = ret[o]
        new = []
        for t in range(TILES):
            idx = jnp.broadcast_to(rank[t : t + 1, :], (8, 128))
            here = jnp.broadcast_to(owner[t : t + 1, :], (8, 128)) == o
            low = jnp.take_along_axis(tile, idx, axis=1, mode="promise_in_bounds")
            high = jnp.take_along_axis(tile, idx + 64, axis=1, mode="promise_in_bounds")
            new.append(jnp.where(here, low, found[2 * t]))
            new.append(jnp.where(here, high, found[2 * t + 1]))
        return tuple(new)

    found = blocks(0, NDEV, UNPACK_OWNERS, one, tuple(jnp.zeros((8, 128), F32) for _ in range(2 * TILES)))
    for t in range(TILES):
        cols = slice(128 * t, 128 * t + 128)
        dep[0:8, cols] = found[2 * t] - innov[0:8, cols]
        dep[8:16, cols] = found[2 * t + 1] - innov[8:16, cols]


def unpack(ret, owner, rank, innov):
    return pl.pallas_call(
        unpack_kernel,
        out_shape=jax.ShapeDtypeStruct((LEV, PROF), F32),
        in_specs=[pl.BlockSpec(memory_space=pltpu.VMEM)] * 4,
        out_specs=pl.BlockSpec(memory_space=pltpu.VMEM),
        compiler_params=pltpu.CompilerParams(vmem_limit_bytes=VMEM_LIMIT),
        name="unpack",
    )(ret, owner, rank, innov)


def pack_sides(main, low_side, high_side, lev):
    slot = lane_iota(lev) // 16

    def group(g, carry):
        low = jnp.zeros((lev, 128), F32)
        high = jnp.zeros((lev, 128), F32)
        for m in range(8):
            at = pl.ds(pl.multiple_of((STEPS + 8 * g + m) * lev, lev), lev)
            here = slot == m
            first = main[0, at, :]
            last = main[1, at, :]
            low = jnp.where(here, first if m == 0 else pltpu.roll(first, 16 * m, axis=1), low)
            high = jnp.where(here, last if m == 7 else pltpu.roll(last, 16 * m + 16, axis=1), high)
        at = pl.ds(pl.multiple_of(g * lev, lev), lev)
        low_side[at, :] = low
        high_side[at, :] = high
        return carry

    lax.fori_loop(0, CX // 8, group, 0)


def unpack_sides(from_high, from_low, side, lev):
    left = lane_iota(lev) < 64

    def group(g, carry):
        at = pl.ds(pl.multiple_of(g * lev, lev), lev)
        right_strip = from_high[at, :]
        left_strip = from_low[at, :]
        for m in range(8):
            right = right_strip if m == 0 else pltpu.roll(right_strip, 128 - 16 * m, axis=1)
            leftv = left_strip if m == 7 else pltpu.roll(left_strip, 112 - 16 * m, axis=1)
            side[pl.ds(pl.multiple_of((8 * g + m) * lev, lev), lev), :] = jnp.where(left, right, leftv)
        return carry

    lax.fori_loop(0, GROUPS, group, 0)


def halo_copies(main, low_side, high_side, from_high, from_low, send_sem, recv_sem, gx, gy, lev):
    west, east = (gx + NGX - 1) % NGX, (gx + 1) % NGX
    south, north = (gy + NGY - 1) % NGY, (gy + 1) % NGY

    def rows(ref, start, count):
        at = pl.ds(start * lev, count * lev)
        return ref.at[:, at, :] if len(ref.shape) == 3 else ref.at[at, :]

    plan = (
        (rows(main, STEPS, STEPS), rows(main, STEPS + CX, STEPS), (west, gy)),
        (rows(main, CX, STEPS), rows(main, 0, STEPS), (east, gy)),
        (rows(low_side, 0, 8), rows(from_high, 2, 8), (gx, south)),
        (rows(high_side, 0, 8), rows(from_low, 2, 8), (gx, north)),
        (rows(low_side, 0, 2), rows(from_high, 10, 2), (west, south)),
        (rows(low_side, 6, 2), rows(from_high, 0, 2), (east, south)),
        (rows(high_side, 0, 2), rows(from_low, 10, 2), (west, north)),
        (rows(high_side, 6, 2), rows(from_low, 0, 2), (east, north)),
    )
    return [
        pltpu.make_async_remote_copy(
            src_ref=src,
            dst_ref=dst,
            send_sem=send_sem.at[i],
            recv_sem=recv_sem.at[i],
            device_id=device,
            device_id_type=MESH,
        )
        for i, (src, dst, device) in enumerate(plan)
    ]


def next_cols(parts, last):
    rolled = [pltpu.roll(part, 127, axis=1) for part in parts]
    return [jnp.where(last, rolled[(i + 1) % 3], rolled[i]) for i in range(3)]


def prev_cols(parts, first):
    rolled = [pltpu.roll(part, 1, axis=1) for part in parts]
    return [jnp.where(first, rolled[(i + 2) % 3], rolled[i]) for i in range(3)]


def blocks(start, count, width, body, carry):
    def many(i, carry):
        for q in range(width):
            carry = body(start + width * i + q, carry)
        return carry

    carry = lax.fori_loop(0, count // width, many, carry)
    for q in range(count - count % width, count):
        carry = body(start + q, carry)
    return carry


def build_faces(coef, coef_side, gy):
    lane = lane_iota(1)
    first_part = jnp.where(gy < NGY - 1, 1.0, 0.0).astype(F32)
    last_part = jnp.where(gy > 0, 1.0, 0.0).astype(F32)
    inside = jnp.where(lane < 64, first_part, last_part)
    last, first = lane == 127, lane == 0

    def row(r, which):
        at = pl.ds(r * 8 + which, 1)
        return [coef[0, at, :], coef[1, at, :], coef_side[pl.ds((r + SPAD) * 8 + which, 1), :]]

    def put(r, which, parts):
        at = pl.ds(r * 8 + which, 1)
        coef[0, at, :] = parts[0]
        coef[1, at, :] = parts[1]
        coef_side[pl.ds((r + SPAD) * 8 + which, 1), :] = parts[2]

    def wet_row(r):
        one, two, side = row(r, 2)
        return [one, two, side * inside]

    def one(r, wet):
        ahead = wet_row(r + 1)
        zonal, merid = row(r, 0), row(r, 1)
        north = next_cols(wet, last)
        south = prev_cols(wet, first)
        merid_south = prev_cols(merid, first)
        put(r, 0, [z * w * a for z, w, a in zip(zonal, wet, ahead)])
        put(r, 1, [m * w * n for m, w, n in zip(merid, wet, north)])
        put(r, 3, [m * w * n for m, w, n in zip(merid_south, south, wet)])
        return tuple(ahead)

    blocks(0, ROWS - 1, 8, one, tuple(wet_row(0)))


def diffuse(first_main, first_side, second_main, second_side, coef, coef_side):
    lane = lane_iota(LEV)
    last, first = lane == 127, lane == 0

    def face(r, which):
        at = pl.ds(r * 8 + which, 1)
        parts = [coef[0, at, :], coef[1, at, :], coef_side[pl.ds((r + SPAD) * 8 + which, 1), :]]
        return [jnp.broadcast_to(part, (LEV, 128)) for part in parts]

    for step in range(STEPS):
        even = step % 2 == 0
        main, side = (first_main, first_side) if even else (second_main, second_side)
        new_main, new_side = (second_main, second_side) if even else (first_main, first_side)
        final = step == STEPS - 1

        def field(r):
            at = pl.ds(pl.multiple_of(r * LEV, LEV), LEV)
            return [main[0, at, :], main[1, at, :], side[pl.ds(pl.multiple_of((r + SPAD) * LEV, LEV), LEV), :]]

        def flux(r, here, ahead):
            return [f * (a - h) for f, a, h in zip(face(r, 0), ahead, here)]

        def one(r, carry):
            here, behind = carry[:3], carry[3:]
            ahead = field(r + 1)
            east = flux(r, here, ahead)
            north = [f * (n - h) for f, n, h in zip(face(r, 1), next_cols(here, last), here)]
            south = [f * (h - p) for f, p, h in zip(face(r, 3), prev_cols(here, first), here)]
            new = [h + ((e - w) + (n - s)) for h, e, w, n, s in zip(here, east, behind, north, south)]
            at = pl.ds(pl.multiple_of(r * LEV, LEV), LEV)
            new_main[0, at, :] = new[0]
            new_main[1, at, :] = new[1]
            if not final:
                new_side[pl.ds(pl.multiple_of((r + SPAD) * LEV, LEV), LEV), :] = new[2]
            return tuple(ahead) + tuple(east)

        start = step + 1
        here = field(start)
        behind = flux(start - 1, field(start - 1), here)
        blocks(start, ROWS - 2 * start, DIFFUSE_ROWS, one, tuple(here) + tuple(behind))


SOLVE_ROWS = 32


def load_level(ref, level, x, lev, count):
    at = pl.ds((STEPS + x) * lev + level, count, stride=lev)
    return jnp.concatenate([ref[0, at, :], ref[1, at, :]], axis=1)


def store_level(ref, level, x, lev, count, value):
    at = pl.ds((STEPS + x) * lev + level, count, stride=lev)
    ref[0, at, :] = value[:, 0:128]
    ref[1, at, :] = value[:, 128:256]


def solve_first(control, vert, mask, upper, inverse, reduced, main):
    for x in range(0, CX, SOLVE_ROWS):
        rows = slice(x, x + SOLVE_ROWS)
        wet = mask[rows, :].astype(F32)
        previous = None
        for k in range(LEV):
            rhs = wet * control[k, rows, :]
            diagonal = 1.0
            if k > 0:
                below = vert[k - 1, rows, :]
                diagonal = diagonal + below
            if k < LEV - 1:
                above = vert[k, rows, :]
                diagonal = diagonal + above
            if k > 0:
                diagonal = diagonal + below * up
                rhs = rhs + below * previous
            inv = 1.0 / diagonal
            inverse[k, rows, :] = inv
            if k < LEV - 1:
                up = -above * inv
                upper[k, rows, :] = up
            previous = rhs * inv
            if k < LEV - 1:
                reduced[k, rows, :] = previous
        value = previous
        store_level(main, LEV - 1, x, LEV, SOLVE_ROWS, value)
        for k in range(LEV - 2, -1, -1):
            value = reduced[k, rows, :] - upper[k, rows, :] * value
            store_level(main, k, x, LEV, SOLVE_ROWS, value)


def solve_last(main, control, vert, mask, upper, inverse, reduced, grad):
    for x in range(0, CX, SOLVE_ROWS):
        rows = slice(x, x + SOLVE_ROWS)
        wet = mask[rows, :].astype(F32)
        previous = None
        for k in range(LEV):
            rhs = load_level(main, k, x, LEV, SOLVE_ROWS)
            if k > 0:
                rhs = rhs + vert[k - 1, rows, :] * previous
            previous = rhs * inverse[k, rows, :]
            if k < LEV - 1:
                reduced[k, rows, :] = previous
        value = previous
        grad[LEV - 1, rows, :] = control[LEV - 1, rows, :] + wet * value
        for k in range(LEV - 2, -1, -1):
            value = reduced[k, rows, :] - upper[k, rows, :] * value
            grad[k, rows, :] = control[k, rows, :] + wet * value


def observe_all(recv, field3, adj, ret_send):
    left = lane_iota(8) < 64
    rows_b = lax.broadcasted_iota(jnp.int32, (CY, 256), 0).astype(F32)
    rows_a = lax.broadcasted_iota(jnp.int32, (CX, 256), 0).astype(F32)

    def observe(i, carry):
        pairs = []
        for h in range(2):
            one, two = recv[4 * i + 2 * h], recv[4 * i + 2 * h + 1]
            place = jnp.where(left, one[0:8], pltpu.roll(two[0:8], 64, axis=1))
            low_i = jnp.where(left, one[8:16], pltpu.roll(two[8:16], 64, axis=1))
            high_i = jnp.where(left, pltpu.roll(one[8:16], 64, axis=1), two[8:16])
            low_o = jnp.where(left, one[16:24], pltpu.roll(two[16:24], 64, axis=1))
            high_o = jnp.where(left, pltpu.roll(one[16:24], 64, axis=1), two[16:24])
            pairs.append((place, jnp.concatenate([low_i, high_i], axis=0), jnp.concatenate([low_o, high_o], axis=0)))
        place, innov, obsw = [jnp.concatenate([pairs[0][n], pairs[1][n]], axis=1) for n in range(3)]
        cell, along_x, along_y = place[0:1], place[1:2], place[2:3]
        cell_a = jnp.floor(cell * (1.0 / CY))
        cell_b = cell - CY * cell_a
        from_a = rows_a - cell_a
        from_b = rows_b - cell_b
        in_x = jnp.where(from_a == 0.0, 1.0 - along_x, jnp.where(from_a == 1.0, along_x, 0.0))
        in_y = jnp.where(from_b == 0.0, 1.0 - along_y, jnp.where(from_b == 1.0, along_y, 0.0))
        y_high = in_y.astype(BF16)
        y_low = (in_y - y_high.astype(F32)).astype(BF16)
        rows = jnp.dot(
            field3[...], jnp.concatenate([y_high, y_low, y_high], axis=0), preferred_element_type=F32
        )
        vals = jnp.sum(rows.reshape(LEV, CX, 256) * in_x[None], axis=1)
        forcing = obsw * (vals - innov)
        for h in range(2):
            cols = slice(128 * h, 128 * h + 128)
            first, second = split_pair(vals[0:8, cols], vals[8:16, cols], left)
            ret_send[4 * i + 2 * h] = first
            ret_send[4 * i + 2 * h + 1] = second
        spread = (in_x[None] * forcing[:, None, :]).reshape(LEV * CX, 256)
        high = spread.astype(BF16)
        low = (spread - high.astype(F32)).astype(BF16)
        adj[...] += lax.dot_general(
            jnp.concatenate([high, high, low], axis=1),
            jnp.concatenate([y_high, y_low, y_high], axis=1),
            (((1,), (1,)), ((), ())),
            preferred_element_type=F32,
        )
        return carry

    lax.fori_loop(0, NDEV // 4, observe, 0)


def main_kernel(
    control, sigma, vert, zonal, merid, mask, rec, inc, ret, grad,
    recv, ret_send, coef, coef_side, coef_low, coef_high, coef_from_high, coef_from_low,
    main_a, side_a, main_b, side_b, main_c, side_c,
    low_a, high_a, from_high_a, from_low_a, low_c, high_c, from_high_c, from_low_c,
    upper, inverse, reduced, field3, adj,
    rec_send_sem, rec_recv_sem, ret_send_sem, ret_recv_sem, self_sem, halo_send, halo_recv,
):
    gx, gy = lax.axis_index("gx"), lax.axis_index("gy")
    me = gx * NGY + gy

    barrier = pltpu.get_barrier_semaphore()

    def greet(d, carry):
        to = (me + d) % NDEV
        pl.semaphore_signal(barrier, inc=1, device_id=(to // NGY, to % NGY), device_id_type=MESH)
        return carry

    lax.fori_loop(1, NDEV, greet, 0)
    pl.semaphore_wait(barrier, NDEV - 1)

    def rec_copy(to):
        return pltpu.make_async_remote_copy(
            src_ref=rec.at[to], dst_ref=recv.at[me], send_sem=rec_send_sem, recv_sem=rec_recv_sem,
            device_id=(to // NGY, to % NGY), device_id_type=MESH,
        )

    def ret_copy(to):
        return pltpu.make_async_remote_copy(
            src_ref=ret_send.at[to], dst_ref=ret.at[me], send_sem=ret_send_sem, recv_sem=ret_recv_sem,
            device_id=(to // NGY, to % NGY), device_id_type=MESH,
        )

    for half in range(2):
        coef[half, STEPS * 8 : (STEPS + CX) * 8, :] = jnp.zeros((CX * 8, 128), F32)
    for x in range(0, CX, SOLVE_ROWS):
        rows = slice(x, x + SOLVE_ROWS)
        store_level(coef, 0, x, 8, SOLVE_ROWS, zonal[rows, :])
        store_level(coef, 1, x, 8, SOLVE_ROWS, merid[rows, :])
        store_level(coef, 2, x, 8, SOLVE_ROWS, mask[rows, :].astype(F32))
    pack_sides(coef, coef_low, coef_high, 8)
    coef_copies = halo_copies(
        coef, coef_low, coef_high, coef_from_high, coef_from_low, halo_send.at[0], halo_recv.at[0], gx, gy, 8
    )
    for copy in coef_copies:
        copy.start()

    solve_first(control, vert, mask, upper, inverse, reduced, main_a)
    pack_sides(main_a, low_a, high_a, LEV)
    field_copies = halo_copies(
        main_a, low_a, high_a, from_high_a, from_low_a, halo_send.at[1], halo_recv.at[1], gx, gy, LEV
    )
    for copy in field_copies:
        copy.start()

    def send_rec(d, carry):
        rec_copy((me + d) % NDEV).start()
        return carry

    lax.fori_loop(1, NDEV, send_rec, 0)
    own = pltpu.make_async_copy(rec.at[me], recv.at[me], self_sem)
    own.start()

    for copy in coef_copies:
        copy.wait()
    unpack_sides(coef_from_high, coef_from_low, coef_side, 8)
    build_faces(coef, coef_side, gy)
    for copy in field_copies:
        copy.wait()
    unpack_sides(from_high_a, from_low_a, side_a, LEV)
    diffuse(main_a, side_a, main_b, side_b, coef, coef_side)

    def scale(k, carry):
        for x in range(0, CX, 16):
            value = sigma[k, x : x + 16, :] * load_level(main_a, k, x, LEV, 16)
            inc[k, x : x + 16, :] = value
            high = value.astype(BF16)
            low = (value - high.astype(F32)).astype(BF16)
            at = pl.ds(pl.multiple_of(k * CX + x, 16), 16)
            field3[at, 0:256] = high
            field3[at, 256:512] = high
            field3[at, 512:768] = low
        return carry

    lax.fori_loop(0, LEV, scale, 0)

    own.wait()
    whole = pltpu.make_async_remote_copy(
        src_ref=rec.at[pl.ds(0, NDEV - 1)], dst_ref=recv.at[pl.ds(0, NDEV - 1)],
        send_sem=rec_send_sem, recv_sem=rec_recv_sem, device_id=(gx, gy), device_id_type=MESH,
    )
    whole.wait_recv()
    whole.wait_send()

    adj[...] = jnp.zeros_like(adj)
    observe_all(recv, field3, adj, ret_send)

    def weigh(k, carry):
        for x in range(0, CX, SOLVE_ROWS):
            at = pl.ds(pl.multiple_of(k * CX + x, SOLVE_ROWS), SOLVE_ROWS)
            store_level(main_c, k, x, LEV, SOLVE_ROWS, sigma[k, x : x + SOLVE_ROWS, :] * adj[at, :])
        return carry

    lax.fori_loop(0, LEV, weigh, 0)
    pack_sides(main_c, low_c, high_c, LEV)
    adj_copies = halo_copies(
        main_c, low_c, high_c, from_high_c, from_low_c, halo_send.at[2], halo_recv.at[2], gx, gy, LEV
    )
    for copy in adj_copies:
        copy.start()

    def send_ret(d, carry):
        ret_copy((me + d) % NDEV).start()
        return carry

    lax.fori_loop(1, NDEV, send_ret, 0)
    own = pltpu.make_async_copy(ret_send.at[me], ret.at[me], self_sem)
    own.start()

    for copy in adj_copies:
        copy.wait()
    unpack_sides(from_high_c, from_low_c, side_c, LEV)
    diffuse(main_c, side_c, main_b, side_b, coef, coef_side)
    solve_last(main_c, control, vert, mask, upper, inverse, reduced, grad)

    own.wait()
    whole = pltpu.make_async_remote_copy(
        src_ref=ret_send.at[pl.ds(0, NDEV - 1)], dst_ref=ret.at[pl.ds(0, NDEV - 1)],
        send_sem=ret_send_sem, recv_sem=ret_recv_sem, device_id=(gx, gy), device_id_type=MESH,
    )
    whole.wait_recv()
    whole.wait_send()


def gradient_call(control, sigma, vert, zonal, merid, mask, rec):
    vmem = pl.BlockSpec(memory_space=pltpu.VMEM)

    def field(rows, lanes, lev=LEV):
        shape = (rows * lev, 128)
        return pltpu.VMEM(shape if lanes == 128 else (2,) + shape, F32)

    def sides(lev):
        return [field(8, 128, lev), field(8, 128, lev), field(GROUPS, 128, lev), field(GROUPS, 128, lev)]

    return pl.pallas_call(
        main_kernel,
        out_shape=(
            jax.ShapeDtypeStruct((LEV, CX, CY), F32),
            jax.ShapeDtypeStruct((NDEV, 8, 128), F32),
            jax.ShapeDtypeStruct((LEV, CX, CY), F32),
        ),
        in_specs=[vmem] * 7,
        out_specs=(vmem,) * 3,
        scratch_shapes=[
            pltpu.VMEM((NDEV, REC, 128), F32),
            pltpu.VMEM((NDEV, 8, 128), F32),
            field(ROWS, 256, 8), field(SROWS, 128, 8), *sides(8),
            field(ROWS, 256), field(SROWS, 128),
            field(ROWS, 256), field(SROWS, 128),
            field(ROWS, 256), field(SROWS, 128),
            *sides(LEV), *sides(LEV),
            pltpu.VMEM((LEV, CX, CY), F32),
            pltpu.VMEM((LEV, CX, CY), F32),
            pltpu.VMEM((LEV, CX, CY), F32),
            pltpu.VMEM((LEV * CX, 3 * CY), BF16),
            pltpu.VMEM((LEV * CX, CY), F32),
            pltpu.SemaphoreType.DMA, pltpu.SemaphoreType.DMA, pltpu.SemaphoreType.DMA, pltpu.SemaphoreType.DMA,
            pltpu.SemaphoreType.DMA,
            pltpu.SemaphoreType.DMA((3, 8)), pltpu.SemaphoreType.DMA((3, 8)),
        ],
        compiler_params=pltpu.CompilerParams(
            collective_id=0, has_side_effects=True, vmem_limit_bytes=VMEM_LIMIT
        ),
        name="gradient",
    )(control, sigma, vert, zonal, merid, mask, rec)


def shards(control, sigma, vert_diff, zonal_diff, merid_diff, ocean_mask, owner, cell, interp_weights, innovation, obs_weight):
    owner_rows = owner.reshape(TILES, 128)
    cell_rows = cell.reshape(TILES, 128)
    rec, rank = pack(owner_rows, cell_rows, interp_weights, innovation, obs_weight)
    increment, ret, gradient = gradient_call(
        control, sigma, vert_diff, zonal_diff, merid_diff, ocean_mask, rec
    )
    departures = unpack(ret, owner_rows, rank, innovation)
    return increment, departures, gradient


def solution(mesh):
    in_specs = (
        P(None, "gx", "gy"),
        P(None, "gx", "gy"),
        P(None, "gx", "gy"),
        P("gx", "gy"),
        P("gx", "gy"),
        P("gx", "gy"),
        P(("gx", "gy"), None),
        P(("gx", "gy")),
        P(None, ("gx", "gy")),
        P(None, ("gx", "gy")),
        P(None, ("gx", "gy")),
    )
    out_specs = (P(None, "gx", "gy"), P(None, ("gx", "gy")), P(None, "gx", "gy"))
    return jax.shard_map(shards, mesh=mesh, in_specs=in_specs, out_specs=out_specs, check_vma=False)
```

```python
import functools

import jax
import jax.numpy as jnp
from jax import lax
from jax.experimental import pallas as pl
from jax.experimental.pallas import tpu as pltpu
from jax.sharding import PartitionSpec as P

MESH = pl.DeviceIdType.MESH
F32 = jnp.float32
BF16 = jnp.bfloat16
VMEM_LIMIT = 60 * 1024 * 1024

LEV = 16
STEPS = 10
CX = 64
CY = 256
NGX = 16
NGY = 8
NDEV = NGX * NGY
PROF = 2048
CAP = 64
TILES = PROF // 128
ROWS = CX + 2 * STEPS
SPAD = 6
SROWS = 96
GROUPS = 12
REC = 18
DIFFUSE_ROWS = 16
PACK_PAIRS = 8
OBSERVE_TILES = 8
UNPACK_TILES = 2


def lane_iota(rows):
    return lax.broadcasted_iota(jnp.int32, (rows, 128), 1)


def blocks(start, count, width, body, carry):
    def many(i, carry):
        for q in range(width):
            carry = body(start + width * i + q, carry)
        return carry

    carry = lax.fori_loop(0, count // width, many, carry)
    for q in range(count - count % width, count):
        carry = body(start + q, carry)
    return carry


def lane_gather(source, lane):
    return jnp.take_along_axis(source, lane, axis=1, mode="promise_in_bounds")


def split_pair(low, high, left):
    first = jnp.where(left, low, pltpu.roll(high, 64, axis=1))
    second = jnp.where(left, pltpu.roll(low, 64, axis=1), high)
    return first, second


def pack_kernel(owner, cell, weights, innov, obsw, rec, rank_out, tab, lanes, tiles, cst, found_ref):
    rows_o = lax.broadcasted_iota(jnp.int32, (NDEV, 256), 0)
    before = (
        lax.broadcasted_iota(jnp.int32, (256, 256), 0) < lax.broadcasted_iota(jnp.int32, (256, 256), 1)
    ).astype(F32).astype(BF16)
    ones = jnp.ones((256, 256), BF16)
    rows_r = lax.broadcasted_iota(jnp.int32, (CAP, 256), 0)
    cols_p = lax.broadcasted_iota(jnp.int32, (CAP, 256), 1)
    earlier = jnp.zeros((NDEV, 256), F32)
    table = jnp.zeros((NDEV, 128), F32)
    for block in range(PROF // 256):
        owners = jnp.concatenate([owner[2 * block : 2 * block + 1, :], owner[2 * block + 1 : 2 * block + 2, :]], axis=1)
        hot = (rows_o == owners).astype(F32)
        hot16 = hot.astype(BF16)
        count = earlier + jnp.dot(hot16, before, preferred_element_type=F32)
        rank = jnp.sum(hot * count, axis=0, keepdims=True).astype(jnp.int32)
        earlier = earlier + jnp.dot(hot16, ones, preferred_element_type=F32)
        rank_out[2 * block : 2 * block + 1, :] = rank[:, :128]
        rank_out[2 * block + 1 : 2 * block + 2, :] = rank[:, 128:]
        same = rows_r == rank
        lane = jnp.where(same, cols_p % 128, 0).astype(F32).astype(BF16)
        tile = jnp.where(same, 2 * block + 1 + cols_p // 128, 0).astype(F32).astype(BF16)
        table = table + lax.dot_general(
            hot16, jnp.concatenate([lane, tile], axis=0), (((1,), (1,)), ((), ())), preferred_element_type=F32
        )
    tab[...] = table.astype(jnp.int32)
    half = lane_iota(NDEV // 2) < 64
    even, odd = tab[pl.ds(0, NDEV // 2, stride=2), :], tab[pl.ds(1, NDEV // 2, stride=2), :]
    lanes[...] = jnp.where(half, even, pltpu.roll(odd, 64, axis=1))
    tiles[...] = jnp.where(half, pltpu.roll(even, 64, axis=1), odd)

    cst[...] = jnp.zeros_like(cst)
    for tile in range(TILES):
        cols = slice(128 * tile, 128 * tile + 128)
        to = slice(128 * (tile // 2), 128 * (tile // 2) + 128)
        row = 4 * (tile % 2)
        cst[row : row + 1, to] = cell[tile : tile + 1, :].astype(F32)
        cst[row + 1 : row + 2, to] = weights[1:2, cols] + weights[3:4, cols]
        cst[row + 2 : row + 3, to] = weights[2:3, cols] + weights[3:4, cols]

    left = lane_iota(8) < 64
    left_row = lane_iota(1) < 64
    below = lax.broadcasted_iota(jnp.int32, (8, 128), 0) // 4

    def pair(j, carry):
        lane = jnp.broadcast_to(lanes[pl.ds(j, 1), :], (8, 128))
        tile_of = jnp.broadcast_to(tiles[pl.ds(j, 1), :], (8, 128))
        tile_up = tile_of - below
        zero = jnp.zeros((8, 128), F32)
        place, found = zero, [zero] * 4
        for tile in range(TILES):
            cols = slice(128 * tile, 128 * tile + 128)
            here = tile_of == tile + 1
            found = [
                jnp.where(here, lane_gather(source, lane), old)
                for source, old in zip((innov[0:8, cols], innov[8:16, cols], obsw[0:8, cols], obsw[8:16, cols]), found)
            ]
            if tile % 2 == 0:
                both = lane_gather(cst[:, 64 * tile : 64 * tile + 128], lane)
                place = jnp.where(tile_up == tile + 1, both, place)
        found_ref[j] = jnp.concatenate(found + [place], axis=0)
        return carry

    blocks(0, NDEV // 2, PACK_PAIRS, pair, 0)

    def part(j, carry):
        both = found_ref[j]
        place = both[32:36] + both[36:40]
        turned = pltpu.roll(place, 64, axis=1)
        first_i, second_i = split_pair(both[0:8], both[8:16], left)
        first_o, second_o = split_pair(both[16:24], both[24:32], left)
        for q, parts in enumerate((
            [first_i, first_o, jnp.where(left_row, place[0:1], turned[1:2]), place[2:3]],
            [second_i, second_o, jnp.where(left_row, turned[0:1], place[1:2]), turned[2:3]],
        )):
            for row, value in zip((0, 8, 16, 17), parts):
                rec[2 * j + q, row : row + value.shape[0], :] = value
        return carry

    blocks(0, NDEV // 2, 8, part, 0)


def pack(owner, cell, weights, innov, obsw):
    return pl.pallas_call(
        pack_kernel,
        out_shape=(
            jax.ShapeDtypeStruct((NDEV, REC, 128), F32),
            jax.ShapeDtypeStruct((TILES, 128), jnp.int32),
        ),
        in_specs=[pl.BlockSpec(memory_space=pltpu.VMEM)] * 5,
        out_specs=(pl.BlockSpec(memory_space=pltpu.VMEM),) * 2,
        scratch_shapes=[
            pltpu.VMEM((NDEV, 128), jnp.int32),
            pltpu.VMEM((NDEV // 2, 128), jnp.int32),
            pltpu.VMEM((NDEV // 2, 128), jnp.int32),
            pltpu.VMEM((8, PROF // 2), F32),
            pltpu.VMEM((NDEV // 2, 40, 128), F32),
        ],
        compiler_params=pltpu.CompilerParams(vmem_limit_bytes=VMEM_LIMIT),
        name="pack",
    )(owner, cell, weights, innov, obsw)


def unpack_kernel(ret, owner, rank, innov, dep, low_ref, high_ref):
    left = lane_iota(8) < 64

    def pair(j, carry):
        one, two = ret[2 * j], ret[2 * j + 1]
        low_ref[j] = jnp.where(left, one, pltpu.roll(two, 64, axis=1))
        high_ref[j] = jnp.where(left, pltpu.roll(one, 64, axis=1), two)
        return carry

    blocks(0, NDEV // 2, 16, pair, 0)

    def tile(t, carry):
        owners = jnp.broadcast_to(owner[pl.ds(t, 1), :], (8, 128))
        lane = jnp.broadcast_to(rank[pl.ds(t, 1), :], (8, 128)) + 64 * (owners % 2)
        pair_of = owners // 2
        low = high = jnp.zeros((8, 128), F32)
        for j in range(NDEV // 2):
            here = pair_of == j
            low = jnp.where(here, lane_gather(low_ref[j], lane), low)
            high = jnp.where(here, lane_gather(high_ref[j], lane), high)
        cols = pl.ds(pl.multiple_of(128 * t, 128), 128)
        dep[0:8, cols] = low - innov[0:8, cols]
        dep[8:16, cols] = high - innov[8:16, cols]
        return carry

    blocks(0, TILES, UNPACK_TILES, tile, 0)


def unpack(ret, owner, rank, innov):
    return pl.pallas_call(
        unpack_kernel,
        out_shape=jax.ShapeDtypeStruct((LEV, PROF), F32),
        in_specs=[pl.BlockSpec(memory_space=pltpu.VMEM)] * 4,
        out_specs=pl.BlockSpec(memory_space=pltpu.VMEM),
        scratch_shapes=[pltpu.VMEM((NDEV // 2, 8, 128), F32)] * 2,
        compiler_params=pltpu.CompilerParams(vmem_limit_bytes=VMEM_LIMIT),
        name="unpack",
    )(ret, owner, rank, innov)


def pack_sides(main, low_side, high_side, lev):
    slot = lane_iota(lev) // 16

    def group(g, carry):
        low = jnp.zeros((lev, 128), F32)
        high = jnp.zeros((lev, 128), F32)
        for m in range(8):
            at = pl.ds(pl.multiple_of((STEPS + 8 * g + m) * lev, lev), lev)
            here = slot == m
            first = main[0, at, :]
            last = main[1, at, :]
            low = jnp.where(here, first if m == 0 else pltpu.roll(first, 16 * m, axis=1), low)
            high = jnp.where(here, last if m == 7 else pltpu.roll(last, 16 * m + 16, axis=1), high)
        at = pl.ds(pl.multiple_of(g * lev, lev), lev)
        low_side[at, :] = low
        high_side[at, :] = high
        return carry

    lax.fori_loop(0, CX // 8, group, 0)


def unpack_sides(from_high, from_low, side, lev):
    left = lane_iota(lev) < 64

    def group(g, carry):
        at = pl.ds(pl.multiple_of(g * lev, lev), lev)
        right_strip = from_high[at, :]
        left_strip = from_low[at, :]
        for m in range(8):
            right = right_strip if m == 0 else pltpu.roll(right_strip, 128 - 16 * m, axis=1)
            leftv = left_strip if m == 7 else pltpu.roll(left_strip, 112 - 16 * m, axis=1)
            side[pl.ds(pl.multiple_of((8 * g + m) * lev, lev), lev), :] = jnp.where(left, right, leftv)
        return carry

    lax.fori_loop(0, GROUPS, group, 0)


def halo_copies(main, low_side, high_side, from_high, from_low, send_sem, recv_sem, gx, gy, lev):
    west, east = (gx + NGX - 1) % NGX, (gx + 1) % NGX
    south, north = (gy + NGY - 1) % NGY, (gy + 1) % NGY

    def rows(ref, start, count):
        at = pl.ds(start * lev, count * lev)
        return ref.at[:, at, :] if len(ref.shape) == 3 else ref.at[at, :]

    plan = (
        (rows(main, STEPS, STEPS), rows(main, STEPS + CX, STEPS), (west, gy)),
        (rows(main, CX, STEPS), rows(main, 0, STEPS), (east, gy)),
        (rows(low_side, 0, 8), rows(from_high, 2, 8), (gx, south)),
        (rows(high_side, 0, 8), rows(from_low, 2, 8), (gx, north)),
        (rows(low_side, 0, 2), rows(from_high, 10, 2), (west, south)),
        (rows(low_side, 6, 2), rows(from_high, 0, 2), (east, south)),
        (rows(high_side, 0, 2), rows(from_low, 10, 2), (west, north)),
        (rows(high_side, 6, 2), rows(from_low, 0, 2), (east, north)),
    )
    return [
        pltpu.make_async_remote_copy(
            src_ref=src,
            dst_ref=dst,
            send_sem=send_sem.at[i],
            recv_sem=recv_sem.at[i],
            device_id=device,
            device_id_type=MESH,
        )
        for i, (src, dst, device) in enumerate(plan)
    ]


def next_cols(parts, last):
    rolled = [pltpu.roll(part, 127, axis=1) for part in parts]
    return [jnp.where(last, rolled[(i + 1) % 3], rolled[i]) for i in range(3)]


def prev_cols(parts, first):
    rolled = [pltpu.roll(part, 1, axis=1) for part in parts]
    return [jnp.where(first, rolled[(i + 2) % 3], rolled[i]) for i in range(3)]


def build_faces(coef, coef_side, gy):
    lane = lane_iota(1)
    first_part = jnp.where(gy < NGY - 1, 1.0, 0.0).astype(F32)
    last_part = jnp.where(gy > 0, 1.0, 0.0).astype(F32)
    inside = jnp.where(lane < 64, first_part, last_part)
    last, first = lane == 127, lane == 0

    def row(r, which):
        at = pl.ds(r * 8 + which, 1)
        return [coef[0, at, :], coef[1, at, :], coef_side[pl.ds((r + SPAD) * 8 + which, 1), :]]

    def put(r, which, parts):
        at = pl.ds(r * 8 + which, 1)
        coef[0, at, :] = parts[0]
        coef[1, at, :] = parts[1]
        coef_side[pl.ds((r + SPAD) * 8 + which, 1), :] = parts[2]

    def wet_row(r):
        one, two, side = row(r, 2)
        return [one, two, side * inside]

    def one(r, wet):
        ahead = wet_row(r + 1)
        zonal, merid = row(r, 0), row(r, 1)
        north = next_cols(wet, last)
        south = prev_cols(wet, first)
        merid_south = prev_cols(merid, first)
        put(r, 0, [z * w * a for z, w, a in zip(zonal, wet, ahead)])
        put(r, 1, [m * w * n for m, w, n in zip(merid, wet, north)])
        put(r, 3, [m * w * n for m, w, n in zip(merid_south, south, wet)])
        return tuple(ahead)

    blocks(0, ROWS - 1, 8, one, tuple(wet_row(0)))


def diffuse(first_main, first_side, second_main, second_side, coef, coef_side):
    lane = lane_iota(LEV)
    last, first = lane == 127, lane == 0

    def face(r, which):
        at = pl.ds(r * 8 + which, 1)
        parts = [coef[0, at, :], coef[1, at, :], coef_side[pl.ds((r + SPAD) * 8 + which, 1), :]]
        return [jnp.broadcast_to(part, (LEV, 128)) for part in parts]

    for step in range(STEPS):
        even = step % 2 == 0
        main, side = (first_main, first_side) if even else (second_main, second_side)
        new_main, new_side = (second_main, second_side) if even else (first_main, first_side)
        final = step == STEPS - 1

        def field(r):
            at = pl.ds(pl.multiple_of(r * LEV, LEV), LEV)
            return [main[0, at, :], main[1, at, :], side[pl.ds(pl.multiple_of((r + SPAD) * LEV, LEV), LEV), :]]

        def flux(r, here, ahead):
            return [f * (a - h) for f, a, h in zip(face(r, 0), ahead, here)]

        def one(r, carry):
            here, behind = carry[:3], carry[3:]
            ahead = field(r + 1)
            east = flux(r, here, ahead)
            north = [f * (n - h) for f, n, h in zip(face(r, 1), next_cols(here, last), here)]
            south = [f * (h - p) for f, p, h in zip(face(r, 3), prev_cols(here, first), here)]
            new = [h + ((e - w) + (n - s)) for h, e, w, n, s in zip(here, east, behind, north, south)]
            at = pl.ds(pl.multiple_of(r * LEV, LEV), LEV)
            new_main[0, at, :] = new[0]
            new_main[1, at, :] = new[1]
            if not final:
                new_side[pl.ds(pl.multiple_of((r + SPAD) * LEV, LEV), LEV), :] = new[2]
            return tuple(ahead) + tuple(east)

        start = step + 1
        here = field(start)
        behind = flux(start - 1, field(start - 1), here)
        blocks(start, ROWS - 2 * start, DIFFUSE_ROWS, one, tuple(here) + tuple(behind))


SOLVE_ROWS = 32


def load_level(ref, level, x, lev, count):
    at = pl.ds((STEPS + x) * lev + level, count, stride=lev)
    return jnp.concatenate([ref[0, at, :], ref[1, at, :]], axis=1)


def store_level(ref, level, x, lev, count, value):
    at = pl.ds((STEPS + x) * lev + level, count, stride=lev)
    ref[0, at, :] = value[:, 0:128]
    ref[1, at, :] = value[:, 128:256]


def solve_first(control, vert, mask, upper, inverse, reduced, main):
    for x in range(0, CX, SOLVE_ROWS):
        rows = slice(x, x + SOLVE_ROWS)
        wet = mask[rows, :].astype(F32)
        previous = None
        for k in range(LEV):
            rhs = wet * control[k, rows, :]
            diagonal = 1.0
            if k > 0:
                below = vert[k - 1, rows, :]
                diagonal = diagonal + below
            if k < LEV - 1:
                above = vert[k, rows, :]
                diagonal = diagonal + above
            if k > 0:
                diagonal = diagonal + below * up
                rhs = rhs + below * previous
            inv = 1.0 / diagonal
            inverse[k, rows, :] = inv
            if k < LEV - 1:
                up = -above * inv
                upper[k, rows, :] = up
            previous = rhs * inv
            if k < LEV - 1:
                reduced[k, rows, :] = previous
        value = previous
        store_level(main, LEV - 1, x, LEV, SOLVE_ROWS, value)
        for k in range(LEV - 2, -1, -1):
            value = reduced[k, rows, :] - upper[k, rows, :] * value
            store_level(main, k, x, LEV, SOLVE_ROWS, value)


def solve_last(main, control, vert, mask, upper, inverse, reduced, grad):
    for x in range(0, CX, SOLVE_ROWS):
        rows = slice(x, x + SOLVE_ROWS)
        wet = mask[rows, :].astype(F32)
        previous = None
        for k in range(LEV):
            rhs = load_level(main, k, x, LEV, SOLVE_ROWS)
            if k > 0:
                rhs = rhs + vert[k - 1, rows, :] * previous
            previous = rhs * inverse[k, rows, :]
            if k < LEV - 1:
                reduced[k, rows, :] = previous
        value = previous
        grad[LEV - 1, rows, :] = control[LEV - 1, rows, :] + wet * value
        for k in range(LEV - 2, -1, -1):
            value = reduced[k, rows, :] - upper[k, rows, :] * value
            grad[k, rows, :] = control[k, rows, :] + wet * value


def observe_all(recv, field3, adj, ret_send):
    left = lane_iota(8) < 64
    left_row = lane_iota(1) < 64
    width = OBSERVE_TILES * 128
    rows_b = lax.broadcasted_iota(jnp.int32, (CY, width), 0).astype(F32)
    rows_a = lax.broadcasted_iota(jnp.int32, (CX, width), 0).astype(F32)

    def observe(i, carry):
        parts = []
        for h in range(OBSERVE_TILES):
            one, two = recv[2 * (OBSERVE_TILES * i + h)], recv[2 * (OBSERVE_TILES * i + h) + 1]
            turned_one, turned_two = pltpu.roll(one, 64, axis=1), pltpu.roll(two, 64, axis=1)
            parts.append((
                jnp.where(left_row, one[16:17], turned_two[16:17]),
                jnp.where(left_row, turned_one[16:17], two[16:17]),
                jnp.where(left_row, one[17:18], turned_two[17:18]),
                jnp.where(left, one[0:8], turned_two[0:8]),
                jnp.where(left, turned_one[0:8], two[0:8]),
                jnp.where(left, one[8:16], turned_two[8:16]),
                jnp.where(left, turned_one[8:16], two[8:16]),
            ))
        cell, along_x, along_y, low_i, high_i, low_o, high_o = [jnp.concatenate(part, axis=1) for part in zip(*parts)]
        innov = jnp.concatenate([low_i, high_i], axis=0)
        obsw = jnp.concatenate([low_o, high_o], axis=0)
        cell_a = jnp.floor(cell * (1.0 / CY))
        cell_b = cell - CY * cell_a
        from_a = rows_a - cell_a
        from_b = rows_b - cell_b
        in_x = jnp.where(from_a == 0.0, 1.0 - along_x, jnp.where(from_a == 1.0, along_x, 0.0))
        in_y = jnp.where(from_b == 0.0, 1.0 - along_y, jnp.where(from_b == 1.0, along_y, 0.0))
        y_high = in_y.astype(BF16)
        y_low = (in_y - y_high.astype(F32)).astype(BF16)
        y_rows = jnp.concatenate([y_high, y_low, y_high], axis=0)
        vals = []
        for k in range(0, LEV, 4):
            rows = jnp.dot(field3[CX * k : CX * (k + 4), :], y_rows, preferred_element_type=F32)
            vals.append(jnp.sum(rows.reshape(4, CX, width) * in_x[None], axis=1))
        vals = jnp.concatenate(vals, axis=0)
        forcing = obsw * (vals - innov)
        for h in range(OBSERVE_TILES):
            cols = slice(128 * h, 128 * h + 128)
            first, second = split_pair(vals[0:8, cols], vals[8:16, cols], left)
            ret_send[2 * (OBSERVE_TILES * i + h)] = first
            ret_send[2 * (OBSERVE_TILES * i + h) + 1] = second
        spread = (in_x[None] * forcing[:, None, :]).reshape(LEV * CX, width)
        high = spread.astype(BF16)
        low = (spread - high.astype(F32)).astype(BF16)
        adj[...] += lax.dot_general(
            jnp.concatenate([high, high, low], axis=1),
            jnp.concatenate([y_high, y_low, y_high], axis=1),
            (((1,), (1,)), ((), ())),
            preferred_element_type=F32,
        )
        return carry

    lax.fori_loop(0, NDEV // 2 // OBSERVE_TILES, observe, 0)


def main_kernel(
    control, sigma, vert, zonal, merid, mask, rec, inc, ret, grad,
    recv, ret_send, coef, coef_side, coef_low, coef_high, coef_from_high, coef_from_low,
    main_a, side_a, main_b, side_b, main_c, side_c,
    low_a, high_a, from_high_a, from_low_a, low_c, high_c, from_high_c, from_low_c,
    upper, inverse, reduced, field3, adj,
    rec_send_sem, rec_recv_sem, ret_send_sem, ret_recv_sem, self_sem, halo_send, halo_recv,
):
    gx, gy = lax.axis_index("gx"), lax.axis_index("gy")
    me = gx * NGY + gy

    barrier = pltpu.get_barrier_semaphore()

    def greet(d, carry):
        to = (me + d) % NDEV
        pl.semaphore_signal(barrier, inc=1, device_id=(to // NGY, to % NGY), device_id_type=MESH)
        return carry

    lax.fori_loop(1, NDEV, greet, 0)
    pl.semaphore_wait(barrier, NDEV - 1)

    def rec_copy(to):
        return pltpu.make_async_remote_copy(
            src_ref=rec.at[to], dst_ref=recv.at[me], send_sem=rec_send_sem, recv_sem=rec_recv_sem,
            device_id=(to // NGY, to % NGY), device_id_type=MESH,
        )

    def ret_copy(to):
        return pltpu.make_async_remote_copy(
            src_ref=ret_send.at[to], dst_ref=ret.at[me], send_sem=ret_send_sem, recv_sem=ret_recv_sem,
            device_id=(to // NGY, to % NGY), device_id_type=MESH,
        )

    for half in range(2):
        coef[half, STEPS * 8 : (STEPS + CX) * 8, :] = jnp.zeros((CX * 8, 128), F32)
    for x in range(0, CX, SOLVE_ROWS):
        rows = slice(x, x + SOLVE_ROWS)
        store_level(coef, 0, x, 8, SOLVE_ROWS, zonal[rows, :])
        store_level(coef, 1, x, 8, SOLVE_ROWS, merid[rows, :])
        store_level(coef, 2, x, 8, SOLVE_ROWS, mask[rows, :].astype(F32))
    pack_sides(coef, coef_low, coef_high, 8)
    coef_copies = halo_copies(
        coef, coef_low, coef_high, coef_from_high, coef_from_low, halo_send.at[0], halo_recv.at[0], gx, gy, 8
    )
    for copy in coef_copies:
        copy.start()

    solve_first(control, vert, mask, upper, inverse, reduced, main_a)
    pack_sides(main_a, low_a, high_a, LEV)
    field_copies = halo_copies(
        main_a, low_a, high_a, from_high_a, from_low_a, halo_send.at[1], halo_recv.at[1], gx, gy, LEV
    )
    for copy in field_copies:
        copy.start()

    def send_rec(d, carry):
        rec_copy((me + d) % NDEV).start()
        return carry

    lax.fori_loop(1, NDEV, send_rec, 0)
    own = pltpu.make_async_copy(rec.at[me], recv.at[me], self_sem)
    own.start()

    for copy in coef_copies:
        copy.wait()
    unpack_sides(coef_from_high, coef_from_low, coef_side, 8)
    build_faces(coef, coef_side, gy)
    for copy in field_copies:
        copy.wait()
    unpack_sides(from_high_a, from_low_a, side_a, LEV)
    diffuse(main_a, side_a, main_b, side_b, coef, coef_side)

    def scale(k, carry):
        for x in range(0, CX, 16):
            value = sigma[k, x : x + 16, :] * load_level(main_a, k, x, LEV, 16)
            inc[k, x : x + 16, :] = value
            high = value.astype(BF16)
            low = (value - high.astype(F32)).astype(BF16)
            at = pl.ds(pl.multiple_of(k * CX + x, 16), 16)
            field3[at, 0:256] = high
            field3[at, 256:512] = high
            field3[at, 512:768] = low
        return carry

    lax.fori_loop(0, LEV, scale, 0)

    own.wait()
    whole = pltpu.make_async_remote_copy(
        src_ref=rec.at[pl.ds(0, NDEV - 1)], dst_ref=recv.at[pl.ds(0, NDEV - 1)],
        send_sem=rec_send_sem, recv_sem=rec_recv_sem, device_id=(gx, gy), device_id_type=MESH,
    )
    whole.wait_recv()
    whole.wait_send()

    adj[...] = jnp.zeros_like(adj)
    observe_all(recv, field3, adj, ret_send)

    def weigh(k, carry):
        for x in range(0, CX, SOLVE_ROWS):
            at = pl.ds(pl.multiple_of(k * CX + x, SOLVE_ROWS), SOLVE_ROWS)
            store_level(main_c, k, x, LEV, SOLVE_ROWS, sigma[k, x : x + SOLVE_ROWS, :] * adj[at, :])
        return carry

    lax.fori_loop(0, LEV, weigh, 0)
    pack_sides(main_c, low_c, high_c, LEV)
    adj_copies = halo_copies(
        main_c, low_c, high_c, from_high_c, from_low_c, halo_send.at[2], halo_recv.at[2], gx, gy, LEV
    )
    for copy in adj_copies:
        copy.start()

    def send_ret(d, carry):
        ret_copy((me + d) % NDEV).start()
        return carry

    lax.fori_loop(1, NDEV, send_ret, 0)
    own = pltpu.make_async_copy(ret_send.at[me], ret.at[me], self_sem)
    own.start()

    for copy in adj_copies:
        copy.wait()
    unpack_sides(from_high_c, from_low_c, side_c, LEV)
    diffuse(main_c, side_c, main_b, side_b, coef, coef_side)
    solve_last(main_c, control, vert, mask, upper, inverse, reduced, grad)

    own.wait()
    whole = pltpu.make_async_remote_copy(
        src_ref=ret_send.at[pl.ds(0, NDEV - 1)], dst_ref=ret.at[pl.ds(0, NDEV - 1)],
        send_sem=ret_send_sem, recv_sem=ret_recv_sem, device_id=(gx, gy), device_id_type=MESH,
    )
    whole.wait_recv()
    whole.wait_send()


def gradient_call(control, sigma, vert, zonal, merid, mask, rec):
    vmem = pl.BlockSpec(memory_space=pltpu.VMEM)

    def field(rows, lanes, lev=LEV):
        shape = (rows * lev, 128)
        return pltpu.VMEM(shape if lanes == 128 else (2,) + shape, F32)

    def sides(lev):
        return [field(8, 128, lev), field(8, 128, lev), field(GROUPS, 128, lev), field(GROUPS, 128, lev)]

    return pl.pallas_call(
        main_kernel,
        out_shape=(
            jax.ShapeDtypeStruct((LEV, CX, CY), F32),
            jax.ShapeDtypeStruct((NDEV, 8, 128), F32),
            jax.ShapeDtypeStruct((LEV, CX, CY), F32),
        ),
        in_specs=[vmem] * 7,
        out_specs=(vmem,) * 3,
        scratch_shapes=[
            pltpu.VMEM((NDEV, REC, 128), F32),
            pltpu.VMEM((NDEV, 8, 128), F32),
            field(ROWS, 256, 8), field(SROWS, 128, 8), *sides(8),
            field(ROWS, 256), field(SROWS, 128),
            field(ROWS, 256), field(SROWS, 128),
            field(ROWS, 256), field(SROWS, 128),
            *sides(LEV), *sides(LEV),
            pltpu.VMEM((LEV, CX, CY), F32),
            pltpu.VMEM((LEV, CX, CY), F32),
            pltpu.VMEM((LEV, CX, CY), F32),
            pltpu.VMEM((LEV * CX, 3 * CY), BF16),
            pltpu.VMEM((LEV * CX, CY), F32),
            pltpu.SemaphoreType.DMA, pltpu.SemaphoreType.DMA, pltpu.SemaphoreType.DMA, pltpu.SemaphoreType.DMA,
            pltpu.SemaphoreType.DMA,
            pltpu.SemaphoreType.DMA((3, 8)), pltpu.SemaphoreType.DMA((3, 8)),
        ],
        compiler_params=pltpu.CompilerParams(
            collective_id=0, has_side_effects=True, vmem_limit_bytes=VMEM_LIMIT
        ),
        name="gradient",
    )(control, sigma, vert, zonal, merid, mask, rec)


def shards(control, sigma, vert_diff, zonal_diff, merid_diff, ocean_mask, owner, cell, interp_weights, innovation, obs_weight):
    owner_rows = owner.reshape(TILES, 128)
    cell_rows = cell.reshape(TILES, 128)
    rec, rank = pack(owner_rows, cell_rows, interp_weights, innovation, obs_weight)
    increment, ret, gradient = gradient_call(
        control, sigma, vert_diff, zonal_diff, merid_diff, ocean_mask, rec
    )
    departures = unpack(ret, owner_rows, rank, innovation)
    return increment, departures, gradient


def solution(mesh):
    in_specs = (
        P(None, "gx", "gy"),
        P(None, "gx", "gy"),
        P(None, "gx", "gy"),
        P("gx", "gy"),
        P("gx", "gy"),
        P("gx", "gy"),
        P(("gx", "gy"), None),
        P(("gx", "gy")),
        P(None, ("gx", "gy")),
        P(None, ("gx", "gy")),
        P(None, ("gx", "gy")),
    )
    out_specs = (P(None, "gx", "gy"), P(None, ("gx", "gy")), P(None, "gx", "gy"))
    return jax.shard_map(shards, mesh=mesh, in_specs=in_specs, out_specs=out_specs, check_vma=False)
```

```python
import functools

import jax
import jax.numpy as jnp
from jax import lax
from jax.experimental import pallas as pl
from jax.experimental.pallas import tpu as pltpu
from jax.sharding import PartitionSpec as P

MESH = pl.DeviceIdType.MESH
F32 = jnp.float32
BF16 = jnp.bfloat16
VMEM_LIMIT = 60 * 1024 * 1024

LEV = 16
STEPS = 10
CX = 64
CY = 256
NGX = 16
NGY = 8
NDEV = NGX * NGY
PROF = 2048
CAP = 64
TILES = PROF // 128
ROWS = CX + 2 * STEPS
SPAD = 6
SROWS = 96
GROUPS = 12
REC = 18
DIFFUSE_ROWS = 16
PACK_PAIRS = 8
OBSERVE_TILES = 8
UNPACK_TILES = 2


def lane_iota(rows):
    return lax.broadcasted_iota(jnp.int32, (rows, 128), 1)


def blocks(start, count, width, body, carry):
    def many(i, carry):
        for q in range(width):
            carry = body(start + width * i + q, carry)
        return carry

    carry = lax.fori_loop(0, count // width, many, carry)
    for q in range(count - count % width, count):
        carry = body(start + q, carry)
    return carry


def lane_gather(source, lane):
    return jnp.take_along_axis(source, lane, axis=1, mode="promise_in_bounds")


def split_pair(low, high, left):
    first = jnp.where(left, low, pltpu.roll(high, 64, axis=1))
    second = jnp.where(left, pltpu.roll(low, 64, axis=1), high)
    return first, second


def slot_table(owner, cell, weights, rank_out, tab, lanes, tiles, cst):
    rows_o = lax.broadcasted_iota(jnp.int32, (NDEV, 256), 0)
    before = (
        lax.broadcasted_iota(jnp.int32, (256, 256), 0) < lax.broadcasted_iota(jnp.int32, (256, 256), 1)
    ).astype(F32).astype(BF16)
    ones = jnp.ones((256, 256), BF16)
    rows_r = lax.broadcasted_iota(jnp.int32, (CAP, 256), 0)
    cols_p = lax.broadcasted_iota(jnp.int32, (CAP, 256), 1)
    earlier = jnp.zeros((NDEV, 256), F32)
    table = jnp.zeros((NDEV, 128), F32)
    for block in range(PROF // 256):
        owners = jnp.concatenate([owner[2 * block : 2 * block + 1, :], owner[2 * block + 1 : 2 * block + 2, :]], axis=1)
        hot = (rows_o == owners).astype(F32)
        hot16 = hot.astype(BF16)
        count = earlier + jnp.dot(hot16, before, preferred_element_type=F32)
        rank = jnp.sum(hot * count, axis=0, keepdims=True).astype(jnp.int32)
        earlier = earlier + jnp.dot(hot16, ones, preferred_element_type=F32)
        rank_out[2 * block : 2 * block + 1, :] = rank[:, :128]
        rank_out[2 * block + 1 : 2 * block + 2, :] = rank[:, 128:]
        same = rows_r == rank
        lane = jnp.where(same, cols_p % 128, 0).astype(F32).astype(BF16)
        tile = jnp.where(same, 2 * block + 1 + cols_p // 128, 0).astype(F32).astype(BF16)
        table = table + lax.dot_general(
            hot16, jnp.concatenate([lane, tile], axis=0), (((1,), (1,)), ((), ())), preferred_element_type=F32
        )
    tab[...] = table.astype(jnp.int32)
    half = lane_iota(NDEV // 2) < 64
    even, odd = tab[pl.ds(0, NDEV // 2, stride=2), :], tab[pl.ds(1, NDEV // 2, stride=2), :]
    lanes[...] = jnp.where(half, even, pltpu.roll(odd, 64, axis=1))
    tiles[...] = jnp.where(half, pltpu.roll(even, 64, axis=1), odd)

    cst[...] = jnp.zeros_like(cst)
    for tile in range(TILES):
        cols = slice(128 * tile, 128 * tile + 128)
        to = slice(128 * (tile // 2), 128 * (tile // 2) + 128)
        row = 4 * (tile % 2)
        cst[row : row + 1, to] = cell[tile : tile + 1, :].astype(F32)
        cst[row + 1 : row + 2, to] = weights[1:2, cols] + weights[3:4, cols]
        cst[row + 2 : row + 3, to] = weights[2:3, cols] + weights[3:4, cols]


def pack_records(j0, innov, obsw, lanes, tiles, cst, found_ref, rec):
    left = lane_iota(8) < 64
    left_row = lane_iota(1) < 64
    below = lax.broadcasted_iota(jnp.int32, (8, 128), 0) // 4

    for q in range(PACK_PAIRS):
        j = (j0 + q) % (NDEV // 2)
        lane = jnp.broadcast_to(lanes[pl.ds(j, 1), :], (8, 128))
        tile_of = jnp.broadcast_to(tiles[pl.ds(j, 1), :], (8, 128))
        tile_up = tile_of - below
        zero = jnp.zeros((8, 128), F32)
        place, found = zero, [zero] * 4
        for tile in range(TILES):
            cols = slice(128 * tile, 128 * tile + 128)
            here = tile_of == tile + 1
            found = [
                jnp.where(here, lane_gather(source, lane), old)
                for source, old in zip((innov[0:8, cols], innov[8:16, cols], obsw[0:8, cols], obsw[8:16, cols]), found)
            ]
            if tile % 2 == 0:
                both = lane_gather(cst[:, 64 * tile : 64 * tile + 128], lane)
                place = jnp.where(tile_up == tile + 1, both, place)
        found_ref[q] = jnp.concatenate(found + [place], axis=0)

    for q in range(PACK_PAIRS):
        j = (j0 + q) % (NDEV // 2)
        both = found_ref[q]
        place = both[32:36] + both[36:40]
        turned = pltpu.roll(place, 64, axis=1)
        first_i, second_i = split_pair(both[0:8], both[8:16], left)
        first_o, second_o = split_pair(both[16:24], both[24:32], left)
        for side, parts in enumerate((
            [first_i, first_o, jnp.where(left_row, place[0:1], turned[1:2]), place[2:3]],
            [second_i, second_o, jnp.where(left_row, turned[0:1], place[1:2]), turned[2:3]],
        )):
            for row, value in zip((0, 8, 16, 17), parts):
                rec[2 * j + side, row : row + value.shape[0], :] = value


def unpack(ret, owner, rank, innov, dep, low_ref, high_ref):
    left = lane_iota(8) < 64

    def pair(j, carry):
        one, two = ret[2 * j], ret[2 * j + 1]
        low_ref[j] = jnp.where(left, one, pltpu.roll(two, 64, axis=1))
        high_ref[j] = jnp.where(left, pltpu.roll(one, 64, axis=1), two)
        return carry

    blocks(0, NDEV // 2, 16, pair, 0)

    def tile(t, carry):
        owners = jnp.broadcast_to(owner[pl.ds(t, 1), :], (8, 128))
        lane = jnp.broadcast_to(rank[pl.ds(t, 1), :], (8, 128)) + 64 * (owners % 2)
        pair_of = owners // 2
        low = high = jnp.zeros((8, 128), F32)
        for j in range(NDEV // 2):
            here = pair_of == j
            low = jnp.where(here, lane_gather(low_ref[j], lane), low)
            high = jnp.where(here, lane_gather(high_ref[j], lane), high)
        cols = pl.ds(pl.multiple_of(128 * t, 128), 128)
        dep[0:8, cols] = low - innov[0:8, cols]
        dep[8:16, cols] = high - innov[8:16, cols]
        return carry

    blocks(0, TILES, UNPACK_TILES, tile, 0)


def pack_sides(main, low_side, high_side, lev):
    slot = lane_iota(lev) // 16

    def group(g, carry):
        low = jnp.zeros((lev, 128), F32)
        high = jnp.zeros((lev, 128), F32)
        for m in range(8):
            at = pl.ds(pl.multiple_of((STEPS + 8 * g + m) * lev, lev), lev)
            here = slot == m
            first = main[0, at, :]
            last = main[1, at, :]
            low = jnp.where(here, first if m == 0 else pltpu.roll(first, 16 * m, axis=1), low)
            high = jnp.where(here, last if m == 7 else pltpu.roll(last, 16 * m + 16, axis=1), high)
        at = pl.ds(pl.multiple_of(g * lev, lev), lev)
        low_side[at, :] = low
        high_side[at, :] = high
        return carry

    lax.fori_loop(0, CX // 8, group, 0)


def unpack_sides(from_high, from_low, side, lev):
    left = lane_iota(lev) < 64

    def group(g, carry):
        at = pl.ds(pl.multiple_of(g * lev, lev), lev)
        right_strip = from_high[at, :]
        left_strip = from_low[at, :]
        for m in range(8):
            right = right_strip if m == 0 else pltpu.roll(right_strip, 128 - 16 * m, axis=1)
            leftv = left_strip if m == 7 else pltpu.roll(left_strip, 112 - 16 * m, axis=1)
            side[pl.ds(pl.multiple_of((8 * g + m) * lev, lev), lev), :] = jnp.where(left, right, leftv)
        return carry

    lax.fori_loop(0, GROUPS, group, 0)


def halo_copies(main, low_side, high_side, from_high, from_low, send_sem, recv_sem, gx, gy, lev):
    west, east = (gx + NGX - 1) % NGX, (gx + 1) % NGX
    south, north = (gy + NGY - 1) % NGY, (gy + 1) % NGY

    def rows(ref, start, count):
        at = pl.ds(start * lev, count * lev)
        return ref.at[:, at, :] if len(ref.shape) == 3 else ref.at[at, :]

    plan = (
        (rows(main, STEPS, STEPS), rows(main, STEPS + CX, STEPS), (west, gy)),
        (rows(main, CX, STEPS), rows(main, 0, STEPS), (east, gy)),
        (rows(low_side, 0, 8), rows(from_high, 2, 8), (gx, south)),
        (rows(high_side, 0, 8), rows(from_low, 2, 8), (gx, north)),
        (rows(low_side, 0, 2), rows(from_high, 10, 2), (west, south)),
        (rows(low_side, 6, 2), rows(from_high, 0, 2), (east, south)),
        (rows(high_side, 0, 2), rows(from_low, 10, 2), (west, north)),
        (rows(high_side, 6, 2), rows(from_low, 0, 2), (east, north)),
    )
    return [
        pltpu.make_async_remote_copy(
            src_ref=src,
            dst_ref=dst,
            send_sem=send_sem.at[i],
            recv_sem=recv_sem.at[i],
            device_id=device,
            device_id_type=MESH,
        )
        for i, (src, dst, device) in enumerate(plan)
    ]


def next_cols(parts, last):
    rolled = [pltpu.roll(part, 127, axis=1) for part in parts]
    return [jnp.where(last, rolled[(i + 1) % 3], rolled[i]) for i in range(3)]


def prev_cols(parts, first):
    rolled = [pltpu.roll(part, 1, axis=1) for part in parts]
    return [jnp.where(first, rolled[(i + 2) % 3], rolled[i]) for i in range(3)]


def build_faces(coef, coef_side, gy):
    lane = lane_iota(1)
    first_part = jnp.where(gy < NGY - 1, 1.0, 0.0).astype(F32)
    last_part = jnp.where(gy > 0, 1.0, 0.0).astype(F32)
    inside = jnp.where(lane < 64, first_part, last_part)
    last, first = lane == 127, lane == 0

    def row(r, which):
        at = pl.ds(r * 8 + which, 1)
        return [coef[0, at, :], coef[1, at, :], coef_side[pl.ds((r + SPAD) * 8 + which, 1), :]]

    def put(r, which, parts):
        at = pl.ds(r * 8 + which, 1)
        coef[0, at, :] = parts[0]
        coef[1, at, :] = parts[1]
        coef_side[pl.ds((r + SPAD) * 8 + which, 1), :] = parts[2]

    def wet_row(r):
        one, two, side = row(r, 2)
        return [one, two, side * inside]

    def one(r, wet):
        ahead = wet_row(r + 1)
        zonal, merid = row(r, 0), row(r, 1)
        north = next_cols(wet, last)
        south = prev_cols(wet, first)
        merid_south = prev_cols(merid, first)
        put(r, 0, [z * w * a for z, w, a in zip(zonal, wet, ahead)])
        put(r, 1, [m * w * n for m, w, n in zip(merid, wet, north)])
        put(r, 3, [m * w * n for m, w, n in zip(merid_south, south, wet)])
        return tuple(ahead)

    blocks(0, ROWS - 1, 8, one, tuple(wet_row(0)))


def diffuse(first_main, first_side, second_main, second_side, coef, coef_side):
    lane = lane_iota(LEV)
    last, first = lane == 127, lane == 0

    def face(r, which):
        at = pl.ds(r * 8 + which, 1)
        parts = [coef[0, at, :], coef[1, at, :], coef_side[pl.ds((r + SPAD) * 8 + which, 1), :]]
        return [jnp.broadcast_to(part, (LEV, 128)) for part in parts]

    for step in range(STEPS):
        even = step % 2 == 0
        main, side = (first_main, first_side) if even else (second_main, second_side)
        new_main, new_side = (second_main, second_side) if even else (first_main, first_side)
        final = step == STEPS - 1

        def field(r):
            at = pl.ds(pl.multiple_of(r * LEV, LEV), LEV)
            return [main[0, at, :], main[1, at, :], side[pl.ds(pl.multiple_of((r + SPAD) * LEV, LEV), LEV), :]]

        def flux(r, here, ahead):
            return [f * (a - h) for f, a, h in zip(face(r, 0), ahead, here)]

        def one(r, carry):
            here, behind = carry[:3], carry[3:]
            ahead = field(r + 1)
            east = flux(r, here, ahead)
            north = [f * (n - h) for f, n, h in zip(face(r, 1), next_cols(here, last), here)]
            south = [f * (h - p) for f, p, h in zip(face(r, 3), prev_cols(here, first), here)]
            new = [h + ((e - w) + (n - s)) for h, e, w, n, s in zip(here, east, behind, north, south)]
            at = pl.ds(pl.multiple_of(r * LEV, LEV), LEV)
            new_main[0, at, :] = new[0]
            new_main[1, at, :] = new[1]
            if not final:
                new_side[pl.ds(pl.multiple_of((r + SPAD) * LEV, LEV), LEV), :] = new[2]
            return tuple(ahead) + tuple(east)

        start = step + 1
        here = field(start)
        behind = flux(start - 1, field(start - 1), here)
        blocks(start, ROWS - 2 * start, DIFFUSE_ROWS, one, tuple(here) + tuple(behind))


SOLVE_ROWS = 32


def load_level(ref, level, x, lev, count):
    at = pl.ds((STEPS + x) * lev + level, count, stride=lev)
    return jnp.concatenate([ref[0, at, :], ref[1, at, :]], axis=1)


def store_level(ref, level, x, lev, count, value):
    at = pl.ds((STEPS + x) * lev + level, count, stride=lev)
    ref[0, at, :] = value[:, 0:128]
    ref[1, at, :] = value[:, 128:256]


def solve_first(control, vert, mask, upper, inverse, reduced, main):
    for x in range(0, CX, SOLVE_ROWS):
        rows = slice(x, x + SOLVE_ROWS)
        wet = mask[rows, :].astype(F32)
        previous = None
        for k in range(LEV):
            rhs = wet * control[k, rows, :]
            diagonal = 1.0
            if k > 0:
                below = vert[k - 1, rows, :]
                diagonal = diagonal + below
            if k < LEV - 1:
                above = vert[k, rows, :]
                diagonal = diagonal + above
            if k > 0:
                diagonal = diagonal + below * up
                rhs = rhs + below * previous
            inv = 1.0 / diagonal
            inverse[k, rows, :] = inv
            if k < LEV - 1:
                up = -above * inv
                upper[k, rows, :] = up
            previous = rhs * inv
            if k < LEV - 1:
                reduced[k, rows, :] = previous
        value = previous
        store_level(main, LEV - 1, x, LEV, SOLVE_ROWS, value)
        for k in range(LEV - 2, -1, -1):
            value = reduced[k, rows, :] - upper[k, rows, :] * value
            store_level(main, k, x, LEV, SOLVE_ROWS, value)


def solve_last(main, control, vert, mask, upper, inverse, reduced, grad):
    for x in range(0, CX, SOLVE_ROWS):
        rows = slice(x, x + SOLVE_ROWS)
        wet = mask[rows, :].astype(F32)
        previous = None
        for k in range(LEV):
            rhs = load_level(main, k, x, LEV, SOLVE_ROWS)
            if k > 0:
                rhs = rhs + vert[k - 1, rows, :] * previous
            previous = rhs * inverse[k, rows, :]
            if k < LEV - 1:
                reduced[k, rows, :] = previous
        value = previous
        grad[LEV - 1, rows, :] = control[LEV - 1, rows, :] + wet * value
        for k in range(LEV - 2, -1, -1):
            value = reduced[k, rows, :] - upper[k, rows, :] * value
            grad[k, rows, :] = control[k, rows, :] + wet * value


def observe_all(me, recv, field3, adj, ret_send, send):
    left = lane_iota(8) < 64
    left_row = lane_iota(1) < 64
    width = OBSERVE_TILES * 128
    rows_b = lax.broadcasted_iota(jnp.int32, (CY, width), 0).astype(F32)
    rows_a = lax.broadcasted_iota(jnp.int32, (CX, width), 0).astype(F32)

    groups = NDEV // 2 // OBSERVE_TILES

    def observe(n, carry):
        i = (n + me // (2 * OBSERVE_TILES)) % groups
        parts = []
        for h in range(OBSERVE_TILES):
            one, two = recv[2 * (OBSERVE_TILES * i + h)], recv[2 * (OBSERVE_TILES * i + h) + 1]
            turned_one, turned_two = pltpu.roll(one, 64, axis=1), pltpu.roll(two, 64, axis=1)
            parts.append((
                jnp.where(left_row, one[16:17], turned_two[16:17]),
                jnp.where(left_row, turned_one[16:17], two[16:17]),
                jnp.where(left_row, one[17:18], turned_two[17:18]),
                jnp.where(left, one[0:8], turned_two[0:8]),
                jnp.where(left, turned_one[0:8], two[0:8]),
                jnp.where(left, one[8:16], turned_two[8:16]),
                jnp.where(left, turned_one[8:16], two[8:16]),
            ))
        cell, along_x, along_y, low_i, high_i, low_o, high_o = [jnp.concatenate(part, axis=1) for part in zip(*parts)]
        innov = jnp.concatenate([low_i, high_i], axis=0)
        obsw = jnp.concatenate([low_o, high_o], axis=0)
        cell_a = jnp.floor(cell * (1.0 / CY))
        cell_b = cell - CY * cell_a
        from_a = rows_a - cell_a
        from_b = rows_b - cell_b
        in_x = jnp.where(from_a == 0.0, 1.0 - along_x, jnp.where(from_a == 1.0, along_x, 0.0))
        in_y = jnp.where(from_b == 0.0, 1.0 - along_y, jnp.where(from_b == 1.0, along_y, 0.0))
        y_high = in_y.astype(BF16)
        y_low = (in_y - y_high.astype(F32)).astype(BF16)
        y_rows = jnp.concatenate([y_high, y_low, y_high], axis=0)
        vals = []
        for k in range(0, LEV, 4):
            rows = jnp.dot(field3[CX * k : CX * (k + 4), :], y_rows, preferred_element_type=F32)
            vals.append(jnp.sum(rows.reshape(4, CX, width) * in_x[None], axis=1))
        vals = jnp.concatenate(vals, axis=0)
        forcing = obsw * (vals - innov)
        for h in range(OBSERVE_TILES):
            cols = slice(128 * h, 128 * h + 128)
            first, second = split_pair(vals[0:8, cols], vals[8:16, cols], left)
            ret_send[2 * (OBSERVE_TILES * i + h)] = first
            ret_send[2 * (OBSERVE_TILES * i + h) + 1] = second
        lax.fori_loop(2 * OBSERVE_TILES * i, 2 * OBSERVE_TILES * (i + 1), send, 0)
        spread = (in_x[None] * forcing[:, None, :]).reshape(LEV * CX, width)
        high = spread.astype(BF16)
        low = (spread - high.astype(F32)).astype(BF16)
        adj[...] += lax.dot_general(
            jnp.concatenate([high, high, low], axis=1),
            jnp.concatenate([y_high, y_low, y_high], axis=1),
            (((1,), (1,)), ((), ())),
            preferred_element_type=F32,
        )
        return carry

    lax.fori_loop(0, groups, observe, 0)


def main_kernel(
    control, sigma, vert, zonal, merid, mask, owner, cell, weights, innov, obsw, inc, dep, grad,
    rec, recv, ret_send, ret, rank, tab, lanes, tiles, cst, found_ref, ret_low, ret_high,
    coef, coef_side, coef_low, coef_high, coef_from_high, coef_from_low,
    main_a, side_a, main_b, side_b, main_c, side_c,
    low_a, high_a, from_high_a, from_low_a, low_c, high_c, from_high_c, from_low_c,
    upper, inverse, reduced, field3, adj,
    rec_send_sem, rec_recv_sem, ret_send_sem, ret_recv_sem, self_sem, halo_send, halo_recv,
):
    gx, gy = lax.axis_index("gx"), lax.axis_index("gy")
    me = gx * NGY + gy

    barrier = pltpu.get_barrier_semaphore()

    def greet(d, carry):
        to = (me + d) % NDEV
        pl.semaphore_signal(barrier, inc=1, device_id=(to // NGY, to % NGY), device_id_type=MESH)
        return carry

    lax.fori_loop(1, NDEV, greet, 0)

    def to_device(src, dst, send_sem, recv_sem, to):
        return pltpu.make_async_remote_copy(
            src_ref=src, dst_ref=dst, send_sem=send_sem, recv_sem=recv_sem,
            device_id=(to // NGY, to % NGY), device_id_type=MESH,
        )

    def send_rec(to, carry):
        @pl.when(to != me)
        def _():
            to_device(rec.at[to], recv.at[me], rec_send_sem, rec_recv_sem, to).start()

        return carry

    def send_ret(to, carry):
        @pl.when(to != me)
        def _():
            to_device(ret_send.at[to], ret.at[me], ret_send_sem, ret_recv_sem, to).start()

        return carry

    def wait_all(src, dst, send_sem, recv_sem):
        most = pl.ds(0, NDEV - 1)
        whole = to_device(src.at[most], dst.at[most], send_sem, recv_sem, me)
        whole.wait_recv()
        whole.wait_send()

    for half in range(2):
        coef[half, STEPS * 8 : (STEPS + CX) * 8, :] = jnp.zeros((CX * 8, 128), F32)
    for x in range(0, CX, SOLVE_ROWS):
        rows = slice(x, x + SOLVE_ROWS)
        store_level(coef, 0, x, 8, SOLVE_ROWS, zonal[rows, :])
        store_level(coef, 1, x, 8, SOLVE_ROWS, merid[rows, :])
        store_level(coef, 2, x, 8, SOLVE_ROWS, mask[rows, :].astype(F32))
    pack_sides(coef, coef_low, coef_high, 8)
    solve_first(control, vert, mask, upper, inverse, reduced, main_a)
    pack_sides(main_a, low_a, high_a, LEV)

    pl.semaphore_wait(barrier, NDEV - 1)
    coef_copies = halo_copies(
        coef, coef_low, coef_high, coef_from_high, coef_from_low, halo_send.at[0], halo_recv.at[0], gx, gy, 8
    )
    field_copies = halo_copies(
        main_a, low_a, high_a, from_high_a, from_low_a, halo_send.at[1], halo_recv.at[1], gx, gy, LEV
    )
    for copy in coef_copies + field_copies:
        copy.start()

    slot_table(owner, cell, weights, rank, tab, lanes, tiles, cst)

    def pack_some(n, carry):
        j0 = (me // 2 + n * PACK_PAIRS) % (NDEV // 2)
        pack_records(j0, innov, obsw, lanes, tiles, cst, found_ref, rec)

        def send_one(q, carry):
            return send_rec((2 * j0 + q) % NDEV, carry)

        return lax.fori_loop(0, 2 * PACK_PAIRS, send_one, carry)

    lax.fori_loop(0, NDEV // 2 // PACK_PAIRS, pack_some, 0)
    own = pltpu.make_async_copy(rec.at[me], recv.at[me], self_sem)
    own.start()

    for copy in coef_copies:
        copy.wait()
    unpack_sides(coef_from_high, coef_from_low, coef_side, 8)
    build_faces(coef, coef_side, gy)
    for copy in field_copies:
        copy.wait()
    unpack_sides(from_high_a, from_low_a, side_a, LEV)
    diffuse(main_a, side_a, main_b, side_b, coef, coef_side)

    def scale(k, carry):
        for x in range(0, CX, 16):
            value = sigma[k, x : x + 16, :] * load_level(main_a, k, x, LEV, 16)
            inc[k, x : x + 16, :] = value
            high = value.astype(BF16)
            low = (value - high.astype(F32)).astype(BF16)
            at = pl.ds(pl.multiple_of(k * CX + x, 16), 16)
            field3[at, 0:256] = high
            field3[at, 256:512] = high
            field3[at, 512:768] = low
        return carry

    lax.fori_loop(0, LEV, scale, 0)
    adj[...] = jnp.zeros_like(adj)

    own.wait()
    wait_all(rec, recv, rec_send_sem, rec_recv_sem)
    observe_all(me, recv, field3, adj, ret_send, send_ret)
    own = pltpu.make_async_copy(ret_send.at[me], ret.at[me], self_sem)
    own.start()

    def weigh(k, carry):
        for x in range(0, CX, SOLVE_ROWS):
            at = pl.ds(pl.multiple_of(k * CX + x, SOLVE_ROWS), SOLVE_ROWS)
            store_level(main_c, k, x, LEV, SOLVE_ROWS, sigma[k, x : x + SOLVE_ROWS, :] * adj[at, :])
        return carry

    lax.fori_loop(0, LEV, weigh, 0)
    pack_sides(main_c, low_c, high_c, LEV)
    adj_copies = halo_copies(
        main_c, low_c, high_c, from_high_c, from_low_c, halo_send.at[2], halo_recv.at[2], gx, gy, LEV
    )
    for copy in adj_copies:
        copy.start()

    own.wait()
    wait_all(ret_send, ret, ret_send_sem, ret_recv_sem)
    unpack(ret, owner, rank, innov, dep, ret_low, ret_high)

    for copy in adj_copies:
        copy.wait()
    unpack_sides(from_high_c, from_low_c, side_c, LEV)
    diffuse(main_c, side_c, main_b, side_b, coef, coef_side)
    solve_last(main_c, control, vert, mask, upper, inverse, reduced, grad)


def gradient_call(*args):
    vmem = pl.BlockSpec(memory_space=pltpu.VMEM)

    def field(rows, lanes, lev=LEV):
        shape = (rows * lev, 128)
        return pltpu.VMEM(shape if lanes == 128 else (2,) + shape, F32)

    def sides(lev):
        return [field(8, 128, lev), field(8, 128, lev), field(GROUPS, 128, lev), field(GROUPS, 128, lev)]

    return pl.pallas_call(
        main_kernel,
        out_shape=(
            jax.ShapeDtypeStruct((LEV, CX, CY), F32),
            jax.ShapeDtypeStruct((LEV, PROF), F32),
            jax.ShapeDtypeStruct((LEV, CX, CY), F32),
        ),
        in_specs=[vmem] * 11,
        out_specs=(vmem,) * 3,
        scratch_shapes=[
            pltpu.VMEM((NDEV, REC, 128), F32),
            pltpu.VMEM((NDEV, REC, 128), F32),
            pltpu.VMEM((NDEV, 8, 128), F32),
            pltpu.VMEM((NDEV, 8, 128), F32),
            pltpu.VMEM((TILES, 128), jnp.int32),
            pltpu.VMEM((NDEV, 128), jnp.int32),
            pltpu.VMEM((NDEV // 2, 128), jnp.int32),
            pltpu.VMEM((NDEV // 2, 128), jnp.int32),
            pltpu.VMEM((8, PROF // 2), F32),
            pltpu.VMEM((PACK_PAIRS, 40, 128), F32),
            pltpu.VMEM((NDEV // 2, 8, 128), F32),
            pltpu.VMEM((NDEV // 2, 8, 128), F32),
            field(ROWS, 256, 8), field(SROWS, 128, 8), *sides(8),
            field(ROWS, 256), field(SROWS, 128),
            field(ROWS, 256), field(SROWS, 128),
            field(ROWS, 256), field(SROWS, 128),
            *sides(LEV), *sides(LEV),
            pltpu.VMEM((LEV, CX, CY), F32),
            pltpu.VMEM((LEV, CX, CY), F32),
            pltpu.VMEM((LEV, CX, CY), F32),
            pltpu.VMEM((LEV * CX, 3 * CY), BF16),
            pltpu.VMEM((LEV * CX, CY), F32),
            pltpu.SemaphoreType.DMA, pltpu.SemaphoreType.DMA, pltpu.SemaphoreType.DMA, pltpu.SemaphoreType.DMA,
            pltpu.SemaphoreType.DMA,
            pltpu.SemaphoreType.DMA((3, 8)), pltpu.SemaphoreType.DMA((3, 8)),
        ],
        compiler_params=pltpu.CompilerParams(
            collective_id=0, has_side_effects=True, vmem_limit_bytes=VMEM_LIMIT
        ),
        name="gradient",
    )(*args)


def shards(control, sigma, vert_diff, zonal_diff, merid_diff, ocean_mask, owner, cell, interp_weights, innovation, obs_weight):
    return gradient_call(
        control, sigma, vert_diff, zonal_diff, merid_diff, ocean_mask,
        owner.reshape(TILES, 128), cell.reshape(TILES, 128), interp_weights, innovation, obs_weight,
    )


def solution(mesh):
    in_specs = (
        P(None, "gx", "gy"),
        P(None, "gx", "gy"),
        P(None, "gx", "gy"),
        P("gx", "gy"),
        P("gx", "gy"),
        P("gx", "gy"),
        P(("gx", "gy"), None),
        P(("gx", "gy")),
        P(None, ("gx", "gy")),
        P(None, ("gx", "gy")),
        P(None, ("gx", "gy")),
    )
    out_specs = (P(None, "gx", "gy"), P(None, ("gx", "gy")), P(None, "gx", "gy"))
    return jax.shard_map(shards, mesh=mesh, in_specs=in_specs, out_specs=out_specs, check_vma=False)
```

```python
import functools

import jax
import jax.numpy as jnp
from jax import lax
from jax.experimental import pallas as pl
from jax.experimental.pallas import tpu as pltpu
from jax.sharding import PartitionSpec as P

MESH = pl.DeviceIdType.MESH
F32 = jnp.float32
BF16 = jnp.bfloat16
VMEM_LIMIT = 60 * 1024 * 1024

LEV = 16
STEPS = 10
CX = 64
CY = 256
NGX = 16
NGY = 8
NDEV = NGX * NGY
PROF = 2048
CAP = 64
TILES = PROF // 128
ROWS = CX + 2 * STEPS
SPAD = 6
SROWS = 96
GROUPS = 12
REC = 18
DIFFUSE_TILES = 4
SEG = 11
ALL_ROWS = 8 * SEG
EDGE = 24
COLS = CY + 2 * EDGE
PAIR_STRIDE = 21
PACK_PAIRS = 8
OBSERVE_TILES = 8
UNPACK_TILES = 2


def lane_iota(rows):
    return lax.broadcasted_iota(jnp.int32, (rows, 128), 1)


def blocks(start, count, width, body, carry):
    def many(i, carry):
        for q in range(width):
            carry = body(start + width * i + q, carry)
        return carry

    carry = lax.fori_loop(0, count // width, many, carry)
    for q in range(count - count % width, count):
        carry = body(start + q, carry)
    return carry


def lane_gather(source, lane):
    return jnp.take_along_axis(source, lane, axis=1, mode="promise_in_bounds")


def split_pair(low, high, left):
    first = jnp.where(left, low, pltpu.roll(high, 64, axis=1))
    second = jnp.where(left, pltpu.roll(low, 64, axis=1), high)
    return first, second


def slot_table(owner, cell, weights, rank_out, tab, lanes, tiles, cst):
    rows_o = lax.broadcasted_iota(jnp.int32, (NDEV, 256), 0)
    before = (
        lax.broadcasted_iota(jnp.int32, (256, 256), 0) < lax.broadcasted_iota(jnp.int32, (256, 256), 1)
    ).astype(F32).astype(BF16)
    ones = jnp.ones((256, 256), BF16)
    rows_r = lax.broadcasted_iota(jnp.int32, (CAP, 256), 0)
    cols_p = lax.broadcasted_iota(jnp.int32, (CAP, 256), 1)
    earlier = jnp.zeros((NDEV, 256), F32)
    table = jnp.zeros((NDEV, 128), F32)
    for block in range(PROF // 256):
        owners = jnp.concatenate([owner[2 * block : 2 * block + 1, :], owner[2 * block + 1 : 2 * block + 2, :]], axis=1)
        hot = (rows_o == owners).astype(F32)
        hot16 = hot.astype(BF16)
        count = earlier + jnp.dot(hot16, before, preferred_element_type=F32)
        rank = jnp.sum(hot * count, axis=0, keepdims=True).astype(jnp.int32)
        earlier = earlier + jnp.dot(hot16, ones, preferred_element_type=F32)
        rank_out[2 * block : 2 * block + 1, :] = rank[:, :128]
        rank_out[2 * block + 1 : 2 * block + 2, :] = rank[:, 128:]
        same = rows_r == rank
        lane = jnp.where(same, cols_p % 128, 0).astype(F32).astype(BF16)
        tile = jnp.where(same, 2 * block + 1 + cols_p // 128, 0).astype(F32).astype(BF16)
        table = table + lax.dot_general(
            hot16, jnp.concatenate([lane, tile], axis=0), (((1,), (1,)), ((), ())), preferred_element_type=F32
        )
    tab[...] = table.astype(jnp.int32)
    half = lane_iota(NDEV // 2) < 64
    even, odd = tab[pl.ds(0, NDEV // 2, stride=2), :], tab[pl.ds(1, NDEV // 2, stride=2), :]
    lanes[...] = jnp.where(half, even, pltpu.roll(odd, 64, axis=1))
    tiles[...] = jnp.where(half, pltpu.roll(even, 64, axis=1), odd)

    cst[...] = jnp.zeros_like(cst)
    for tile in range(TILES):
        cols = slice(128 * tile, 128 * tile + 128)
        to = slice(128 * (tile // 2), 128 * (tile // 2) + 128)
        row = 4 * (tile % 2)
        cst[row : row + 1, to] = cell[tile : tile + 1, :].astype(F32)
        cst[row + 1 : row + 2, to] = weights[1:2, cols] + weights[3:4, cols]
        cst[row + 2 : row + 3, to] = weights[2:3, cols] + weights[3:4, cols]


def pack_records(j0, innov, obsw, lanes, tiles, cst, found_ref, rec):
    left = lane_iota(8) < 64
    left_row = lane_iota(1) < 64
    below = lax.broadcasted_iota(jnp.int32, (8, 128), 0) // 4

    for q in range(PACK_PAIRS):
        j = lax.rem(j0 + q * PAIR_STRIDE, NDEV // 2)
        lane = jnp.broadcast_to(lanes[pl.ds(j, 1), :], (8, 128))
        tile_of = jnp.broadcast_to(tiles[pl.ds(j, 1), :], (8, 128))
        tile_up = tile_of - below
        zero = jnp.zeros((8, 128), F32)
        place, found = zero, [zero] * 4
        for tile in range(TILES):
            cols = slice(128 * tile, 128 * tile + 128)
            here = tile_of == tile + 1
            found = [
                jnp.where(here, lane_gather(source, lane), old)
                for source, old in zip((innov[0:8, cols], innov[8:16, cols], obsw[0:8, cols], obsw[8:16, cols]), found)
            ]
            if tile % 2 == 0:
                both = lane_gather(cst[:, 64 * tile : 64 * tile + 128], lane)
                place = jnp.where(tile_up == tile + 1, both, place)
        found_ref[q] = jnp.concatenate(found + [place], axis=0)

    for q in range(PACK_PAIRS):
        j = lax.rem(j0 + q * PAIR_STRIDE, NDEV // 2)
        both = found_ref[q]
        place = both[32:36] + both[36:40]
        turned = pltpu.roll(place, 64, axis=1)
        first_i, second_i = split_pair(both[0:8], both[8:16], left)
        first_o, second_o = split_pair(both[16:24], both[24:32], left)
        for side, parts in enumerate((
            [first_i, first_o, jnp.where(left_row, place[0:1], turned[1:2]), place[2:3]],
            [second_i, second_o, jnp.where(left_row, turned[0:1], place[1:2]), turned[2:3]],
        )):
            for row, value in zip((0, 8, 16, 17), parts):
                rec[2 * j + side, row : row + value.shape[0], :] = value


def unpack(ret, owner, rank, innov, dep, low_ref, high_ref):
    left = lane_iota(8) < 64

    def pair(j, carry):
        one, two = ret[2 * j], ret[2 * j + 1]
        low_ref[j] = jnp.where(left, one, pltpu.roll(two, 64, axis=1))
        high_ref[j] = jnp.where(left, pltpu.roll(one, 64, axis=1), two)
        return carry

    blocks(0, NDEV // 2, 16, pair, 0)

    def tile(t, carry):
        owners = jnp.broadcast_to(owner[pl.ds(t, 1), :], (8, 128))
        lane = jnp.broadcast_to(rank[pl.ds(t, 1), :], (8, 128)) + 64 * (owners % 2)
        pair_of = owners // 2
        low = high = jnp.zeros((8, 128), F32)
        for j in range(NDEV // 2):
            here = pair_of == j
            low = jnp.where(here, lane_gather(low_ref[j], lane), low)
            high = jnp.where(here, lane_gather(high_ref[j], lane), high)
        cols = pl.ds(pl.multiple_of(128 * t, 128), 128)
        dep[0:8, cols] = low - innov[0:8, cols]
        dep[8:16, cols] = high - innov[8:16, cols]
        return carry

    blocks(0, TILES, UNPACK_TILES, tile, 0)


def pack_sides(main, low_side, high_side, lev):
    slot = lane_iota(lev) // 16

    def group(g, carry):
        low = jnp.zeros((lev, 128), F32)
        high = jnp.zeros((lev, 128), F32)
        for m in range(8):
            at = pl.ds(pl.multiple_of((STEPS + 8 * g + m) * lev, lev), lev)
            here = slot == m
            first = main[0, at, :]
            last = main[1, at, :]
            low = jnp.where(here, first if m == 0 else pltpu.roll(first, 16 * m, axis=1), low)
            high = jnp.where(here, last if m == 7 else pltpu.roll(last, 16 * m + 16, axis=1), high)
        at = pl.ds(pl.multiple_of(g * lev, lev), lev)
        low_side[at, :] = low
        high_side[at, :] = high
        return carry

    lax.fori_loop(0, CX // 8, group, 0)


def unpack_sides(from_high, from_low, side, lev):
    left = lane_iota(lev) < 64

    def group(g, carry):
        at = pl.ds(pl.multiple_of(g * lev, lev), lev)
        right_strip = from_high[at, :]
        left_strip = from_low[at, :]
        for m in range(8):
            right = right_strip if m == 0 else pltpu.roll(right_strip, 128 - 16 * m, axis=1)
            leftv = left_strip if m == 7 else pltpu.roll(left_strip, 112 - 16 * m, axis=1)
            side[pl.ds(pl.multiple_of((8 * g + m) * lev, lev), lev), :] = jnp.where(left, right, leftv)
        return carry

    lax.fori_loop(0, GROUPS, group, 0)


def halo_copies(main, low_side, high_side, from_high, from_low, send_sem, recv_sem, gx, gy, lev):
    west, east = (gx + NGX - 1) % NGX, (gx + 1) % NGX
    south, north = (gy + NGY - 1) % NGY, (gy + 1) % NGY

    def rows(ref, start, count):
        at = pl.ds(start * lev, count * lev)
        return ref.at[:, at, :] if len(ref.shape) == 3 else ref.at[at, :]

    plan = (
        (rows(main, STEPS, STEPS), rows(main, STEPS + CX, STEPS), (west, gy)),
        (rows(main, CX, STEPS), rows(main, 0, STEPS), (east, gy)),
        (rows(low_side, 0, 8), rows(from_high, 2, 8), (gx, south)),
        (rows(high_side, 0, 8), rows(from_low, 2, 8), (gx, north)),
        (rows(low_side, 0, 2), rows(from_high, 10, 2), (west, south)),
        (rows(low_side, 6, 2), rows(from_high, 0, 2), (east, south)),
        (rows(high_side, 0, 2), rows(from_low, 10, 2), (west, north)),
        (rows(high_side, 6, 2), rows(from_low, 0, 2), (east, north)),
    )
    return [
        pltpu.make_async_remote_copy(
            src_ref=src,
            dst_ref=dst,
            send_sem=send_sem.at[i],
            recv_sem=recv_sem.at[i],
            device_id=device,
            device_id_type=MESH,
        )
        for i, (src, dst, device) in enumerate(plan)
    ]


def next_cols(parts, last):
    rolled = [pltpu.roll(part, 127, axis=1) for part in parts]
    return [jnp.where(last, rolled[(i + 1) % 3], rolled[i]) for i in range(3)]


def build_faces(coef, coef_side, gy):
    lane = lane_iota(1)
    first_part = jnp.where(gy < NGY - 1, 1.0, 0.0).astype(F32)
    last_part = jnp.where(gy > 0, 1.0, 0.0).astype(F32)
    inside = jnp.where(lane < 64, first_part, last_part)
    last = lane == 127

    def row(r, which):
        at = pl.ds(r * 8 + which, 1)
        return [coef[0, at, :], coef[1, at, :], coef_side[pl.ds((r + SPAD) * 8 + which, 1), :]]

    def put(r, which, parts):
        at = pl.ds(r * 8 + which, 1)
        coef[0, at, :] = parts[0]
        coef[1, at, :] = parts[1]
        coef_side[pl.ds((r + SPAD) * 8 + which, 1), :] = parts[2]

    def wet_row(r):
        one, two, side = row(r, 2)
        return [one, two, side * inside]

    def one(r, wet):
        ahead = wet_row(r + 1)
        zonal, merid = row(r, 0), row(r, 1)
        north = next_cols(wet, last)
        put(r, 0, [z * w * a for z, w, a in zip(zonal, wet, ahead)])
        put(r, 1, [m * w * n for m, w, n in zip(merid, wet, north)])
        return tuple(ahead)

    blocks(0, ROWS - 1, 8, one, tuple(wet_row(0)))


def put_columns(plane, parts):
    first, second, side = [part.T for part in parts]
    plane[EDGE : EDGE + 128, :] = first
    plane[EDGE + 128 : EDGE + 256, :] = second
    plane[EDGE + CY : EDGE + CY + 16, :] = side[0:16]
    plane[EDGE - 16 : EDGE, :] = side[112:128]


def expand_faces(coef, coef_side, face_x, face_y):
    def one(place, carry):
        for which, planes, to in ((0, face_x, place + 1), (1, face_y, place)):
            parts = []
            for ref, pad in ((coef.at[0], 0), (coef.at[1], 0), (coef_side, SPAD)):
                rows = [ref[pl.ds((SEG * seg + place + pad) * 8 + which, 1), :] for seg in range(8)]
                parts.append(jnp.concatenate([jnp.broadcast_to(row, (LEV, 128)) for row in rows], axis=0))
            put_columns(planes.at[to], parts)
        return carry

    blocks(0, SEG, 2, one, 0)
    face_x[0] = pltpu.roll(face_x[SEG], LEV, axis=1)


def turn_edges(field):
    field[0] = pltpu.roll(field[SEG], LEV, axis=1)
    field[SEG + 1] = pltpu.roll(field[1], 128 - LEV, axis=1)


def diffuse(main, side, field_a, field_b, face_x, face_y):
    def enter(place, carry):
        parts = []
        for ref, pad in ((main.at[0], 0), (main.at[1], 0), (side, SPAD)):
            rows = [pl.ds(pl.multiple_of((SEG * seg + place + pad) * LEV, LEV), LEV) for seg in range(8)]
            parts.append(jnp.concatenate([ref[at, :] for at in rows], axis=0))
        put_columns(field_a.at[place + 1], parts)
        return carry

    blocks(0, SEG, 4, enter, 0)
    bottom = lax.broadcasted_iota(jnp.int32, (8, 128), 0) == 7
    turn_edges(field_a)

    for step in range(STEPS):
        now, new = (field_a, field_b) if step % 2 == 0 else (field_b, field_a)

        def north_flux(t, p, here):
            row = pl.multiple_of(8 * t, 8)
            return face_y[p - 1, pl.ds(row, 8), :] * (now[p, pl.ds(row + 1, 8), :] - here)

        def tile(t, carry):
            at = pl.ds(pl.multiple_of(8 * t, 8), 8)
            here, west = now[1, at, :], face_x[0, at, :] * (now[1, at, :] - now[0, at, :])
            norths = []
            for p in range(1, SEG + 1):
                ahead = now[p + 1, at, :]
                east = face_x[p, at, :] * (ahead - here)
                north = north_flux(t, p, here)
                south = pltpu.roll(jnp.where(bottom, carry[p - 1], north), 1, axis=0)
                new[p, at, :] = here + ((east - west) + (north - south))
                here, west = ahead, east
                norths.append(north)
            return tuple(norths)

        first = (EDGE - (STEPS - 1 - step)) // 8
        last = (EDGE + CY + (STEPS - 1 - step) + 7) // 8
        before = [north_flux(first - 1, p, now[p, 8 * first - 8 : 8 * first, :]) for p in range(1, SEG + 1)]
        blocks(first, last - first, DIFFUSE_TILES, tile, tuple(before))
        if step < STEPS - 1:
            turn_edges(new)

    def leave(place, carry):
        for half in range(2):
            rows = field_a[place + 1, EDGE + 128 * half : EDGE + 128 * half + 128, :].T
            for seg in range(8):
                at = pl.ds(pl.multiple_of((SEG * seg + place) * LEV, LEV), LEV)
                main[half, at, :] = rows[LEV * seg : LEV * seg + LEV]
        return carry

    blocks(0, SEG, 4, leave, 0)


SOLVE_ROWS = 32


def load_level(ref, level, x, lev, count):
    at = pl.ds((STEPS + x) * lev + level, count, stride=lev)
    return jnp.concatenate([ref[0, at, :], ref[1, at, :]], axis=1)


def store_level(ref, level, x, lev, count, value):
    at = pl.ds((STEPS + x) * lev + level, count, stride=lev)
    ref[0, at, :] = value[:, 0:128]
    ref[1, at, :] = value[:, 128:256]


def solve_first(control, vert, mask, upper, inverse, reduced, main):
    for x in range(0, CX, SOLVE_ROWS):
        rows = slice(x, x + SOLVE_ROWS)
        wet = mask[rows, :].astype(F32)
        previous = None
        for k in range(LEV):
            rhs = wet * control[k, rows, :]
            diagonal = 1.0
            if k > 0:
                below = vert[k - 1, rows, :]
                diagonal = diagonal + below
            if k < LEV - 1:
                above = vert[k, rows, :]
                diagonal = diagonal + above
            if k > 0:
                diagonal = diagonal + below * up
                rhs = rhs + below * previous
            inv = 1.0 / diagonal
            inverse[k, rows, :] = inv
            if k < LEV - 1:
                up = -above * inv
                upper[k, rows, :] = up
            previous = rhs * inv
            if k < LEV - 1:
                reduced[k, rows, :] = previous
        value = previous
        store_level(main, LEV - 1, x, LEV, SOLVE_ROWS, value)
        for k in range(LEV - 2, -1, -1):
            value = reduced[k, rows, :] - upper[k, rows, :] * value
            store_level(main, k, x, LEV, SOLVE_ROWS, value)


def solve_last(main, control, vert, mask, upper, inverse, reduced, grad):
    for x in range(0, CX, SOLVE_ROWS):
        rows = slice(x, x + SOLVE_ROWS)
        wet = mask[rows, :].astype(F32)
        previous = None
        for k in range(LEV):
            rhs = load_level(main, k, x, LEV, SOLVE_ROWS)
            if k > 0:
                rhs = rhs + vert[k - 1, rows, :] * previous
            previous = rhs * inverse[k, rows, :]
            if k < LEV - 1:
                reduced[k, rows, :] = previous
        value = previous
        grad[LEV - 1, rows, :] = control[LEV - 1, rows, :] + wet * value
        for k in range(LEV - 2, -1, -1):
            value = reduced[k, rows, :] - upper[k, rows, :] * value
            grad[k, rows, :] = control[k, rows, :] + wet * value


def send_first(n, j, partner, send):
    @pl.when(n > 0)
    def _():
        send(2 * j)
        send(2 * j + 1)

    @pl.when(n == 0)
    def _():
        send(partner)


def observe_all(mine, partner, recv, field3, adj, ret_send, send):
    left = lane_iota(8) < 64
    left_row = lane_iota(1) < 64
    width = OBSERVE_TILES * 128
    rows_b = lax.broadcasted_iota(jnp.int32, (CY, width), 0).astype(F32)
    rows_a = lax.broadcasted_iota(jnp.int32, (CX, width), 0).astype(F32)

    groups = NDEV // 2 // OBSERVE_TILES

    def observe(n, carry):
        pairs = [lax.rem(mine + n + groups * h, NDEV // 2) for h in range(OBSERVE_TILES)]
        parts = []
        for h in range(OBSERVE_TILES):
            one, two = recv[2 * pairs[h]], recv[2 * pairs[h] + 1]
            turned_one, turned_two = pltpu.roll(one, 64, axis=1), pltpu.roll(two, 64, axis=1)
            parts.append((
                jnp.where(left_row, one[16:17], turned_two[16:17]),
                jnp.where(left_row, turned_one[16:17], two[16:17]),
                jnp.where(left_row, one[17:18], turned_two[17:18]),
                jnp.where(left, one[0:8], turned_two[0:8]),
                jnp.where(left, turned_one[0:8], two[0:8]),
                jnp.where(left, one[8:16], turned_two[8:16]),
                jnp.where(left, turned_one[8:16], two[8:16]),
            ))
        cell, along_x, along_y, low_i, high_i, low_o, high_o = [jnp.concatenate(part, axis=1) for part in zip(*parts)]
        innov = jnp.concatenate([low_i, high_i], axis=0)
        obsw = jnp.concatenate([low_o, high_o], axis=0)
        cell_a = jnp.floor(cell * (1.0 / CY))
        cell_b = cell - CY * cell_a
        from_a = rows_a - cell_a
        from_b = rows_b - cell_b
        in_x = jnp.where(from_a == 0.0, 1.0 - along_x, jnp.where(from_a == 1.0, along_x, 0.0))
        in_y = jnp.where(from_b == 0.0, 1.0 - along_y, jnp.where(from_b == 1.0, along_y, 0.0))
        y_high = in_y.astype(BF16)
        y_low = (in_y - y_high.astype(F32)).astype(BF16)
        y_rows = jnp.concatenate([y_high, y_low, y_high], axis=0)
        vals = []
        for k in range(0, LEV, 4):
            rows = jnp.dot(field3[CX * k : CX * (k + 4), :], y_rows, preferred_element_type=F32)
            vals.append(jnp.sum(rows.reshape(4, CX, width) * in_x[None], axis=1))
        vals = jnp.concatenate(vals, axis=0)
        forcing = obsw * (vals - innov)
        for h in range(OBSERVE_TILES):
            cols = slice(128 * h, 128 * h + 128)
            first, second = split_pair(vals[0:8, cols], vals[8:16, cols], left)
            ret_send[2 * pairs[h]] = first
            ret_send[2 * pairs[h] + 1] = second
        for h in range(1, OBSERVE_TILES):
            send(2 * pairs[h])
            send(2 * pairs[h] + 1)
        spread = (in_x[None] * forcing[:, None, :]).reshape(LEV * CX, width)
        high = spread.astype(BF16)
        low = (spread - high.astype(F32)).astype(BF16)
        adj[...] += lax.dot_general(
            jnp.concatenate([high, high, low], axis=1),
            jnp.concatenate([y_high, y_low, y_high], axis=1),
            (((1,), (1,)), ((), ())),
            preferred_element_type=F32,
        )
        send_first(n, pairs[0], partner, send)
        return carry

    lax.fori_loop(0, groups, observe, 0)


def main_kernel(
    control_in, sigma_in, vert_in, zonal_in, merid_in, mask_in, owner_in, cell_in, weights_in, innov_in, obsw_in,
    inc_out, dep_out, grad_out,
    control, sigma, vert, zonal, merid, mask, owner, cell, weights, innov, obsw, inc, dep, grad, io_sem,
    rec, recv, ret_send, ret, rank, tab, lanes, tiles, cst, found_ref, ret_low, ret_high,
    coef, coef_side, coef_low, coef_high, coef_from_high, coef_from_low,
    main_a, side_a, main_c, side_c, field_a, field_b, face_x, face_y,
    low_a, high_a, from_high_a, from_low_a, low_c, high_c, from_high_c, from_low_c,
    upper, inverse, reduced, field3, adj,
    rec_send_sem, rec_recv_sem, ret_send_sem, ret_recv_sem, self_sem, halo_send, halo_recv,
):
    gx, gy = lax.axis_index("gx"), lax.axis_index("gy")
    me = gx * NGY + gy

    field_ins = ((zonal_in, zonal), (merid_in, merid), (mask_in, mask), (vert_in, vert), (control_in, control))
    late_ins = ((owner_in, owner), (cell_in, cell), (weights_in, weights), (innov_in, innov), (obsw_in, obsw))
    loads = [
        pltpu.make_async_copy(src, dst, io_sem.at[n])
        for n, (src, dst) in enumerate(field_ins + late_ins + ((sigma_in, sigma),))
    ]
    stores = [
        pltpu.make_async_copy(src, dst, io_sem.at[len(loads) + n])
        for n, (src, dst) in enumerate(((inc, inc_out), (dep, dep_out), (grad, grad_out)))
    ]
    for copy in loads:
        copy.start()

    barrier = pltpu.get_barrier_semaphore()

    def greet(d, carry):
        to = lax.rem(me + d, NDEV)
        pl.semaphore_signal(barrier, inc=1, device_id=(lax.div(to, NGY), lax.rem(to, NGY)), device_id_type=MESH)
        return carry

    blocks(1, NDEV - 1, 8, greet, 0)

    def to_device(src, dst, send_sem, recv_sem, to):
        return pltpu.make_async_remote_copy(
            src_ref=src, dst_ref=dst, send_sem=send_sem, recv_sem=recv_sem,
            device_id=(lax.div(to, NGY), lax.rem(to, NGY)), device_id_type=MESH,
        )

    mine = lax.div(me, 2)
    partner = 2 * mine + 1 - lax.rem(me, 2)

    def send_rec(to):
        to_device(rec.at[to], recv.at[me], rec_send_sem, rec_recv_sem, to).start()

    def send_ret(to):
        to_device(ret_send.at[to], ret.at[me], ret_send_sem, ret_recv_sem, to).start()

    def wait_all(src, dst, send_sem, recv_sem):
        most = pl.ds(0, NDEV - 1)
        whole = to_device(src.at[most], dst.at[most], send_sem, recv_sem, me)
        whole.wait_recv()
        whole.wait_send()

    for copy in loads[:5]:
        copy.wait()
    for half in range(2):
        coef[half, STEPS * 8 : (STEPS + CX) * 8, :] = jnp.zeros((CX * 8, 128), F32)
        coef[half, ROWS * 8 :, :] = jnp.zeros(((ALL_ROWS - ROWS) * 8, 128), F32)
        for main in (main_a, main_c):
            main[half, ROWS * LEV :, :] = jnp.zeros(((ALL_ROWS - ROWS) * LEV, 128), F32)
    for x in range(0, CX, SOLVE_ROWS):
        rows = slice(x, x + SOLVE_ROWS)
        store_level(coef, 0, x, 8, SOLVE_ROWS, zonal[rows, :])
        store_level(coef, 1, x, 8, SOLVE_ROWS, merid[rows, :])
        store_level(coef, 2, x, 8, SOLVE_ROWS, mask[rows, :].astype(F32))
    pack_sides(coef, coef_low, coef_high, 8)
    solve_first(control, vert, mask, upper, inverse, reduced, main_a)
    pack_sides(main_a, low_a, high_a, LEV)

    pl.semaphore_wait(barrier, NDEV - 1)
    coef_copies = halo_copies(
        coef, coef_low, coef_high, coef_from_high, coef_from_low, halo_send.at[0], halo_recv.at[0], gx, gy, 8
    )
    field_copies = halo_copies(
        main_a, low_a, high_a, from_high_a, from_low_a, halo_send.at[1], halo_recv.at[1], gx, gy, LEV
    )
    for copy in coef_copies + field_copies:
        copy.start()

    for copy in loads[5:10]:
        copy.wait()
    slot_table(owner, cell, weights, rank, tab, lanes, tiles, cst)

    def pack_some(n, carry):
        j0 = lax.rem(mine + n * (PACK_PAIRS * PAIR_STRIDE), NDEV // 2)
        pack_records(j0, innov, obsw, lanes, tiles, cst, found_ref, rec)
        for q in range(1, PACK_PAIRS):
            j = lax.rem(j0 + q * PAIR_STRIDE, NDEV // 2)
            send_rec(2 * j)
            send_rec(2 * j + 1)
        send_first(n, j0, partner, send_rec)
        return carry

    lax.fori_loop(0, NDEV // 2 // PACK_PAIRS, pack_some, 0)
    own = pltpu.make_async_copy(rec.at[me], recv.at[me], self_sem)
    own.start()

    for copy in coef_copies:
        copy.wait()
    unpack_sides(coef_from_high, coef_from_low, coef_side, 8)
    build_faces(coef, coef_side, gy)
    expand_faces(coef, coef_side, face_x, face_y)
    for copy in field_copies:
        copy.wait()
    unpack_sides(from_high_a, from_low_a, side_a, LEV)
    diffuse(main_a, side_a, field_a, field_b, face_x, face_y)

    loads[10].wait()

    def scale(k, carry):
        for x in range(0, CX, 16):
            value = sigma[k, x : x + 16, :] * load_level(main_a, k, x, LEV, 16)
            inc[k, x : x + 16, :] = value
            high = value.astype(BF16)
            low = (value - high.astype(F32)).astype(BF16)
            at = pl.ds(pl.multiple_of(k * CX + x, 16), 16)
            field3[at, 0:256] = high
            field3[at, 256:512] = high
            field3[at, 512:768] = low
        return carry

    lax.fori_loop(0, LEV, scale, 0)
    stores[0].start()
    adj[...] = jnp.zeros_like(adj)

    own.wait()
    wait_all(rec, recv, rec_send_sem, rec_recv_sem)
    observe_all(mine, partner, recv, field3, adj, ret_send, send_ret)
    own = pltpu.make_async_copy(ret_send.at[me], ret.at[me], self_sem)
    own.start()

    def weigh(k, carry):
        for x in range(0, CX, SOLVE_ROWS):
            at = pl.ds(pl.multiple_of(k * CX + x, SOLVE_ROWS), SOLVE_ROWS)
            store_level(main_c, k, x, LEV, SOLVE_ROWS, sigma[k, x : x + SOLVE_ROWS, :] * adj[at, :])
        return carry

    lax.fori_loop(0, LEV, weigh, 0)
    pack_sides(main_c, low_c, high_c, LEV)
    adj_copies = halo_copies(
        main_c, low_c, high_c, from_high_c, from_low_c, halo_send.at[2], halo_recv.at[2], gx, gy, LEV
    )
    for copy in adj_copies:
        copy.start()

    own.wait()
    wait_all(ret_send, ret, ret_send_sem, ret_recv_sem)
    unpack(ret, owner, rank, innov, dep, ret_low, ret_high)
    stores[1].start()

    for copy in adj_copies:
        copy.wait()
    unpack_sides(from_high_c, from_low_c, side_c, LEV)
    diffuse(main_c, side_c, field_a, field_b, face_x, face_y)
    solve_last(main_c, control, vert, mask, upper, inverse, reduced, grad)
    stores[2].start()
    for copy in stores:
        copy.wait()


def gradient_call(*args):
    anywhere = pl.BlockSpec(memory_space=pl.ANY)

    def field(rows, lanes, lev=LEV):
        shape = (rows * lev, 128)
        return pltpu.VMEM(shape if lanes == 128 else (2,) + shape, F32)

    def sides(lev):
        return [field(8, 128, lev), field(8, 128, lev), field(GROUPS, 128, lev), field(GROUPS, 128, lev)]

    outs = (
        jax.ShapeDtypeStruct((LEV, CX, CY), F32),
        jax.ShapeDtypeStruct((LEV, PROF), F32),
        jax.ShapeDtypeStruct((LEV, CX, CY), F32),
    )
    return pl.pallas_call(
        main_kernel,
        out_shape=outs,
        in_specs=[anywhere] * len(args),
        out_specs=(anywhere,) * len(outs),
        scratch_shapes=[
            *[pltpu.VMEM(a.shape, a.dtype) for a in args + outs],
            pltpu.SemaphoreType.DMA((len(args) + len(outs),)),
            pltpu.VMEM((NDEV, REC, 128), F32),
            pltpu.VMEM((NDEV, REC, 128), F32),
            pltpu.VMEM((NDEV, 8, 128), F32),
            pltpu.VMEM((NDEV, 8, 128), F32),
            pltpu.VMEM((TILES, 128), jnp.int32),
            pltpu.VMEM((NDEV, 128), jnp.int32),
            pltpu.VMEM((NDEV // 2, 128), jnp.int32),
            pltpu.VMEM((NDEV // 2, 128), jnp.int32),
            pltpu.VMEM((8, PROF // 2), F32),
            pltpu.VMEM((PACK_PAIRS, 40, 128), F32),
            pltpu.VMEM((NDEV // 2, 8, 128), F32),
            pltpu.VMEM((NDEV // 2, 8, 128), F32),
            field(ALL_ROWS, 256, 8), field(SROWS, 128, 8), *sides(8),
            field(ALL_ROWS, 256), field(SROWS, 128),
            field(ALL_ROWS, 256), field(SROWS, 128),
            pltpu.VMEM((SEG + 2, COLS, 128), F32), pltpu.VMEM((SEG + 2, COLS, 128), F32),
            pltpu.VMEM((SEG + 1, COLS, 128), F32), pltpu.VMEM((SEG, COLS, 128), F32),
            *sides(LEV), *sides(LEV),
            pltpu.VMEM((LEV, CX, CY), F32),
            pltpu.VMEM((LEV, CX, CY), F32),
            pltpu.VMEM((LEV, CX, CY), F32),
            pltpu.VMEM((LEV * CX, 3 * CY), BF16),
            pltpu.VMEM((LEV * CX, CY), F32),
            pltpu.SemaphoreType.DMA, pltpu.SemaphoreType.DMA, pltpu.SemaphoreType.DMA, pltpu.SemaphoreType.DMA,
            pltpu.SemaphoreType.DMA,
            pltpu.SemaphoreType.DMA((3, 8)), pltpu.SemaphoreType.DMA((3, 8)),
        ],
        compiler_params=pltpu.CompilerParams(
            collective_id=0, has_side_effects=True, vmem_limit_bytes=VMEM_LIMIT
        ),
        name="gradient",
    )(*args)


def shards(control, sigma, vert_diff, zonal_diff, merid_diff, ocean_mask, owner, cell, interp_weights, innovation, obs_weight):
    return gradient_call(
        control, sigma, vert_diff, zonal_diff, merid_diff, ocean_mask,
        owner.reshape(TILES, 128), cell.reshape(TILES, 128), interp_weights, innovation, obs_weight,
    )


def solution(mesh):
    in_specs = (
        P(None, "gx", "gy"),
        P(None, "gx", "gy"),
        P(None, "gx", "gy"),
        P("gx", "gy"),
        P("gx", "gy"),
        P("gx", "gy"),
        P(("gx", "gy"), None),
        P(("gx", "gy")),
        P(None, ("gx", "gy")),
        P(None, ("gx", "gy")),
        P(None, ("gx", "gy")),
    )
    out_specs = (P(None, "gx", "gy"), P(None, ("gx", "gy")), P(None, "gx", "gy"))
    return jax.shard_map(shards, mesh=mesh, in_specs=in_specs, out_specs=out_specs, check_vma=False)
```

```python
import functools

import jax
import jax.numpy as jnp
from jax import lax
from jax.experimental import pallas as pl
from jax.experimental.pallas import tpu as pltpu
from jax.sharding import PartitionSpec as P

MESH = pl.DeviceIdType.MESH
F32 = jnp.float32
BF16 = jnp.bfloat16
VMEM_LIMIT = 60 * 1024 * 1024

LEV = 16
STEPS = 10
CX = 64
CY = 256
NGX = 16
NGY = 8
NDEV = NGX * NGY
PROF = 2048
CAP = 64
TILES = PROF // 128
ROWS = CX + 2 * STEPS
SPAD = 6
SROWS = 96
GROUPS = 12
REC = 18
DIFFUSE_TILES = 4
SEG = 11
ALL_ROWS = 8 * SEG
EDGE = 24
COLS = CY + 2 * EDGE
PACK_PAIRS = 8
WAVES = NDEV // 2 // PACK_PAIRS
OBSERVE_TILES = 8
UNPACK_TILES = 2


def lane_iota(rows):
    return lax.broadcasted_iota(jnp.int32, (rows, 128), 1)


def blocks(start, count, width, body, carry):
    def many(i, carry):
        for q in range(width):
            carry = body(start + width * i + q, carry)
        return carry

    carry = lax.fori_loop(0, count // width, many, carry)
    for q in range(count - count % width, count):
        carry = body(start + q, carry)
    return carry


def lane_gather(source, lane):
    return jnp.take_along_axis(source, lane, axis=1, mode="promise_in_bounds")


def split_pair(low, high, left):
    first = jnp.where(left, low, pltpu.roll(high, 64, axis=1))
    second = jnp.where(left, pltpu.roll(low, 64, axis=1), high)
    return first, second


def slot_table(owner, cell, weights, rank_out, tab, lanes, tiles, cst):
    rows_o = lax.broadcasted_iota(jnp.int32, (NDEV, 256), 0)
    before = (
        lax.broadcasted_iota(jnp.int32, (256, 256), 0) < lax.broadcasted_iota(jnp.int32, (256, 256), 1)
    ).astype(F32).astype(BF16)
    ones = jnp.ones((256, 256), BF16)
    rows_r = lax.broadcasted_iota(jnp.int32, (CAP, 256), 0)
    cols_p = lax.broadcasted_iota(jnp.int32, (CAP, 256), 1)
    earlier = jnp.zeros((NDEV, 256), F32)
    table = jnp.zeros((NDEV, 128), F32)
    for block in range(PROF // 256):
        owners = jnp.concatenate([owner[2 * block : 2 * block + 1, :], owner[2 * block + 1 : 2 * block + 2, :]], axis=1)
        hot = (rows_o == owners).astype(F32)
        hot16 = hot.astype(BF16)
        count = earlier + jnp.dot(hot16, before, preferred_element_type=F32)
        rank = jnp.sum(hot * count, axis=0, keepdims=True).astype(jnp.int32)
        earlier = earlier + jnp.dot(hot16, ones, preferred_element_type=F32)
        rank_out[2 * block : 2 * block + 1, :] = rank[:, :128]
        rank_out[2 * block + 1 : 2 * block + 2, :] = rank[:, 128:]
        same = rows_r == rank
        lane = jnp.where(same, cols_p % 128, 0).astype(F32).astype(BF16)
        tile = jnp.where(same, 2 * block + 1 + cols_p // 128, 0).astype(F32).astype(BF16)
        table = table + lax.dot_general(
            hot16, jnp.concatenate([lane, tile], axis=0), (((1,), (1,)), ((), ())), preferred_element_type=F32
        )
    tab[...] = table.astype(jnp.int32)
    half = lane_iota(NDEV // 2) < 64
    even, odd = tab[pl.ds(0, NDEV // 2, stride=2), :], tab[pl.ds(1, NDEV // 2, stride=2), :]
    lanes[...] = jnp.where(half, even, pltpu.roll(odd, 64, axis=1))
    tiles[...] = jnp.where(half, pltpu.roll(even, 64, axis=1), odd)

    cst[...] = jnp.zeros_like(cst)
    for tile in range(TILES):
        cols = slice(128 * tile, 128 * tile + 128)
        to = slice(128 * (tile // 2), 128 * (tile // 2) + 128)
        row = 4 * (tile % 2)
        cst[row : row + 1, to] = cell[tile : tile + 1, :].astype(F32)
        cst[row + 1 : row + 2, to] = weights[1:2, cols] + weights[3:4, cols]
        cst[row + 2 : row + 3, to] = weights[2:3, cols] + weights[3:4, cols]


def pack_records(j0, innov, obsw, lanes, tiles, cst, found_ref, rec):
    left = lane_iota(8) < 64
    left_row = lane_iota(1) < 64
    below = lax.broadcasted_iota(jnp.int32, (8, 128), 0) // 4

    for q in range(PACK_PAIRS):
        j = lax.rem(j0 + q * WAVES, NDEV // 2)
        lane = jnp.broadcast_to(lanes[pl.ds(j, 1), :], (8, 128))
        tile_of = jnp.broadcast_to(tiles[pl.ds(j, 1), :], (8, 128))
        tile_up = tile_of - below
        zero = jnp.zeros((8, 128), F32)
        place, found = zero, [zero] * 4
        for tile in range(TILES):
            cols = slice(128 * tile, 128 * tile + 128)
            here = tile_of == tile + 1
            found = [
                jnp.where(here, lane_gather(source, lane), old)
                for source, old in zip((innov[0:8, cols], innov[8:16, cols], obsw[0:8, cols], obsw[8:16, cols]), found)
            ]
            if tile % 2 == 0:
                both = lane_gather(cst[:, 64 * tile : 64 * tile + 128], lane)
                place = jnp.where(tile_up == tile + 1, both, place)
        found_ref[q] = jnp.concatenate(found + [place], axis=0)

    for q in range(PACK_PAIRS):
        j = lax.rem(j0 + q * WAVES, NDEV // 2)
        both = found_ref[q]
        place = both[32:36] + both[36:40]
        turned = pltpu.roll(place, 64, axis=1)
        first_i, second_i = split_pair(both[0:8], both[8:16], left)
        first_o, second_o = split_pair(both[16:24], both[24:32], left)
        for side, parts in enumerate((
            [first_i, first_o, jnp.where(left_row, place[0:1], turned[1:2]), place[2:3]],
            [second_i, second_o, jnp.where(left_row, turned[0:1], place[1:2]), turned[2:3]],
        )):
            for row, value in zip((0, 8, 16, 17), parts):
                rec[2 * j + side, row : row + value.shape[0], :] = value


def unpack(ret, owner, rank, innov, dep, low_ref, high_ref):
    left = lane_iota(8) < 64

    def pair(j, carry):
        one, two = ret[2 * j], ret[2 * j + 1]
        low_ref[j] = jnp.where(left, one, pltpu.roll(two, 64, axis=1))
        high_ref[j] = jnp.where(left, pltpu.roll(one, 64, axis=1), two)
        return carry

    blocks(0, NDEV // 2, 16, pair, 0)

    def tile(t, carry):
        owners = jnp.broadcast_to(owner[pl.ds(t, 1), :], (8, 128))
        lane = jnp.broadcast_to(rank[pl.ds(t, 1), :], (8, 128)) + 64 * (owners % 2)
        pair_of = owners // 2
        low = high = jnp.zeros((8, 128), F32)
        for j in range(NDEV // 2):
            here = pair_of == j
            low = jnp.where(here, lane_gather(low_ref[j], lane), low)
            high = jnp.where(here, lane_gather(high_ref[j], lane), high)
        cols = pl.ds(pl.multiple_of(128 * t, 128), 128)
        dep[0:8, cols] = low - innov[0:8, cols]
        dep[8:16, cols] = high - innov[8:16, cols]
        return carry

    blocks(0, TILES, UNPACK_TILES, tile, 0)


def pack_sides(main, low_side, high_side, lev):
    slot = lane_iota(lev) // 16

    def group(g, carry):
        low = jnp.zeros((lev, 128), F32)
        high = jnp.zeros((lev, 128), F32)
        for m in range(8):
            at = pl.ds(pl.multiple_of((STEPS + 8 * g + m) * lev, lev), lev)
            here = slot == m
            first = main[0, at, :]
            last = main[1, at, :]
            low = jnp.where(here, first if m == 0 else pltpu.roll(first, 16 * m, axis=1), low)
            high = jnp.where(here, last if m == 7 else pltpu.roll(last, 16 * m + 16, axis=1), high)
        at = pl.ds(pl.multiple_of(g * lev, lev), lev)
        low_side[at, :] = low
        high_side[at, :] = high
        return carry

    lax.fori_loop(0, CX // 8, group, 0)


def unpack_sides(from_high, from_low, side, lev):
    left = lane_iota(lev) < 64

    def group(g, carry):
        at = pl.ds(pl.multiple_of(g * lev, lev), lev)
        right_strip = from_high[at, :]
        left_strip = from_low[at, :]
        for m in range(8):
            right = right_strip if m == 0 else pltpu.roll(right_strip, 128 - 16 * m, axis=1)
            leftv = left_strip if m == 7 else pltpu.roll(left_strip, 112 - 16 * m, axis=1)
            side[pl.ds(pl.multiple_of((8 * g + m) * lev, lev), lev), :] = jnp.where(left, right, leftv)
        return carry

    lax.fori_loop(0, GROUPS, group, 0)


def halo_copies(main, low_side, high_side, from_high, from_low, send_sem, recv_sem, gx, gy, lev):
    west, east = (gx + NGX - 1) % NGX, (gx + 1) % NGX
    south, north = (gy + NGY - 1) % NGY, (gy + 1) % NGY

    def rows(ref, start, count):
        at = pl.ds(start * lev, count * lev)
        return ref.at[:, at, :] if len(ref.shape) == 3 else ref.at[at, :]

    plan = (
        (rows(main, STEPS, STEPS), rows(main, STEPS + CX, STEPS), (west, gy)),
        (rows(main, CX, STEPS), rows(main, 0, STEPS), (east, gy)),
        (rows(low_side, 0, 8), rows(from_high, 2, 8), (gx, south)),
        (rows(high_side, 0, 8), rows(from_low, 2, 8), (gx, north)),
        (rows(low_side, 0, 2), rows(from_high, 10, 2), (west, south)),
        (rows(low_side, 6, 2), rows(from_high, 0, 2), (east, south)),
        (rows(high_side, 0, 2), rows(from_low, 10, 2), (west, north)),
        (rows(high_side, 6, 2), rows(from_low, 0, 2), (east, north)),
    )
    return [
        pltpu.make_async_remote_copy(
            src_ref=src,
            dst_ref=dst,
            send_sem=send_sem.at[i],
            recv_sem=recv_sem.at[i],
            device_id=device,
            device_id_type=MESH,
        )
        for i, (src, dst, device) in enumerate(plan)
    ]


def next_cols(parts, last):
    rolled = [pltpu.roll(part, 127, axis=1) for part in parts]
    return [jnp.where(last, rolled[(i + 1) % 3], rolled[i]) for i in range(3)]


def build_faces(coef, coef_side, gy):
    lane = lane_iota(1)
    first_part = jnp.where(gy < NGY - 1, 1.0, 0.0).astype(F32)
    last_part = jnp.where(gy > 0, 1.0, 0.0).astype(F32)
    inside = jnp.where(lane < 64, first_part, last_part)
    last = lane == 127

    def row(r, which):
        at = pl.ds(r * 8 + which, 1)
        return [coef[0, at, :], coef[1, at, :], coef_side[pl.ds((r + SPAD) * 8 + which, 1), :]]

    def put(r, which, parts):
        at = pl.ds(r * 8 + which, 1)
        coef[0, at, :] = parts[0]
        coef[1, at, :] = parts[1]
        coef_side[pl.ds((r + SPAD) * 8 + which, 1), :] = parts[2]

    def wet_row(r):
        one, two, side = row(r, 2)
        return [one, two, side * inside]

    def one(r, wet):
        ahead = wet_row(r + 1)
        zonal, merid = row(r, 0), row(r, 1)
        north = next_cols(wet, last)
        put(r, 0, [z * w * a for z, w, a in zip(zonal, wet, ahead)])
        put(r, 1, [m * w * n for m, w, n in zip(merid, wet, north)])
        return tuple(ahead)

    blocks(0, ROWS - 1, 8, one, tuple(wet_row(0)))


def put_columns(plane, parts):
    first, second, side = [part.T for part in parts]
    plane[EDGE : EDGE + 128, :] = first
    plane[EDGE + 128 : EDGE + 256, :] = second
    plane[EDGE + CY : EDGE + CY + 16, :] = side[0:16]
    plane[EDGE - 16 : EDGE, :] = side[112:128]


def expand_faces(coef, coef_side, face_x, face_y):
    def one(place, carry):
        for which, planes, to in ((0, face_x, place + 1), (1, face_y, place)):
            parts = []
            for ref, pad in ((coef.at[0], 0), (coef.at[1], 0), (coef_side, SPAD)):
                rows = [ref[pl.ds((SEG * seg + place + pad) * 8 + which, 1), :] for seg in range(8)]
                parts.append(jnp.concatenate([jnp.broadcast_to(row, (LEV, 128)) for row in rows], axis=0))
            put_columns(planes.at[to], parts)
        return carry

    blocks(0, SEG, 2, one, 0)
    face_x[0] = pltpu.roll(face_x[SEG], LEV, axis=1)


def turn_edges(field):
    field[0] = pltpu.roll(field[SEG], LEV, axis=1)
    field[SEG + 1] = pltpu.roll(field[1], 128 - LEV, axis=1)


def diffuse(main, side, field_a, field_b, face_x, face_y):
    def enter(place, carry):
        parts = []
        for ref, pad in ((main.at[0], 0), (main.at[1], 0), (side, SPAD)):
            rows = [pl.ds(pl.multiple_of((SEG * seg + place + pad) * LEV, LEV), LEV) for seg in range(8)]
            parts.append(jnp.concatenate([ref[at, :] for at in rows], axis=0))
        put_columns(field_a.at[place + 1], parts)
        return carry

    blocks(0, SEG, 4, enter, 0)
    bottom = lax.broadcasted_iota(jnp.int32, (8, 128), 0) == 7
    turn_edges(field_a)

    for step in range(STEPS):
        now, new = (field_a, field_b) if step % 2 == 0 else (field_b, field_a)

        def north_flux(t, p, here):
            row = pl.multiple_of(8 * t, 8)
            return face_y[p - 1, pl.ds(row, 8), :] * (now[p, pl.ds(row + 1, 8), :] - here)

        def tile(t, carry):
            at = pl.ds(pl.multiple_of(8 * t, 8), 8)
            here, west = now[1, at, :], face_x[0, at, :] * (now[1, at, :] - now[0, at, :])
            norths = []
            for p in range(1, SEG + 1):
                ahead = now[p + 1, at, :]
                east = face_x[p, at, :] * (ahead - here)
                north = north_flux(t, p, here)
                south = pltpu.roll(jnp.where(bottom, carry[p - 1], north), 1, axis=0)
                new[p, at, :] = here + ((east - west) + (north - south))
                here, west = ahead, east
                norths.append(north)
            return tuple(norths)

        first = (EDGE - (STEPS - 1 - step)) // 8
        last = (EDGE + CY + (STEPS - 1 - step) + 7) // 8
        before = [north_flux(first - 1, p, now[p, 8 * first - 8 : 8 * first, :]) for p in range(1, SEG + 1)]
        blocks(first, last - first, DIFFUSE_TILES, tile, tuple(before))
        if step < STEPS - 1:
            turn_edges(new)

    def leave(place, carry):
        for half in range(2):
            rows = field_a[place + 1, EDGE + 128 * half : EDGE + 128 * half + 128, :].T
            for seg in range(8):
                at = pl.ds(pl.multiple_of((SEG * seg + place) * LEV, LEV), LEV)
                main[half, at, :] = rows[LEV * seg : LEV * seg + LEV]
        return carry

    blocks(0, SEG, 4, leave, 0)


SOLVE_ROWS = 32


def load_level(ref, level, x, lev, count):
    at = pl.ds((STEPS + x) * lev + level, count, stride=lev)
    return jnp.concatenate([ref[0, at, :], ref[1, at, :]], axis=1)


def store_level(ref, level, x, lev, count, value):
    at = pl.ds((STEPS + x) * lev + level, count, stride=lev)
    ref[0, at, :] = value[:, 0:128]
    ref[1, at, :] = value[:, 128:256]


def solve_first(control, vert, mask, upper, inverse, reduced, main):
    for x in range(0, CX, SOLVE_ROWS):
        rows = slice(x, x + SOLVE_ROWS)
        wet = mask[rows, :].astype(F32)
        previous = None
        for k in range(LEV):
            rhs = wet * control[k, rows, :]
            diagonal = 1.0
            if k > 0:
                below = vert[k - 1, rows, :]
                diagonal = diagonal + below
            if k < LEV - 1:
                above = vert[k, rows, :]
                diagonal = diagonal + above
            if k > 0:
                diagonal = diagonal + below * up
                rhs = rhs + below * previous
            inv = 1.0 / diagonal
            inverse[k, rows, :] = inv
            if k < LEV - 1:
                up = -above * inv
                upper[k, rows, :] = up
            previous = rhs * inv
            if k < LEV - 1:
                reduced[k, rows, :] = previous
        value = previous
        store_level(main, LEV - 1, x, LEV, SOLVE_ROWS, value)
        for k in range(LEV - 2, -1, -1):
            value = reduced[k, rows, :] - upper[k, rows, :] * value
            store_level(main, k, x, LEV, SOLVE_ROWS, value)


def solve_last(main, control, vert, mask, upper, inverse, reduced, grad):
    for x in range(0, CX, SOLVE_ROWS):
        rows = slice(x, x + SOLVE_ROWS)
        wet = mask[rows, :].astype(F32)
        previous = None
        for k in range(LEV):
            rhs = load_level(main, k, x, LEV, SOLVE_ROWS)
            if k > 0:
                rhs = rhs + vert[k - 1, rows, :] * previous
            previous = rhs * inverse[k, rows, :]
            if k < LEV - 1:
                reduced[k, rows, :] = previous
        value = previous
        grad[LEV - 1, rows, :] = control[LEV - 1, rows, :] + wet * value
        for k in range(LEV - 2, -1, -1):
            value = reduced[k, rows, :] - upper[k, rows, :] * value
            grad[k, rows, :] = control[k, rows, :] + wet * value


def send_first(n, j, partner, send):
    @pl.when(n > 0)
    def _():
        send(2 * j)
        send(2 * j + 1)

    @pl.when(n == 0)
    def _():
        send(partner)


def observe_all(mine, partner, arrived, recv, field3, adj, ret_send, send):
    left = lane_iota(8) < 64
    left_row = lane_iota(1) < 64
    width = OBSERVE_TILES * 128
    rows_b = lax.broadcasted_iota(jnp.int32, (CY, width), 0).astype(F32)
    rows_a = lax.broadcasted_iota(jnp.int32, (CX, width), 0).astype(F32)

    groups = NDEV // 2 // OBSERVE_TILES
    assert groups == WAVES

    def observe(n, carry):
        pairs = [lax.rem(mine + n + groups * h, NDEV // 2) for h in range(OBSERVE_TILES)]
        arrived(n)
        parts = []
        for h in range(OBSERVE_TILES):
            one, two = recv[2 * pairs[h]], recv[2 * pairs[h] + 1]
            turned_one, turned_two = pltpu.roll(one, 64, axis=1), pltpu.roll(two, 64, axis=1)
            parts.append((
                jnp.where(left_row, one[16:17], turned_two[16:17]),
                jnp.where(left_row, turned_one[16:17], two[16:17]),
                jnp.where(left_row, one[17:18], turned_two[17:18]),
                jnp.where(left, one[0:8], turned_two[0:8]),
                jnp.where(left, turned_one[0:8], two[0:8]),
                jnp.where(left, one[8:16], turned_two[8:16]),
                jnp.where(left, turned_one[8:16], two[8:16]),
            ))
        cell, along_x, along_y, low_i, high_i, low_o, high_o = [jnp.concatenate(part, axis=1) for part in zip(*parts)]
        innov = jnp.concatenate([low_i, high_i], axis=0)
        obsw = jnp.concatenate([low_o, high_o], axis=0)
        cell_a = jnp.floor(cell * (1.0 / CY))
        cell_b = cell - CY * cell_a
        from_a = rows_a - cell_a
        from_b = rows_b - cell_b
        in_x = jnp.where(from_a == 0.0, 1.0 - along_x, jnp.where(from_a == 1.0, along_x, 0.0))
        in_y = jnp.where(from_b == 0.0, 1.0 - along_y, jnp.where(from_b == 1.0, along_y, 0.0))
        y_high = in_y.astype(BF16)
        y_low = (in_y - y_high.astype(F32)).astype(BF16)
        y_rows = jnp.concatenate([y_high, y_low, y_high], axis=0)
        vals = []
        for k in range(0, LEV, 4):
            rows = jnp.dot(field3[CX * k : CX * (k + 4), :], y_rows, preferred_element_type=F32)
            vals.append(jnp.sum(rows.reshape(4, CX, width) * in_x[None], axis=1))
        vals = jnp.concatenate(vals, axis=0)
        forcing = obsw * (vals - innov)
        for h in range(OBSERVE_TILES):
            cols = slice(128 * h, 128 * h + 128)
            first, second = split_pair(vals[0:8, cols], vals[8:16, cols], left)
            ret_send[2 * pairs[h]] = first
            ret_send[2 * pairs[h] + 1] = second
        for h in range(1, OBSERVE_TILES):
            send(2 * pairs[h])
            send(2 * pairs[h] + 1)
        spread = (in_x[None] * forcing[:, None, :]).reshape(LEV * CX, width)
        high = spread.astype(BF16)
        low = (spread - high.astype(F32)).astype(BF16)
        adj[...] += lax.dot_general(
            jnp.concatenate([high, high, low], axis=1),
            jnp.concatenate([y_high, y_low, y_high], axis=1),
            (((1,), (1,)), ((), ())),
            preferred_element_type=F32,
        )
        send_first(n, pairs[0], partner, send)
        return carry

    lax.fori_loop(0, groups, observe, 0)


def main_kernel(
    control_in, sigma_in, vert_in, zonal_in, merid_in, mask_in, owner_in, cell_in, weights_in, innov_in, obsw_in,
    inc_out, dep_out, grad_out,
    control, sigma, vert, zonal, merid, mask, owner, cell, weights, innov, obsw, inc, dep, grad, io_sem,
    rec, recv, ret_send, ret, rank, tab, lanes, tiles, cst, found_ref, ret_low, ret_high,
    coef, coef_side, coef_low, coef_high, coef_from_high, coef_from_low,
    main_a, side_a, main_c, side_c, field_a, field_b, face_x, face_y,
    low_a, high_a, from_high_a, from_low_a, low_c, high_c, from_high_c, from_low_c,
    upper, inverse, reduced, field3, adj,
    rec_send_sem, rec_recv_sem, ret_send_sem, ret_recv_sem, self_sem, halo_send, halo_recv,
):
    gx, gy = lax.axis_index("gx"), lax.axis_index("gy")
    me = gx * NGY + gy

    field_ins = ((zonal_in, zonal), (merid_in, merid), (mask_in, mask), (vert_in, vert), (control_in, control))
    late_ins = ((owner_in, owner), (cell_in, cell), (weights_in, weights), (innov_in, innov), (obsw_in, obsw))
    loads = [
        pltpu.make_async_copy(src, dst, io_sem.at[n])
        for n, (src, dst) in enumerate(field_ins + late_ins + ((sigma_in, sigma),))
    ]
    stores = [
        pltpu.make_async_copy(src, dst, io_sem.at[len(loads) + n])
        for n, (src, dst) in enumerate(((inc, inc_out), (dep, dep_out), (grad, grad_out)))
    ]
    for copy in loads:
        copy.start()

    barrier = pltpu.get_barrier_semaphore()

    def greet(d, carry):
        to = lax.rem(me + d, NDEV)
        pl.semaphore_signal(barrier, inc=1, device_id=(lax.div(to, NGY), lax.rem(to, NGY)), device_id_type=MESH)
        return carry

    blocks(1, NDEV - 1, 8, greet, 0)

    def to_device(src, dst, send_sem, recv_sem, to):
        return pltpu.make_async_remote_copy(
            src_ref=src, dst_ref=dst, send_sem=send_sem, recv_sem=recv_sem,
            device_id=(lax.div(to, NGY), lax.rem(to, NGY)), device_id_type=MESH,
        )

    mine = lax.div(me, 2)
    partner = 2 * mine + 1 - lax.rem(me, 2)

    def rec_copy(to, wave):
        return to_device(rec.at[to], recv.at[me], rec_send_sem, rec_recv_sem.at[wave], to)

    def send_ret(to):
        to_device(ret_send.at[to], ret.at[me], ret_send_sem, ret_recv_sem, to).start()

    def wait_all(src, dst, send_sem, recv_sem):
        most = pl.ds(0, NDEV - 1)
        whole = to_device(src.at[most], dst.at[most], send_sem, recv_sem, me)
        whole.wait_recv()
        whole.wait_send()

    for copy in loads[:5]:
        copy.wait()
    for half in range(2):
        coef[half, STEPS * 8 : (STEPS + CX) * 8, :] = jnp.zeros((CX * 8, 128), F32)
        coef[half, ROWS * 8 :, :] = jnp.zeros(((ALL_ROWS - ROWS) * 8, 128), F32)
        for main in (main_a, main_c):
            main[half, ROWS * LEV :, :] = jnp.zeros(((ALL_ROWS - ROWS) * LEV, 128), F32)
    for x in range(0, CX, SOLVE_ROWS):
        rows = slice(x, x + SOLVE_ROWS)
        store_level(coef, 0, x, 8, SOLVE_ROWS, zonal[rows, :])
        store_level(coef, 1, x, 8, SOLVE_ROWS, merid[rows, :])
        store_level(coef, 2, x, 8, SOLVE_ROWS, mask[rows, :].astype(F32))
    pack_sides(coef, coef_low, coef_high, 8)
    solve_first(control, vert, mask, upper, inverse, reduced, main_a)
    pack_sides(main_a, low_a, high_a, LEV)

    pl.semaphore_wait(barrier, NDEV - 1)
    coef_copies = halo_copies(
        coef, coef_low, coef_high, coef_from_high, coef_from_low, halo_send.at[0], halo_recv.at[0], gx, gy, 8
    )
    field_copies = halo_copies(
        main_a, low_a, high_a, from_high_a, from_low_a, halo_send.at[1], halo_recv.at[1], gx, gy, LEV
    )
    for copy in coef_copies + field_copies:
        copy.start()

    for copy in loads[5:10]:
        copy.wait()
    slot_table(owner, cell, weights, rank, tab, lanes, tiles, cst)

    def pack_some(n, carry):
        j0 = lax.rem(mine + NDEV // 2 - n, NDEV // 2)
        pack_records(j0, innov, obsw, lanes, tiles, cst, found_ref, rec)
        return carry

    def send_some(n, carry):
        j0 = lax.rem(mine + NDEV // 2 - n, NDEV // 2)

        def send(to):
            rec_copy(to, n).start()

        for q in range(1, PACK_PAIRS):
            j = lax.rem(j0 + q * WAVES, NDEV // 2)
            send(2 * j)
            send(2 * j + 1)
        send_first(n, j0, partner, send)
        return carry

    lax.fori_loop(0, WAVES, pack_some, 0)
    own = pltpu.make_async_copy(rec.at[me], recv.at[me], self_sem)
    own.start()

    for copy in coef_copies:
        copy.wait()
    unpack_sides(coef_from_high, coef_from_low, coef_side, 8)
    build_faces(coef, coef_side, gy)
    expand_faces(coef, coef_side, face_x, face_y)
    for copy in field_copies:
        copy.wait()
    lax.fori_loop(0, WAVES, send_some, 0)
    unpack_sides(from_high_a, from_low_a, side_a, LEV)
    diffuse(main_a, side_a, field_a, field_b, face_x, face_y)

    loads[10].wait()

    def scale(k, carry):
        for x in range(0, CX, 16):
            value = sigma[k, x : x + 16, :] * load_level(main_a, k, x, LEV, 16)
            inc[k, x : x + 16, :] = value
            high = value.astype(BF16)
            low = (value - high.astype(F32)).astype(BF16)
            at = pl.ds(pl.multiple_of(k * CX + x, 16), 16)
            field3[at, 0:256] = high
            field3[at, 256:512] = high
            field3[at, 512:768] = low
        return carry

    lax.fori_loop(0, LEV, scale, 0)
    stores[0].start()
    adj[...] = jnp.zeros_like(adj)

    own.wait()

    def arrived(n):
        def some(count):
            at = pl.ds(0, count)
            to_device(rec.at[at], recv.at[at], rec_send_sem, rec_recv_sem.at[n], me).wait_recv()

        @pl.when(n == 0)
        def _():
            some(2 * PACK_PAIRS - 1)

        @pl.when(n > 0)
        def _():
            some(2 * PACK_PAIRS)

    observe_all(mine, partner, arrived, recv, field3, adj, ret_send, send_ret)
    most = pl.ds(0, NDEV - 1)
    to_device(rec.at[most], recv.at[most], rec_send_sem, rec_recv_sem.at[0], me).wait_send()
    own = pltpu.make_async_copy(ret_send.at[me], ret.at[me], self_sem)
    own.start()

    def weigh(k, carry):
        for x in range(0, CX, SOLVE_ROWS):
            at = pl.ds(pl.multiple_of(k * CX + x, SOLVE_ROWS), SOLVE_ROWS)
            store_level(main_c, k, x, LEV, SOLVE_ROWS, sigma[k, x : x + SOLVE_ROWS, :] * adj[at, :])
        return carry

    lax.fori_loop(0, LEV, weigh, 0)
    pack_sides(main_c, low_c, high_c, LEV)
    adj_copies = halo_copies(
        main_c, low_c, high_c, from_high_c, from_low_c, halo_send.at[2], halo_recv.at[2], gx, gy, LEV
    )
    for copy in adj_copies:
        copy.start()

    own.wait()
    wait_all(ret_send, ret, ret_send_sem, ret_recv_sem)
    unpack(ret, owner, rank, innov, dep, ret_low, ret_high)
    stores[1].start()

    for copy in adj_copies:
        copy.wait()
    unpack_sides(from_high_c, from_low_c, side_c, LEV)
    diffuse(main_c, side_c, field_a, field_b, face_x, face_y)
    solve_last(main_c, control, vert, mask, upper, inverse, reduced, grad)
    stores[2].start()
    for copy in stores:
        copy.wait()


def gradient_call(*args):
    anywhere = pl.BlockSpec(memory_space=pl.ANY)

    def field(rows, lanes, lev=LEV):
        shape = (rows * lev, 128)
        return pltpu.VMEM(shape if lanes == 128 else (2,) + shape, F32)

    def sides(lev):
        return [field(8, 128, lev), field(8, 128, lev), field(GROUPS, 128, lev), field(GROUPS, 128, lev)]

    outs = (
        jax.ShapeDtypeStruct((LEV, CX, CY), F32),
        jax.ShapeDtypeStruct((LEV, PROF), F32),
        jax.ShapeDtypeStruct((LEV, CX, CY), F32),
    )
    return pl.pallas_call(
        main_kernel,
        out_shape=outs,
        in_specs=[anywhere] * len(args),
        out_specs=(anywhere,) * len(outs),
        scratch_shapes=[
            *[pltpu.VMEM(a.shape, a.dtype) for a in args + outs],
            pltpu.SemaphoreType.DMA((len(args) + len(outs),)),
            pltpu.VMEM((NDEV, REC, 128), F32),
            pltpu.VMEM((NDEV, REC, 128), F32),
            pltpu.VMEM((NDEV, 8, 128), F32),
            pltpu.VMEM((NDEV, 8, 128), F32),
            pltpu.VMEM((TILES, 128), jnp.int32),
            pltpu.VMEM((NDEV, 128), jnp.int32),
            pltpu.VMEM((NDEV // 2, 128), jnp.int32),
            pltpu.VMEM((NDEV // 2, 128), jnp.int32),
            pltpu.VMEM((8, PROF // 2), F32),
            pltpu.VMEM((PACK_PAIRS, 40, 128), F32),
            pltpu.VMEM((NDEV // 2, 8, 128), F32),
            pltpu.VMEM((NDEV // 2, 8, 128), F32),
            field(ALL_ROWS, 256, 8), field(SROWS, 128, 8), *sides(8),
            field(ALL_ROWS, 256), field(SROWS, 128),
            field(ALL_ROWS, 256), field(SROWS, 128),
            pltpu.VMEM((SEG + 2, COLS, 128), F32), pltpu.VMEM((SEG + 2, COLS, 128), F32),
            pltpu.VMEM((SEG + 1, COLS, 128), F32), pltpu.VMEM((SEG, COLS, 128), F32),
            *sides(LEV), *sides(LEV),
            pltpu.VMEM((LEV, CX, CY), F32),
            pltpu.VMEM((LEV, CX, CY), F32),
            pltpu.VMEM((LEV, CX, CY), F32),
            pltpu.VMEM((LEV * CX, 3 * CY), BF16),
            pltpu.VMEM((LEV * CX, CY), F32),
            pltpu.SemaphoreType.DMA, pltpu.SemaphoreType.DMA((WAVES,)), pltpu.SemaphoreType.DMA, pltpu.SemaphoreType.DMA,
            pltpu.SemaphoreType.DMA,
            pltpu.SemaphoreType.DMA((3, 8)), pltpu.SemaphoreType.DMA((3, 8)),
        ],
        compiler_params=pltpu.CompilerParams(
            collective_id=0, has_side_effects=True, vmem_limit_bytes=VMEM_LIMIT
        ),
        name="gradient",
    )(*args)


def shards(control, sigma, vert_diff, zonal_diff, merid_diff, ocean_mask, owner, cell, interp_weights, innovation, obs_weight):
    return gradient_call(
        control, sigma, vert_diff, zonal_diff, merid_diff, ocean_mask,
        owner.reshape(TILES, 128), cell.reshape(TILES, 128), interp_weights, innovation, obs_weight,
    )


def solution(mesh):
    in_specs = (
        P(None, "gx", "gy"),
        P(None, "gx", "gy"),
        P(None, "gx", "gy"),
        P("gx", "gy"),
        P("gx", "gy"),
        P("gx", "gy"),
        P(("gx", "gy"), None),
        P(("gx", "gy")),
        P(None, ("gx", "gy")),
        P(None, ("gx", "gy")),
        P(None, ("gx", "gy")),
    )
    out_specs = (P(None, "gx", "gy"), P(None, ("gx", "gy")), P(None, "gx", "gy"))
    return jax.shard_map(shards, mesh=mesh, in_specs=in_specs, out_specs=out_specs, check_vma=False)
```

```python
import functools

import jax
import jax.numpy as jnp
from jax import lax
from jax.experimental import pallas as pl
from jax.experimental.pallas import tpu as pltpu
from jax.sharding import PartitionSpec as P

MESH = pl.DeviceIdType.MESH
F32 = jnp.float32
BF16 = jnp.bfloat16
VMEM_LIMIT = 60 * 1024 * 1024

LEV = 16
STEPS = 10
CX = 64
CY = 256
NGX = 16
NGY = 8
NDEV = NGX * NGY
PROF = 2048
CAP = 64
TILES = PROF // 128
ROWS = CX + 2 * STEPS
SPAD = 6
SROWS = 96
GROUPS = 12
REC = 18
DIFFUSE_TILES = 8
SEG = 11
ALL_ROWS = 8 * SEG
EDGE = 24
COLS = CY + 2 * EDGE
PACK_PAIRS = 8
WAVES = NDEV // 2 // PACK_PAIRS
OBSERVE_TILES = 8
UNPACK_TILES = 2


def lane_iota(rows):
    return lax.broadcasted_iota(jnp.int32, (rows, 128), 1)


def blocks(start, count, width, body, carry):
    def many(i, carry):
        for q in range(width):
            carry = body(start + width * i + q, carry)
        return carry

    carry = lax.fori_loop(0, count // width, many, carry)
    for q in range(count - count % width, count):
        carry = body(start + q, carry)
    return carry


def lane_gather(source, lane):
    return jnp.take_along_axis(source, lane, axis=1, mode="promise_in_bounds")


def split_pair(low, high, left):
    first = jnp.where(left, low, pltpu.roll(high, 64, axis=1))
    second = jnp.where(left, pltpu.roll(low, 64, axis=1), high)
    return first, second


def slot_table(owner, cell, weights, rank_out, tab, lanes, tiles, cst):
    rows_o = lax.broadcasted_iota(jnp.int32, (NDEV, 256), 0)
    before = (
        lax.broadcasted_iota(jnp.int32, (256, 256), 0) < lax.broadcasted_iota(jnp.int32, (256, 256), 1)
    ).astype(F32).astype(BF16)
    ones = jnp.ones((256, 256), BF16)
    rows_r = lax.broadcasted_iota(jnp.int32, (CAP, 256), 0)
    cols_p = lax.broadcasted_iota(jnp.int32, (CAP, 256), 1)
    earlier = jnp.zeros((NDEV, 256), F32)
    table = jnp.zeros((NDEV, 128), F32)
    for block in range(PROF // 256):
        owners = jnp.concatenate([owner[2 * block : 2 * block + 1, :], owner[2 * block + 1 : 2 * block + 2, :]], axis=1)
        hot = (rows_o == owners).astype(F32)
        hot16 = hot.astype(BF16)
        count = earlier + jnp.dot(hot16, before, preferred_element_type=F32)
        rank = jnp.sum(hot * count, axis=0, keepdims=True).astype(jnp.int32)
        earlier = earlier + jnp.dot(hot16, ones, preferred_element_type=F32)
        rank_out[2 * block : 2 * block + 1, :] = rank[:, :128]
        rank_out[2 * block + 1 : 2 * block + 2, :] = rank[:, 128:]
        same = rows_r == rank
        lane = jnp.where(same, cols_p % 128, 0).astype(F32).astype(BF16)
        tile = jnp.where(same, 2 * block + 1 + cols_p // 128, 0).astype(F32).astype(BF16)
        table = table + lax.dot_general(
            hot16, jnp.concatenate([lane, tile], axis=0), (((1,), (1,)), ((), ())), preferred_element_type=F32
        )
    tab[...] = table.astype(jnp.int32)
    half = lane_iota(NDEV // 2) < 64
    even, odd = tab[pl.ds(0, NDEV // 2, stride=2), :], tab[pl.ds(1, NDEV // 2, stride=2), :]
    lanes[...] = jnp.where(half, even, pltpu.roll(odd, 64, axis=1))
    tiles[...] = jnp.where(half, pltpu.roll(even, 64, axis=1), odd)

    cst[...] = jnp.zeros_like(cst)
    for tile in range(TILES):
        cols = slice(128 * tile, 128 * tile + 128)
        to = slice(128 * (tile // 2), 128 * (tile // 2) + 128)
        row = 4 * (tile % 2)
        cst[row : row + 1, to] = cell[tile : tile + 1, :].astype(F32)
        cst[row + 1 : row + 2, to] = weights[1:2, cols] + weights[3:4, cols]
        cst[row + 2 : row + 3, to] = weights[2:3, cols] + weights[3:4, cols]


def pack_records(j0, innov, obsw, lanes, tiles, cst, found_ref, rec):
    left = lane_iota(8) < 64
    left_row = lane_iota(1) < 64
    below = lax.broadcasted_iota(jnp.int32, (8, 128), 0) // 4

    for q in range(PACK_PAIRS):
        j = lax.rem(j0 + q * WAVES, NDEV // 2)
        lane = jnp.broadcast_to(lanes[pl.ds(j, 1), :], (8, 128))
        tile_of = jnp.broadcast_to(tiles[pl.ds(j, 1), :], (8, 128))
        tile_up = tile_of - below
        zero = jnp.zeros((8, 128), F32)
        place, found = zero, [zero] * 4
        for tile in range(TILES):
            cols = slice(128 * tile, 128 * tile + 128)
            here = tile_of == tile + 1
            found = [
                jnp.where(here, lane_gather(source, lane), old)
                for source, old in zip((innov[0:8, cols], innov[8:16, cols], obsw[0:8, cols], obsw[8:16, cols]), found)
            ]
            if tile % 2 == 0:
                both = lane_gather(cst[:, 64 * tile : 64 * tile + 128], lane)
                place = jnp.where(tile_up == tile + 1, both, place)
        found_ref[q] = jnp.concatenate(found + [place], axis=0)

    for q in range(PACK_PAIRS):
        j = lax.rem(j0 + q * WAVES, NDEV // 2)
        both = found_ref[q]
        place = both[32:36] + both[36:40]
        turned = pltpu.roll(place, 64, axis=1)
        first_i, second_i = split_pair(both[0:8], both[8:16], left)
        first_o, second_o = split_pair(both[16:24], both[24:32], left)
        for side, parts in enumerate((
            [first_i, first_o, jnp.where(left_row, place[0:1], turned[1:2]), place[2:3]],
            [second_i, second_o, jnp.where(left_row, turned[0:1], place[1:2]), turned[2:3]],
        )):
            for row, value in zip((0, 8, 16, 17), parts):
                rec[2 * j + side, row : row + value.shape[0], :] = value


def unpack(ret, owner, rank, innov, dep, low_ref, high_ref):
    left = lane_iota(8) < 64

    def pair(j, carry):
        one, two = ret[2 * j], ret[2 * j + 1]
        low_ref[j] = jnp.where(left, one, pltpu.roll(two, 64, axis=1))
        high_ref[j] = jnp.where(left, pltpu.roll(one, 64, axis=1), two)
        return carry

    blocks(0, NDEV // 2, 16, pair, 0)

    def tile(t, carry):
        owners = jnp.broadcast_to(owner[pl.ds(t, 1), :], (8, 128))
        lane = jnp.broadcast_to(rank[pl.ds(t, 1), :], (8, 128)) + 64 * (owners % 2)
        pair_of = owners // 2
        low = high = jnp.zeros((8, 128), F32)
        for j in range(NDEV // 2):
            here = pair_of == j
            low = jnp.where(here, lane_gather(low_ref[j], lane), low)
            high = jnp.where(here, lane_gather(high_ref[j], lane), high)
        cols = pl.ds(pl.multiple_of(128 * t, 128), 128)
        dep[0:8, cols] = low - innov[0:8, cols]
        dep[8:16, cols] = high - innov[8:16, cols]
        return carry

    blocks(0, TILES, UNPACK_TILES, tile, 0)


def pack_sides(main, low_side, high_side, lev):
    slot = lane_iota(lev) // 16

    def group(g, carry):
        low = jnp.zeros((lev, 128), F32)
        high = jnp.zeros((lev, 128), F32)
        for m in range(8):
            at = pl.ds(pl.multiple_of((STEPS + 8 * g + m) * lev, lev), lev)
            here = slot == m
            first = main[0, at, :]
            last = main[1, at, :]
            low = jnp.where(here, first if m == 0 else pltpu.roll(first, 16 * m, axis=1), low)
            high = jnp.where(here, last if m == 7 else pltpu.roll(last, 16 * m + 16, axis=1), high)
        at = pl.ds(pl.multiple_of(g * lev, lev), lev)
        low_side[at, :] = low
        high_side[at, :] = high
        return carry

    lax.fori_loop(0, CX // 8, group, 0)


def unpack_sides(from_high, from_low, side, lev):
    left = lane_iota(lev) < 64

    def group(g, carry):
        at = pl.ds(pl.multiple_of(g * lev, lev), lev)
        right_strip = from_high[at, :]
        left_strip = from_low[at, :]
        for m in range(8):
            right = right_strip if m == 0 else pltpu.roll(right_strip, 128 - 16 * m, axis=1)
            leftv = left_strip if m == 7 else pltpu.roll(left_strip, 112 - 16 * m, axis=1)
            side[pl.ds(pl.multiple_of((8 * g + m) * lev, lev), lev), :] = jnp.where(left, right, leftv)
        return carry

    lax.fori_loop(0, GROUPS, group, 0)


def halo_copies(main, low_side, high_side, from_high, from_low, send_sem, recv_sem, gx, gy, lev):
    west, east = (gx + NGX - 1) % NGX, (gx + 1) % NGX
    south, north = (gy + NGY - 1) % NGY, (gy + 1) % NGY

    def rows(ref, start, count):
        at = pl.ds(start * lev, count * lev)
        return ref.at[:, at, :] if len(ref.shape) == 3 else ref.at[at, :]

    plan = (
        (rows(main, STEPS, STEPS), rows(main, STEPS + CX, STEPS), (west, gy)),
        (rows(main, CX, STEPS), rows(main, 0, STEPS), (east, gy)),
        (rows(low_side, 0, 8), rows(from_high, 2, 8), (gx, south)),
        (rows(high_side, 0, 8), rows(from_low, 2, 8), (gx, north)),
        (rows(low_side, 0, 2), rows(from_high, 10, 2), (west, south)),
        (rows(low_side, 6, 2), rows(from_high, 0, 2), (east, south)),
        (rows(high_side, 0, 2), rows(from_low, 10, 2), (west, north)),
        (rows(high_side, 6, 2), rows(from_low, 0, 2), (east, north)),
    )
    return [
        pltpu.make_async_remote_copy(
            src_ref=src,
            dst_ref=dst,
            send_sem=send_sem.at[i],
            recv_sem=recv_sem.at[i],
            device_id=device,
            device_id_type=MESH,
        )
        for i, (src, dst, device) in enumerate(plan)
    ]


def next_cols(parts, last):
    rolled = [pltpu.roll(part, 127, axis=1) for part in parts]
    return [jnp.where(last, rolled[(i + 1) % 3], rolled[i]) for i in range(3)]


def build_faces(coef, coef_side, gy):
    lane = lane_iota(1)
    first_part = jnp.where(gy < NGY - 1, 1.0, 0.0).astype(F32)
    last_part = jnp.where(gy > 0, 1.0, 0.0).astype(F32)
    inside = jnp.where(lane < 64, first_part, last_part)
    last = lane == 127

    def row(r, which):
        at = pl.ds(r * 8 + which, 1)
        return [coef[0, at, :], coef[1, at, :], coef_side[pl.ds((r + SPAD) * 8 + which, 1), :]]

    def put(r, which, parts):
        at = pl.ds(r * 8 + which, 1)
        coef[0, at, :] = parts[0]
        coef[1, at, :] = parts[1]
        coef_side[pl.ds((r + SPAD) * 8 + which, 1), :] = parts[2]

    def wet_row(r):
        one, two, side = row(r, 2)
        return [one, two, side * inside]

    def one(r, wet):
        ahead = wet_row(r + 1)
        zonal, merid = row(r, 0), row(r, 1)
        north = next_cols(wet, last)
        put(r, 0, [z * w * a for z, w, a in zip(zonal, wet, ahead)])
        put(r, 1, [m * w * n for m, w, n in zip(merid, wet, north)])
        return tuple(ahead)

    blocks(0, ROWS - 1, 8, one, tuple(wet_row(0)))


def put_columns(plane, parts):
    first, second, side = [part.T for part in parts]
    plane[EDGE : EDGE + 128, :] = first
    plane[EDGE + 128 : EDGE + 256, :] = second
    plane[EDGE + CY : EDGE + CY + 16, :] = side[0:16]
    plane[EDGE - 16 : EDGE, :] = side[112:128]


def expand_faces(coef, coef_side, face_x, face_y):
    def one(place, carry):
        for which, planes, to in ((0, face_x, place + 1), (1, face_y, place)):
            parts = []
            for ref, pad in ((coef.at[0], 0), (coef.at[1], 0), (coef_side, SPAD)):
                rows = [ref[pl.ds((SEG * seg + place + pad) * 8 + which, 1), :] for seg in range(8)]
                parts.append(jnp.concatenate([jnp.broadcast_to(row, (LEV, 128)) for row in rows], axis=0))
            put_columns(planes.at[to], parts)
        return carry

    blocks(0, SEG, 2, one, 0)
    face_x[0] = pltpu.roll(face_x[SEG], LEV, axis=1)


def turn_edges(field):
    field[0] = pltpu.roll(field[SEG], LEV, axis=1)
    field[SEG + 1] = pltpu.roll(field[1], 128 - LEV, axis=1)


def diffuse(main, side, field_a, field_b, face_x, face_y):
    def enter(place, carry):
        parts = []
        for ref, pad in ((main.at[0], 0), (main.at[1], 0), (side, SPAD)):
            rows = [pl.ds(pl.multiple_of((SEG * seg + place + pad) * LEV, LEV), LEV) for seg in range(8)]
            parts.append(jnp.concatenate([ref[at, :] for at in rows], axis=0))
        put_columns(field_a.at[place + 1], parts)
        return carry

    blocks(0, SEG, 4, enter, 0)
    bottom = lax.broadcasted_iota(jnp.int32, (8, 128), 0) == 7
    turn_edges(field_a)

    for step in range(STEPS):
        now, new = (field_a, field_b) if step % 2 == 0 else (field_b, field_a)

        def north_flux(t, p, here):
            row = pl.multiple_of(8 * t, 8)
            return face_y[p - 1, pl.ds(row, 8), :] * (now[p, pl.ds(row + 1, 8), :] - here)

        def tile(t, carry):
            at = pl.ds(pl.multiple_of(8 * t, 8), 8)
            here, west = now[1, at, :], face_x[0, at, :] * (now[1, at, :] - now[0, at, :])
            norths = []
            for p in range(1, SEG + 1):
                ahead = now[p + 1, at, :]
                east = face_x[p, at, :] * (ahead - here)
                north = north_flux(t, p, here)
                south = pltpu.roll(jnp.where(bottom, carry[p - 1], north), 1, axis=0)
                new[p, at, :] = here + ((east - west) + (north - south))
                here, west = ahead, east
                norths.append(north)
            return tuple(norths)

        first = (EDGE - (STEPS - 1 - step)) // 8
        last = (EDGE + CY + (STEPS - 1 - step) + 7) // 8
        before = [north_flux(first - 1, p, now[p, 8 * first - 8 : 8 * first, :]) for p in range(1, SEG + 1)]
        blocks(first, last - first, DIFFUSE_TILES, tile, tuple(before))
        if step < STEPS - 1:
            turn_edges(new)

    def leave(place, carry):
        for half in range(2):
            rows = field_a[place + 1, EDGE + 128 * half : EDGE + 128 * half + 128, :].T
            for seg in range(8):
                at = pl.ds(pl.multiple_of((SEG * seg + place) * LEV, LEV), LEV)
                main[half, at, :] = rows[LEV * seg : LEV * seg + LEV]
        return carry

    blocks(0, SEG, 4, leave, 0)


SOLVE_ROWS = 32


def load_level(ref, level, x, lev, count):
    at = pl.ds((STEPS + x) * lev + level, count, stride=lev)
    return jnp.concatenate([ref[0, at, :], ref[1, at, :]], axis=1)


def store_level(ref, level, x, lev, count, value):
    at = pl.ds((STEPS + x) * lev + level, count, stride=lev)
    ref[0, at, :] = value[:, 0:128]
    ref[1, at, :] = value[:, 128:256]


def solve_first(control, vert, mask, upper, inverse, reduced, main):
    for x in range(0, CX, SOLVE_ROWS):
        rows = slice(x, x + SOLVE_ROWS)
        wet = mask[rows, :].astype(F32)
        previous = None
        for k in range(LEV):
            rhs = wet * control[k, rows, :]
            diagonal = 1.0
            if k > 0:
                below = vert[k - 1, rows, :]
                diagonal = diagonal + below
            if k < LEV - 1:
                above = vert[k, rows, :]
                diagonal = diagonal + above
            if k > 0:
                diagonal = diagonal + below * up
                rhs = rhs + below * previous
            inv = 1.0 / diagonal
            inverse[k, rows, :] = inv
            if k < LEV - 1:
                up = -above * inv
                upper[k, rows, :] = up
            previous = rhs * inv
            if k < LEV - 1:
                reduced[k, rows, :] = previous
        value = previous
        store_level(main, LEV - 1, x, LEV, SOLVE_ROWS, value)
        for k in range(LEV - 2, -1, -1):
            value = reduced[k, rows, :] - upper[k, rows, :] * value
            store_level(main, k, x, LEV, SOLVE_ROWS, value)


def solve_last(main, control, vert, mask, upper, inverse, reduced, grad):
    for x in range(0, CX, SOLVE_ROWS):
        rows = slice(x, x + SOLVE_ROWS)
        wet = mask[rows, :].astype(F32)
        previous = None
        for k in range(LEV):
            rhs = load_level(main, k, x, LEV, SOLVE_ROWS)
            if k > 0:
                rhs = rhs + vert[k - 1, rows, :] * previous
            previous = rhs * inverse[k, rows, :]
            if k < LEV - 1:
                reduced[k, rows, :] = previous
        value = previous
        grad[LEV - 1, rows, :] = control[LEV - 1, rows, :] + wet * value
        for k in range(LEV - 2, -1, -1):
            value = reduced[k, rows, :] - upper[k, rows, :] * value
            grad[k, rows, :] = control[k, rows, :] + wet * value


def send_first(n, j, partner, send):
    @pl.when(n > 0)
    def _():
        send(2 * j)
        send(2 * j + 1)

    @pl.when(n == 0)
    def _():
        send(partner)


def observe_all(mine, partner, arrived, recv, field3, adj, ret_send, send):
    left = lane_iota(8) < 64
    left_row = lane_iota(1) < 64
    width = OBSERVE_TILES * 128
    rows_b = lax.broadcasted_iota(jnp.int32, (CY, width), 0).astype(F32)
    rows_a = lax.broadcasted_iota(jnp.int32, (CX, width), 0).astype(F32)

    groups = NDEV // 2 // OBSERVE_TILES
    assert groups == WAVES

    def observe(n, carry):
        pairs = [lax.rem(mine + n + groups * h, NDEV // 2) for h in range(OBSERVE_TILES)]
        arrived(n)
        parts = []
        for h in range(OBSERVE_TILES):
            one, two = recv[2 * pairs[h]], recv[2 * pairs[h] + 1]
            turned_one, turned_two = pltpu.roll(one, 64, axis=1), pltpu.roll(two, 64, axis=1)
            parts.append((
                jnp.where(left_row, one[16:17], turned_two[16:17]),
                jnp.where(left_row, turned_one[16:17], two[16:17]),
                jnp.where(left_row, one[17:18], turned_two[17:18]),
                jnp.where(left, one[0:8], turned_two[0:8]),
                jnp.where(left, turned_one[0:8], two[0:8]),
                jnp.where(left, one[8:16], turned_two[8:16]),
                jnp.where(left, turned_one[8:16], two[8:16]),
            ))
        cell, along_x, along_y, low_i, high_i, low_o, high_o = [jnp.concatenate(part, axis=1) for part in zip(*parts)]
        innov = jnp.concatenate([low_i, high_i], axis=0)
        obsw = jnp.concatenate([low_o, high_o], axis=0)
        cell_a = jnp.floor(cell * (1.0 / CY))
        cell_b = cell - CY * cell_a
        from_a = rows_a - cell_a
        from_b = rows_b - cell_b
        in_x = jnp.where(from_a == 0.0, 1.0 - along_x, jnp.where(from_a == 1.0, along_x, 0.0))
        in_y = jnp.where(from_b == 0.0, 1.0 - along_y, jnp.where(from_b == 1.0, along_y, 0.0))
        y_high = in_y.astype(BF16)
        y_low = (in_y - y_high.astype(F32)).astype(BF16)
        y_rows = jnp.concatenate([y_high, y_low, y_high], axis=0)
        vals = []
        for k in range(0, LEV, 4):
            rows = jnp.dot(field3[CX * k : CX * (k + 4), :], y_rows, preferred_element_type=F32)
            vals.append(jnp.sum(rows.reshape(4, CX, width) * in_x[None], axis=1))
        vals = jnp.concatenate(vals, axis=0)
        forcing = obsw * (vals - innov)
        for h in range(OBSERVE_TILES):
            cols = slice(128 * h, 128 * h + 128)
            first, second = split_pair(vals[0:8, cols], vals[8:16, cols], left)
            ret_send[2 * pairs[h]] = first
            ret_send[2 * pairs[h] + 1] = second
        for h in range(1, OBSERVE_TILES):
            send(2 * pairs[h])
            send(2 * pairs[h] + 1)
        spread = (in_x[None] * forcing[:, None, :]).reshape(LEV * CX, width)
        high = spread.astype(BF16)
        low = (spread - high.astype(F32)).astype(BF16)
        adj[...] += lax.dot_general(
            jnp.concatenate([high, high, low], axis=1),
            jnp.concatenate([y_high, y_low, y_high], axis=1),
            (((1,), (1,)), ((), ())),
            preferred_element_type=F32,
        )
        send_first(n, pairs[0], partner, send)
        return carry

    lax.fori_loop(0, groups, observe, 0)


def main_kernel(
    control_in, sigma_in, vert_in, zonal_in, merid_in, mask_in, owner_in, cell_in, weights_in, innov_in, obsw_in,
    inc_out, dep_out, grad_out,
    control, sigma, vert, zonal, merid, mask, owner, cell, weights, innov, obsw, inc, dep, grad, io_sem,
    rec, recv, ret_send, ret, rank, tab, lanes, tiles, cst, found_ref, ret_low, ret_high,
    coef, coef_side, coef_low, coef_high, coef_from_high, coef_from_low,
    main_a, side_a, main_c, side_c, field_a, field_b, face_x, face_y,
    low_a, high_a, from_high_a, from_low_a, low_c, high_c, from_high_c, from_low_c,
    upper, inverse, reduced, field3, adj,
    rec_send_sem, rec_recv_sem, ret_send_sem, ret_recv_sem, self_sem, halo_send, halo_recv,
):
    gx, gy = lax.axis_index("gx"), lax.axis_index("gy")
    me = gx * NGY + gy

    field_ins = ((zonal_in, zonal), (merid_in, merid), (mask_in, mask), (vert_in, vert), (control_in, control))
    late_ins = ((owner_in, owner), (cell_in, cell), (weights_in, weights), (innov_in, innov), (obsw_in, obsw))
    loads = [
        pltpu.make_async_copy(src, dst, io_sem.at[n])
        for n, (src, dst) in enumerate(field_ins + late_ins + ((sigma_in, sigma),))
    ]
    stores = [
        pltpu.make_async_copy(src, dst, io_sem.at[len(loads) + n])
        for n, (src, dst) in enumerate(((inc, inc_out), (dep, dep_out), (grad, grad_out)))
    ]
    for copy in loads:
        copy.start()

    barrier = pltpu.get_barrier_semaphore()

    def greet(d, carry):
        to = lax.rem(me + d, NDEV)
        pl.semaphore_signal(barrier, inc=1, device_id=(lax.div(to, NGY), lax.rem(to, NGY)), device_id_type=MESH)
        return carry

    blocks(1, NDEV - 1, 8, greet, 0)

    def to_device(src, dst, send_sem, recv_sem, to):
        return pltpu.make_async_remote_copy(
            src_ref=src, dst_ref=dst, send_sem=send_sem, recv_sem=recv_sem,
            device_id=(lax.div(to, NGY), lax.rem(to, NGY)), device_id_type=MESH,
        )

    mine = lax.div(me, 2)
    partner = 2 * mine + 1 - lax.rem(me, 2)

    def rec_copy(to, wave):
        return to_device(rec.at[to], recv.at[me], rec_send_sem, rec_recv_sem.at[wave], to)

    def send_ret(to):
        to_device(ret_send.at[to], ret.at[me], ret_send_sem, ret_recv_sem, to).start()

    def wait_all(src, dst, send_sem, recv_sem):
        most = pl.ds(0, NDEV - 1)
        whole = to_device(src.at[most], dst.at[most], send_sem, recv_sem, me)
        whole.wait_recv()
        whole.wait_send()

    for copy in loads[:5]:
        copy.wait()
    for half in range(2):
        coef[half, STEPS * 8 : (STEPS + CX) * 8, :] = jnp.zeros((CX * 8, 128), F32)
        coef[half, ROWS * 8 :, :] = jnp.zeros(((ALL_ROWS - ROWS) * 8, 128), F32)
        for main in (main_a, main_c):
            main[half, ROWS * LEV :, :] = jnp.zeros(((ALL_ROWS - ROWS) * LEV, 128), F32)
    for x in range(0, CX, SOLVE_ROWS):
        rows = slice(x, x + SOLVE_ROWS)
        store_level(coef, 0, x, 8, SOLVE_ROWS, zonal[rows, :])
        store_level(coef, 1, x, 8, SOLVE_ROWS, merid[rows, :])
        store_level(coef, 2, x, 8, SOLVE_ROWS, mask[rows, :].astype(F32))
    pack_sides(coef, coef_low, coef_high, 8)
    solve_first(control, vert, mask, upper, inverse, reduced, main_a)
    pack_sides(main_a, low_a, high_a, LEV)

    pl.semaphore_wait(barrier, NDEV - 1)
    coef_copies = halo_copies(
        coef, coef_low, coef_high, coef_from_high, coef_from_low, halo_send.at[0], halo_recv.at[0], gx, gy, 8
    )
    field_copies = halo_copies(
        main_a, low_a, high_a, from_high_a, from_low_a, halo_send.at[1], halo_recv.at[1], gx, gy, LEV
    )
    for copy in coef_copies + field_copies:
        copy.start()

    for copy in loads[5:10]:
        copy.wait()
    slot_table(owner, cell, weights, rank, tab, lanes, tiles, cst)

    def pack_some(n, carry):
        j0 = lax.rem(mine + NDEV // 2 - n, NDEV // 2)
        pack_records(j0, innov, obsw, lanes, tiles, cst, found_ref, rec)
        return carry

    def send_some(n, carry):
        j0 = lax.rem(mine + NDEV // 2 - n, NDEV // 2)

        def send(to):
            rec_copy(to, n).start()

        for q in range(1, PACK_PAIRS):
            j = lax.rem(j0 + q * WAVES, NDEV // 2)
            send(2 * j)
            send(2 * j + 1)
        send_first(n, j0, partner, send)
        return carry

    lax.fori_loop(0, WAVES, pack_some, 0)
    own = pltpu.make_async_copy(rec.at[me], recv.at[me], self_sem)
    own.start()

    for copy in coef_copies:
        copy.wait()
    unpack_sides(coef_from_high, coef_from_low, coef_side, 8)
    build_faces(coef, coef_side, gy)
    expand_faces(coef, coef_side, face_x, face_y)
    for copy in field_copies:
        copy.wait()
    lax.fori_loop(0, WAVES, send_some, 0)
    unpack_sides(from_high_a, from_low_a, side_a, LEV)
    diffuse(main_a, side_a, field_a, field_b, face_x, face_y)

    loads[10].wait()

    def scale(k, carry):
        for x in range(0, CX, 16):
            value = sigma[k, x : x + 16, :] * load_level(main_a, k, x, LEV, 16)
            inc[k, x : x + 16, :] = value
            high = value.astype(BF16)
            low = (value - high.astype(F32)).astype(BF16)
            at = pl.ds(pl.multiple_of(k * CX + x, 16), 16)
            field3[at, 0:256] = high
            field3[at, 256:512] = high
            field3[at, 512:768] = low
        return carry

    lax.fori_loop(0, LEV, scale, 0)
    stores[0].start()
    adj[...] = jnp.zeros_like(adj)

    own.wait()

    def arrived(n):
        def some(count):
            at = pl.ds(0, count)
            to_device(rec.at[at], recv.at[at], rec_send_sem, rec_recv_sem.at[n], me).wait_recv()

        @pl.when(n == 0)
        def _():
            some(2 * PACK_PAIRS - 1)

        @pl.when(n > 0)
        def _():
            some(2 * PACK_PAIRS)

    observe_all(mine, partner, arrived, recv, field3, adj, ret_send, send_ret)
    most = pl.ds(0, NDEV - 1)
    to_device(rec.at[most], recv.at[most], rec_send_sem, rec_recv_sem.at[0], me).wait_send()
    own = pltpu.make_async_copy(ret_send.at[me], ret.at[me], self_sem)
    own.start()

    def weigh(k, carry):
        for x in range(0, CX, SOLVE_ROWS):
            at = pl.ds(pl.multiple_of(k * CX + x, SOLVE_ROWS), SOLVE_ROWS)
            store_level(main_c, k, x, LEV, SOLVE_ROWS, sigma[k, x : x + SOLVE_ROWS, :] * adj[at, :])
        return carry

    lax.fori_loop(0, LEV, weigh, 0)
    pack_sides(main_c, low_c, high_c, LEV)
    adj_copies = halo_copies(
        main_c, low_c, high_c, from_high_c, from_low_c, halo_send.at[2], halo_recv.at[2], gx, gy, LEV
    )
    for copy in adj_copies:
        copy.start()

    own.wait()
    wait_all(ret_send, ret, ret_send_sem, ret_recv_sem)
    unpack(ret, owner, rank, innov, dep, ret_low, ret_high)
    stores[1].start()

    for copy in adj_copies:
        copy.wait()
    unpack_sides(from_high_c, from_low_c, side_c, LEV)
    diffuse(main_c, side_c, field_a, field_b, face_x, face_y)
    solve_last(main_c, control, vert, mask, upper, inverse, reduced, grad)
    stores[2].start()
    for copy in stores:
        copy.wait()


def gradient_call(*args):
    anywhere = pl.BlockSpec(memory_space=pl.ANY)

    def field(rows, lanes, lev=LEV):
        shape = (rows * lev, 128)
        return pltpu.VMEM(shape if lanes == 128 else (2,) + shape, F32)

    def sides(lev):
        return [field(8, 128, lev), field(8, 128, lev), field(GROUPS, 128, lev), field(GROUPS, 128, lev)]

    outs = (
        jax.ShapeDtypeStruct((LEV, CX, CY), F32),
        jax.ShapeDtypeStruct((LEV, PROF), F32),
        jax.ShapeDtypeStruct((LEV, CX, CY), F32),
    )
    return pl.pallas_call(
        main_kernel,
        out_shape=outs,
        in_specs=[anywhere] * len(args),
        out_specs=(anywhere,) * len(outs),
        scratch_shapes=[
            *[pltpu.VMEM(a.shape, a.dtype) for a in args + outs],
            pltpu.SemaphoreType.DMA((len(args) + len(outs),)),
            pltpu.VMEM((NDEV, REC, 128), F32),
            pltpu.VMEM((NDEV, REC, 128), F32),
            pltpu.VMEM((NDEV, 8, 128), F32),
            pltpu.VMEM((NDEV, 8, 128), F32),
            pltpu.VMEM((TILES, 128), jnp.int32),
            pltpu.VMEM((NDEV, 128), jnp.int32),
            pltpu.VMEM((NDEV // 2, 128), jnp.int32),
            pltpu.VMEM((NDEV // 2, 128), jnp.int32),
            pltpu.VMEM((8, PROF // 2), F32),
            pltpu.VMEM((PACK_PAIRS, 40, 128), F32),
            pltpu.VMEM((NDEV // 2, 8, 128), F32),
            pltpu.VMEM((NDEV // 2, 8, 128), F32),
            field(ALL_ROWS, 256, 8), field(SROWS, 128, 8), *sides(8),
            field(ALL_ROWS, 256), field(SROWS, 128),
            field(ALL_ROWS, 256), field(SROWS, 128),
            pltpu.VMEM((SEG + 2, COLS, 128), F32), pltpu.VMEM((SEG + 2, COLS, 128), F32),
            pltpu.VMEM((SEG + 1, COLS, 128), F32), pltpu.VMEM((SEG, COLS, 128), F32),
            *sides(LEV), *sides(LEV),
            pltpu.VMEM((LEV, CX, CY), F32),
            pltpu.VMEM((LEV, CX, CY), F32),
            pltpu.VMEM((LEV, CX, CY), F32),
            pltpu.VMEM((LEV * CX, 3 * CY), BF16),
            pltpu.VMEM((LEV * CX, CY), F32),
            pltpu.SemaphoreType.DMA, pltpu.SemaphoreType.DMA((WAVES,)), pltpu.SemaphoreType.DMA, pltpu.SemaphoreType.DMA,
            pltpu.SemaphoreType.DMA,
            pltpu.SemaphoreType.DMA((3, 8)), pltpu.SemaphoreType.DMA((3, 8)),
        ],
        compiler_params=pltpu.CompilerParams(
            collective_id=0, has_side_effects=True, vmem_limit_bytes=VMEM_LIMIT
        ),
        name="gradient",
    )(*args)


def settle_kernel(*refs):
    count = (len(refs) - 2) // 3
    sources, targets, held = refs[:count], refs[count : 2 * count], refs[2 * count : 3 * count]
    moves = []
    for n in range(count):
        half = LEV // 2
        for part in range(2):
            at = pl.ds(part * half, half)
            sem = 2 * n + part
            moves.append((
                pltpu.make_async_copy(sources[n].at[at], held[n].at[at], refs[-2].at[sem]),
                pltpu.make_async_copy(held[n].at[at], targets[n].at[at], refs[-1].at[sem]),
            ))
    for load, _ in moves:
        load.start()
    for load, store in moves:
        load.wait()
        store.start()
    for _, store in moves:
        store.wait()


def settle(*arrays):
    anywhere = pl.BlockSpec(memory_space=pl.ANY)
    return pl.pallas_call(
        settle_kernel,
        out_shape=tuple(jax.ShapeDtypeStruct(a.shape, a.dtype) for a in arrays),
        in_specs=[anywhere] * len(arrays),
        out_specs=(anywhere,) * len(arrays),
        scratch_shapes=[
            *[pltpu.VMEM(a.shape, a.dtype) for a in arrays],
            pltpu.SemaphoreType.DMA((2 * len(arrays),)),
            pltpu.SemaphoreType.DMA((2 * len(arrays),)),
        ],
        compiler_params=pltpu.CompilerParams(vmem_limit_bytes=VMEM_LIMIT),
        name="settle",
    )(*arrays)


def shards(control, sigma, vert_diff, zonal_diff, merid_diff, ocean_mask, owner, cell, interp_weights, innovation, obs_weight):
    return settle(*gradient_call(
        control, sigma, vert_diff, zonal_diff, merid_diff, ocean_mask,
        owner.reshape(TILES, 128), cell.reshape(TILES, 128), interp_weights, innovation, obs_weight,
    ))


def solution(mesh):
    in_specs = (
        P(None, "gx", "gy"),
        P(None, "gx", "gy"),
        P(None, "gx", "gy"),
        P("gx", "gy"),
        P("gx", "gy"),
        P("gx", "gy"),
        P(("gx", "gy"), None),
        P(("gx", "gy")),
        P(None, ("gx", "gy")),
        P(None, ("gx", "gy")),
        P(None, ("gx", "gy")),
    )
    out_specs = (P(None, "gx", "gy"), P(None, ("gx", "gy")), P(None, "gx", "gy"))
    return jax.shard_map(shards, mesh=mesh, in_specs=in_specs, out_specs=out_specs, check_vma=False)
```
